32 devices in a mesh: groups: 2 (over y), space: 4 (over z), inst: 2 (over x), row: 2 (over core).
Axes of the slice: x: 2, y: 2, z: 4, core: 2. Of those that a mesh axis runs over, the one named last changes fastest.
Arguments:
- solution: bfloat16 [2, 4, 320, 8192], P('row', 'inst', None, ('groups', 'space')), parts along dimension 3, may hold values from -6 to 6
- forcing: bfloat16 [2, 4, 320, 8192], P('row', 'inst', None, ('groups', 'space')), parts along dimension 3, may hold values from -6 to 6
- metric_scale: float32 [2, 8192], P('row', ('groups', 'space')), parts along dimension 1, may hold values from 0.5 to 2
- frequency: float32 [1], replicated, may hold values from 0.1 to 0.4
- adjacency: int32 [2, 6, 8192], P('row', None, ('groups', 'space')), parts along dimension 2, may hold values from 0 to 1151, as said below
- partner: int32 [2, 4, 512], P('row', 'inst', ('groups', 'space')), parts along dimension 2, may hold values from 0 to 255, as said below
- volume_matrix: bfloat16 [320, 320], replicated, may hold values from -0.3125 to 0.3125
- trace_matrix: bfloat16 [480, 320], replicated, may hold values from -0.3125 to 0.3125
- lift_matrix: bfloat16 [320, 480], replicated, may hold values from -0.25 to 0.25
- block_inverse: bfloat16 [320, 320], replicated, may hold values from -0.3125 to 0.3125
Outputs:
- updated: bfloat16 [2, 4, 320, 8192], P('row', 'inst', None, ('groups', 'space')), parts along dimension 3
The draws below stay inside these ranges and needn't reach their ends.
There are 2 independent parts, one for each index of `groups`. The reference program is written for one: setup_inputs(seed, part) draws one part's arguments, and reference() takes and returns one part's arrays. A program takes and returns all parts, laid end to end along the dimension named above; an argument that names none is the same for every part. Nothing has to cross between parts.
Inputs may be any that keep to these rules, and one draw needn't show every extreme that they name: The element beside e across face f is (e - e % 1024 - 64 + adjacency[s, f, e]) mod 4096 of the same section, never e itself; the relation is mutual (the element beside e across f has e beside it across face f xor 1); faces 0 to 3 stay within e's block of 1024 elements, and faces 4 and 5 leave it only from the first or the last 64 elements of a block. partner[0, n] is a permutation of the 256 interface rows and partner[1, n] its inverse; for every instance, exactly 16 of the rows k with the same k // 64 map to each block of 64 rows.
All inputs are finite; a program needn't handle non-finite values.
Results may differ from the reference program's by a relative error of at most 0.0054.
Values may be sent and summed in bfloat16 or wider, within the bound.
No kernel may reach another device: no remote copies, remote signals or barrier semaphores. Data moves between devices by JAX's collectives and lax.ppermute only.
A program may use at most 64 MiB of HBM per device.

```python
import math
import jax
import jax.numpy as jnp
from jax import lax

DOF = 320
TRACE = 80
LAYER = 64
E_DEV = 1024
RIM = 64
NF_DEV = 64
NI = 4
NE = 4096
NF = 256
CAP = 16


def draw_adjacency(key, part):
    side_cells = 8
    layers_all = NE // LAYER
    keys = jax.random.split(key, 2 * layers_all)
    orders = jax.vmap(lambda single: jax.random.permutation(single, LAYER))(keys).reshape(2, layers_all, LAYER).astype(jnp.int32)
    inverse = jnp.argsort(orders, axis=2).astype(jnp.int32)
    column = orders % side_cells
    line = orders // side_cells
    moves = [(0, line * side_cells + (column - 1) % side_cells), (0, line * side_cells + (column + 1) % side_cells), (0, (line - 1) % side_cells * side_cells + column), (0, (line + 1) % side_cells * side_cells + column), (-1, orders), (1, orders)]
    layer_ids = jnp.arange(layers_all, dtype=jnp.int32)[None, :, None]
    slot_ids = jnp.arange(LAYER, dtype=jnp.int32)[None, None, :]
    own_ids = layer_ids * LAYER + slot_ids
    own_start = own_ids // E_DEV * E_DEV
    faces_out = []
    for layer_step, target_pos in moves:
        rolled = jnp.roll(inverse, -layer_step, axis=1)
        target_slot = jnp.take_along_axis(rolled, target_pos, axis=2)
        target_layer = (layer_ids + layer_step) % layers_all
        target_ids = target_layer * LAYER + target_slot
        local_ids = jnp.mod(target_ids - own_start + RIM, NE)
        faces_out.append(local_ids.reshape(2, NE))
    return jnp.stack(faces_out, axis=1).astype(jnp.int32)


def draw_partner(key, part):
    shards = NF // NF_DEV
    key_first, key_second, key_shift = jax.random.split(key, 3)
    first_keys = jax.random.split(key_first, NI * shards)
    second_keys = jax.random.split(key_second, NI * shards)
    first_perm = jax.vmap(lambda single: jax.random.permutation(single, NF_DEV))(first_keys).reshape(NI, shards, NF_DEV).astype(jnp.int32)
    second_perm = jax.vmap(lambda single: jax.random.permutation(single, NF_DEV))(second_keys).reshape(NI, shards, NF_DEV).astype(jnp.int32)
    shifts = jax.random.randint(key_shift, (NI, 1, 1), 0, shards).astype(jnp.int32)
    source_block = jnp.arange(shards, dtype=jnp.int32)[None, :, None]
    group_ids = first_perm // CAP
    within = first_perm % CAP
    target_block = jnp.mod(source_block + group_ids + shifts, shards)
    target_slot = source_block * CAP + within
    inst_ids = jnp.arange(NI, dtype=jnp.int32)[:, None, None]
    flat_perm = second_perm.reshape(NI * shards, NF_DEV)
    picked = flat_perm[(inst_ids * shards + target_block).reshape(-1), target_slot.reshape(-1)]
    rotor_side = (target_block * NF_DEV + picked.reshape(NI, shards, NF_DEV)).reshape(NI, NF).astype(jnp.int32)
    stator_side = jnp.argsort(rotor_side, axis=1).astype(jnp.int32)
    return jnp.stack([rotor_side, stator_side])


def level_of(rng, dims, cuts, low, high):
    loudness = 1.0
    for axis_at, blocks in cuts:
        heights = jax.random.uniform(jax.random.fold_in(jax.random.fold_in(rng, 6), axis_at), (blocks,), jnp.float32, low / len(cuts), high / len(cuts))
        loudness = loudness * jnp.repeat(jnp.exp(heights), dims[axis_at] // blocks).reshape((-1,) + (1,) * (len(dims) - 1 - axis_at))
    return loudness


def bell_draw(key, shape, scale, bound, cuts=(), kind=jnp.bfloat16):
    drawn = jax.random.normal(key, shape, jnp.float32) * scale
    if len(cuts) > 0:
        drawn = level_of(key, shape, cuts, -0.22, 0.18) * drawn
    return jnp.clip(drawn, min=-bound, max=bound).astype(kind)


def setup_inputs(seed: int = 0, part: int = 0) -> dict:
    seeds = jax.random.split(jax.random.key(seed), 11)
    part_keys = jax.random.split(jax.random.fold_in(seeds[10], part), 11)
    solution = bell_draw(part_keys[0], (2, NI, DOF, NE), 1.0, 6.0, ((0, 2), (1, 2), (3, 4)))
    forcing = bell_draw(part_keys[1], (2, NI, DOF, NE), 1.0, 6.0, ((0, 2), (1, 2), (3, 4)))
    metric_scale = jnp.clip(jnp.exp(math.log(2.0) - 1.3862944 * jax.random.uniform(part_keys[2], (2, NE), jnp.float32) ** level_of(part_keys[2], (2, NE), ((0, 2), (1, 4)), -0.2, 0.2)), 0.5, 2.0)
    frequency = jnp.clip(jnp.exp(jax.random.uniform(seeds[3], (1,), jnp.float32, math.log(0.1), math.log(0.4))), 0.1, 0.4)
    adjacency = draw_adjacency(jax.random.fold_in(jax.random.fold_in(seeds[10], part), 71), part)
    partner = draw_partner(jax.random.fold_in(jax.random.fold_in(seeds[10], part), 71), part)
    volume_matrix = bell_draw(seeds[6], (DOF, DOF), DOF ** -0.5, 0.3125)
    trace_matrix = bell_draw(seeds[7], (6 * TRACE, DOF), DOF ** -0.5, 0.3125)
    lift_matrix = bell_draw(seeds[8], (DOF, 6 * TRACE), (6 * TRACE) ** -0.5, 0.25)
    block_inverse = bell_draw(seeds[9], (DOF, DOF), DOF ** -0.5, 0.3125)
    return dict(solution=solution, forcing=forcing, metric_scale=metric_scale, frequency=frequency, adjacency=adjacency, partner=partner, volume_matrix=volume_matrix, trace_matrix=trace_matrix, lift_matrix=lift_matrix, block_inverse=block_inverse)


OPPOSITE = (1, 0, 3, 2, 5, 4)


def spectral_table(instances, frequency):
    positions = jnp.arange(instances, dtype=jnp.int32)
    distance = (positions[:, None] - positions[None, :]).astype(jnp.float32)
    parity = 1.0 - 2.0 * jnp.mod(positions[:, None] + positions[None, :], 2).astype(jnp.float32)
    angles = jnp.pi * distance / instances
    sine_values = jnp.where(distance == 0.0, 1.0, jnp.sin(angles))
    cotangent = jnp.where(distance == 0.0, 0.0, jnp.cos(angles) / sine_values)
    return frequency * 0.5 * parity * cotangent


def reference(solution, forcing, metric_scale, frequency, adjacency, partner, volume_matrix, trace_matrix, lift_matrix, block_inverse):
    weights_all = spectral_table(NI, frequency[0])
    element_ids = jnp.arange(NE, dtype=jnp.int32)
    shard_start = (element_ids // E_DEV) * E_DEV
    neighbour_ids = jnp.mod(shard_start[None, None, :] - RIM + adjacency, NE).astype(jnp.int32)
    iface_ids = jnp.arange(NF, dtype=jnp.int32)
    iface_elems = ((iface_ids // NF_DEV) * E_DEV + iface_ids % NF_DEV).astype(jnp.int32)
    trace_wide = trace_matrix.astype(jnp.float32)
    lift_wide = lift_matrix.astype(jnp.float32)
    volume_wide = volume_matrix.astype(jnp.float32)
    inverse_wide = block_inverse.astype(jnp.float32)
    scales = metric_scale[:, None, :]

    def one_instance(number):
        current = solution[:, number]
        traces = jnp.einsum("fd,sde->sfe", trace_wide, current.astype(jnp.float32)).astype(jnp.bfloat16)
        gathered = []
        for side_number in range(2):
            pieces = []
            for face_number in range(6):
                facing = OPPOSITE[face_number]
                face_values = traces[side_number, facing * TRACE:(facing + 1) * TRACE]
                pieces.append(jnp.take(face_values, neighbour_ids[side_number, face_number], axis=1))
            beside = jnp.concatenate(pieces, axis=0)
            opposite_side = 1 - side_number
            partner_elems = jnp.take(iface_elems, partner[side_number, number], axis=0)
            incoming = jnp.take(traces[opposite_side, side_number * TRACE:(side_number + 1) * TRACE], partner_elems, axis=1)
            row_offset = opposite_side * TRACE
            beside = beside.at[row_offset:row_offset + TRACE, iface_elems].set(incoming)
            gathered.append(beside)
        beside_all = jnp.stack(gathered)
        coupled = jnp.einsum("df,sfe->sde", lift_wide, beside_all.astype(jnp.float32))
        volume = jnp.einsum("dk,ske->sde", volume_wide, current.astype(jnp.float32))
        source = jnp.einsum("m,smde->sde", weights_all[number], solution.astype(jnp.float32), precision=lax.Precision.HIGHEST).astype(jnp.bfloat16)
        residual = (forcing[:, number].astype(jnp.float32) - scales * (volume + coupled) - source.astype(jnp.float32)).astype(jnp.bfloat16)
        update = jnp.einsum("dk,ske->sde", inverse_wide, residual.astype(jnp.float32))
        return (current.astype(jnp.float32) + update / scales).astype(jnp.bfloat16)

    result = lax.map(one_instance, jnp.arange(NI, dtype=jnp.int32))
    return jnp.transpose(result, (1, 0, 2, 3))
```

```python
import functools

import jax
import jax.numpy as jnp
import numpy as np
from jax import lax
from jax.experimental import pallas as pl
from jax.experimental.pallas import tpu as pltpu
from jax.sharding import PartitionSpec as P

LAYER = 64
OPPOSITE = (1, 0, 3, 2, 5, 4)
LANES = 128
VMEM_LIMIT = 40 * 1024 * 1024


def spectral_table(instances):
    positions = np.arange(instances)
    distance = positions[:, None] - positions[None, :]
    parity = np.where(distance % 2 == 0, 1.0, -1.0)
    angles = np.pi * distance / instances
    sines = np.where(distance == 0, 1.0, np.sin(angles))
    cotangent = np.where(distance == 0, 0.0, np.cos(angles) / sines)
    return (0.5 * parity * cotangent).astype(np.float32)


def one_hot(picked, rows):
    numbers = lax.broadcasted_iota(jnp.int32, (rows, picked.shape[1]), 0)
    return jnp.where(numbers == picked, 1.0, 0.0).astype(jnp.bfloat16)


def dot(left, right):
    return jnp.dot(left, right, preferred_element_type=jnp.float32)


def ends_kernel(place_ref, first_ref, last_ref, trace_ref, up_ref, down_ref, cross_ref):
    width = trace_ref.shape[0] // 6
    section = place_ref[0]
    for n in range(first_ref.shape[0]):
        first = dot(trace_ref[...], first_ref[n]).astype(jnp.bfloat16)
        last = dot(trace_ref[4 * width :, :], last_ref[n]).astype(jnp.bfloat16)
        down_ref[n] = first[4 * width :, :LAYER]
        up_ref[n] = last[:, last.shape[1] - LAYER :]
        rows = cross_ref.shape[2]
        cross_ref[n] = jnp.where(section == 0, first[width : 2 * width, :rows], first[:width, :rows])


def couple_kernel(shards, place_ref, freq_ref, table_ref, adj_ref, partner_ref, all_ref, tile_ref, forcing_ref,
                  scale_ref, trace_ref, lift_ref, volume_ref, low_ref, high_ref, *rest):
    pieces, (out_ref, traces) = rest[:shards], rest[shards:]
    step = pl.program_id(0)
    steps = pl.num_programs(0)
    count, dof, total = all_ref.shape
    width = trace_ref.shape[0] // 6
    tile = tile_ref.shape[2]
    section, inst, space = place_ref[0], place_ref[1], place_ref[2]

    @pl.when(step == 0)
    def _():
        for n in range(count):
            for c in range(total // tile):
                cols = slice(c * tile, (c + 1) * tile)
                made = dot(trace_ref[...], all_ref[n, :, cols]).astype(jnp.bfloat16)
                for f in range(6):
                    traces[f, n * width : (n + 1) * width, cols] = made[f * width : (f + 1) * width]

    column = lax.broadcasted_iota(jnp.int32, (1, tile), 1)
    at_edge = jnp.logical_or(step == 0, step == steps - 1)

    def gathered(edge):
        found = []
        for f in range(6):
            adj = adj_ref[f : f + 1, :]
            values = dot(traces[OPPOSITE[f]], one_hot(adj - LAYER, total))
            if edge and f >= 4:
                part = slice((5 - f) * width, (6 - f) * width)
                below = jnp.concatenate([low_ref[n, part, :] for n in range(count)], axis=0)
                above = jnp.concatenate([high_ref[n, part, :] for n in range(count)], axis=0)
                values += dot(below, one_hot(adj, LAYER))
                values += dot(above, one_hot(adj - (LAYER + total), LAYER))
            values = values.astype(jnp.bfloat16)
            if edge and f < 2:
                rows = partner_ref.shape[1]
                use = jnp.logical_and(step == 0, section == 1 - f)
                crossed = []
                for n in range(count):
                    wanted = partner_ref[n : n + 1, :]
                    arrived = jnp.zeros((width, rows), jnp.float32)
                    for d in range(shards):
                        source = lax.rem(space - d + shards, shards)
                        arrived += dot(pieces[d][n], one_hot(wanted - source * rows, rows))
                    crossed.append(arrived)
                crossed = jnp.concatenate(crossed, axis=0).astype(jnp.bfloat16)
                crossed = jnp.concatenate(
                    [crossed, jnp.zeros((count * width, tile - rows), jnp.bfloat16)], axis=1)
                take = jnp.logical_and(column < rows, use)
                values = jnp.where(take, crossed, values)
            found.append(values)
        return found

    def finish(edge):
        found = gathered(edge)
        frequency = freq_ref[0]
        scale = scale_ref[...]
        for n in range(count):
            beside = jnp.concatenate([v[n * width : (n + 1) * width] for v in found], axis=0)
            inner = dot(lift_ref[...], beside) + dot(volume_ref[...], tile_ref[n])
            value = forcing_ref[n].astype(jnp.float32) - scale * inner
            for m in range(count):
                weight = table_ref[inst * count + n, inst * count + m] * frequency
                value -= weight * tile_ref[m].astype(jnp.float32)
            out_ref[n] = value

    @pl.when(at_edge)
    def _():
        finish(True)

    @pl.when(jnp.logical_not(at_edge))
    def _():
        finish(False)


def update_kernel(peers, place_ref, freq_ref, table_ref, partial_ref, current_ref, scale_ref, inverse_ref, *rest):
    others, out_ref = rest[: peers - 1], rest[peers - 1]
    count = current_ref.shape[0]
    inst = place_ref[1]
    frequency = freq_ref[0]
    inverse_scale = 1.0 / scale_ref[...]
    for n in range(count):
        value = partial_ref[n]
        for d in range(1, peers):
            owner = lax.rem(inst - d + peers, peers)
            for m in range(count):
                weight = table_ref[inst * count + n, owner * count + m] * frequency
                value -= weight * others[d - 1][m].astype(jnp.float32)
        update = dot(inverse_ref[...], value.astype(jnp.bfloat16))
        out_ref[n] = (current_ref[n].astype(jnp.float32) + update * inverse_scale).astype(jnp.bfloat16)


def whole(array):
    return pl.BlockSpec(array.shape, lambda j: (0,) * array.ndim)


def body(solution, forcing, metric_scale, frequency, adjacency, partner, volume_matrix, trace_matrix, lift_matrix,
         block_inverse):
    current = solution[0]
    forcing_local = forcing[0]
    neighbours = adjacency[0]
    partner_rows = partner[0]
    count, dof, total = current.shape
    width = trace_matrix.shape[0] // 6
    iface_rows = partner_rows.shape[1]
    shards = lax.axis_size("space")
    peers = lax.axis_size("inst")
    section = lax.axis_index("row")
    place = jnp.stack([section, lax.axis_index("inst"), lax.axis_index("space")]).astype(jnp.int32)
    table = jnp.asarray(spectral_table(count * peers))
    smem = pl.BlockSpec(memory_space=pltpu.SMEM)
    bf16 = jnp.bfloat16

    with jax.named_scope("instances"):
        others = [lax.ppermute(current, "inst", [(i, (i + d) % peers) for i in range(peers)])
                  for d in range(1, peers)]

    with jax.named_scope("ends"):
        up, down, cross = pl.pallas_call(
            ends_kernel,
            grid=(1,),
            out_shape=(jax.ShapeDtypeStruct((count, 2 * width, LAYER), bf16),
                       jax.ShapeDtypeStruct((count, 2 * width, LAYER), bf16),
                       jax.ShapeDtypeStruct((count, width, iface_rows), bf16)),
            in_specs=[smem,
                      pl.BlockSpec((count, dof, LANES), lambda j: (0, 0, 0)),
                      pl.BlockSpec((count, dof, LANES), lambda j: (0, 0, total // LANES - 1)),
                      whole(trace_matrix)],
            out_specs=(pl.BlockSpec((count, 2 * width, LAYER), lambda j: (0, 0, 0)),
                       pl.BlockSpec((count, 2 * width, LAYER), lambda j: (0, 0, 0)),
                       pl.BlockSpec((count, width, iface_rows), lambda j: (0, 0, 0))),
            compiler_params=pltpu.CompilerParams(vmem_limit_bytes=VMEM_LIMIT),
            cost_estimate=pl.CostEstimate(flops=8 * width * dof * LANES * 2 * count,
                                          bytes_accessed=1_000_000, transcendentals=0),
            name="ends",
        )(place, current, current, trace_matrix)

    with jax.named_scope("halo"):
        low = lax.ppermute(up, "space", [(i, (i + 1) % shards) for i in range(shards)])
        high = lax.ppermute(down, "space", [(i, (i - 1) % shards) for i in range(shards)])
    with jax.named_scope("interface"):
        pieces = [lax.ppermute(cross, ("space", "row"),
                               [(i * 2 + r, (i + d) % shards * 2 + 1 - r) for i in range(shards) for r in range(2)])
                  for d in range(shards)]

    tile = 256
    steps = total // tile
    by_tile = lambda *lead: pl.BlockSpec(lead + (tile,), lambda j: (0,) * len(lead) + (j,))
    with jax.named_scope("couple"):
        partial = pl.pallas_call(
            functools.partial(couple_kernel, shards),
            grid=(steps,),
            out_shape=jax.ShapeDtypeStruct((count, dof, total), jnp.float32),
            in_specs=[smem, smem, smem, by_tile(6), whole(partner_rows), whole(current), by_tile(count, dof),
                      by_tile(count, dof), by_tile(1), whole(trace_matrix), whole(lift_matrix),
                      whole(volume_matrix), whole(low), whole(high)] + [whole(p) for p in pieces],
            out_specs=by_tile(count, dof),
            scratch_shapes=[pltpu.VMEM((6, count * width, total), bf16)],
            compiler_params=pltpu.CompilerParams(vmem_limit_bytes=VMEM_LIMIT),
            cost_estimate=pl.CostEstimate(
                flops=2 * count * total * (6 * width * dof * 2 + dof * dof + 6 * width * total),
                bytes_accessed=count * dof * total * 10, transcendentals=0),
            name="couple",
        )(place, frequency, table, neighbours, partner_rows, current, current, forcing_local, metric_scale,
          trace_matrix, lift_matrix, volume_matrix, low, high, *pieces)

    with jax.named_scope("update"):
        result = pl.pallas_call(
            functools.partial(update_kernel, peers),
            grid=(steps,),
            out_shape=jax.ShapeDtypeStruct((count, dof, total), bf16),
            in_specs=[smem, smem, smem, by_tile(count, dof), by_tile(count, dof), by_tile(1), whole(block_inverse)]
            + [by_tile(count, dof)] * (peers - 1),
            out_specs=by_tile(count, dof),
            compiler_params=pltpu.CompilerParams(vmem_limit_bytes=VMEM_LIMIT),
            cost_estimate=pl.CostEstimate(flops=2 * count * total * dof * dof,
                                          bytes_accessed=count * dof * total * 10, transcendentals=0),
            name="update",
        )(place, frequency, table, partial, current, metric_scale, block_inverse, *others)
    return result[None]


def solution(mesh):
    in_specs = (
        P("row", "inst", None, ("groups", "space")),
        P("row", "inst", None, ("groups", "space")),
        P("row", ("groups", "space")),
        P(),
        P("row", None, ("groups", "space")),
        P("row", "inst", ("groups", "space")),
        P(),
        P(),
        P(),
        P(),
    )
    out_specs = P("row", "inst", None, ("groups", "space"))
    return jax.shard_map(body, mesh=mesh, in_specs=in_specs, out_specs=out_specs, check_vma=False)
```

```python
import functools

import jax
import jax.numpy as jnp
import numpy as np
from jax import lax
from jax.experimental import pallas as pl
from jax.experimental.pallas import tpu as pltpu
from jax.sharding import PartitionSpec as P

LAYER = 64
OPPOSITE = (1, 0, 3, 2, 5, 4)
LANES = 128
VMEM_LIMIT = 40 * 1024 * 1024


def spectral_table(instances):
    positions = np.arange(instances)
    distance = positions[:, None] - positions[None, :]
    parity = np.where(distance % 2 == 0, 1.0, -1.0)
    angles = np.pi * distance / instances
    sines = np.where(distance == 0, 1.0, np.sin(angles))
    cotangent = np.where(distance == 0, 0.0, np.cos(angles) / sines)
    return (0.5 * parity * cotangent).astype(np.float32)


def one_hot(picked, rows):
    numbers = lax.broadcasted_iota(jnp.int32, (rows, picked.shape[1]), 0)
    return jnp.where(numbers == picked, 1.0, 0.0).astype(jnp.bfloat16)


def dot(left, right):
    return jnp.dot(left, right, preferred_element_type=jnp.float32)


def ends_kernel(place_ref, first_ref, last_ref, trace_ref, up_ref, down_ref, cross_ref):
    width = trace_ref.shape[0] // 6
    section = place_ref[0]
    for n in range(first_ref.shape[0]):
        first = dot(trace_ref[...], first_ref[n]).astype(jnp.bfloat16)
        last = dot(trace_ref[4 * width :, :], last_ref[n]).astype(jnp.bfloat16)
        down_ref[n] = first[4 * width :, :LAYER]
        up_ref[n] = last[:, last.shape[1] - LAYER :]
        rows = cross_ref.shape[2]
        cross_ref[n] = jnp.where(section == 0, first[width : 2 * width, :rows], first[:width, :rows])


def couple_kernel(shards, place_ref, freq_ref, table_ref, adj_ref, partner_ref, all_ref, tile_ref, forcing_ref,
                  scale_ref, trace_ref, lift_ref, volume_ref, inverse_ref, low_ref, high_ref, *rest):
    pieces, (out_ref, traces) = rest[:shards], rest[shards:]
    step = pl.program_id(0)
    steps = pl.num_programs(0)
    count, dof, total = all_ref.shape
    width = trace_ref.shape[0] // 6
    tile = tile_ref.shape[2]
    section, inst, space = place_ref[0], place_ref[1], place_ref[2]

    @pl.when(step == 0)
    def _():
        for n in range(count):
            for c in range(total // tile):
                cols = slice(c * tile, (c + 1) * tile)
                made = dot(trace_ref[...], all_ref[n, :, cols]).astype(jnp.bfloat16)
                for f in range(6):
                    traces[f, n * width : (n + 1) * width, cols] = made[f * width : (f + 1) * width]

    column = lax.broadcasted_iota(jnp.int32, (1, tile), 1)
    at_edge = jnp.logical_or(step == 0, step == steps - 1)

    def gathered(edge):
        found = []
        for f in range(6):
            adj = adj_ref[f : f + 1, :]
            values = dot(traces[OPPOSITE[f]], one_hot(adj - LAYER, total))
            if edge and f >= 4:
                part = slice((5 - f) * width, (6 - f) * width)
                below = jnp.concatenate([low_ref[n, part, :] for n in range(count)], axis=0)
                above = jnp.concatenate([high_ref[n, part, :] for n in range(count)], axis=0)
                values += dot(below, one_hot(adj, LAYER))
                values += dot(above, one_hot(adj - (LAYER + total), LAYER))
            values = values.astype(jnp.bfloat16)
            if edge and f < 2:
                rows = partner_ref.shape[1]
                use = jnp.logical_and(step == 0, section == 1 - f)
                crossed = []
                for n in range(count):
                    wanted = partner_ref[n : n + 1, :]
                    arrived = jnp.zeros((width, rows), jnp.float32)
                    for d in range(shards):
                        source = lax.rem(space - d + shards, shards)
                        arrived += dot(pieces[d][n], one_hot(wanted - source * rows, rows))
                    crossed.append(arrived)
                crossed = jnp.concatenate(crossed, axis=0).astype(jnp.bfloat16)
                crossed = jnp.concatenate(
                    [crossed, jnp.zeros((count * width, tile - rows), jnp.bfloat16)], axis=1)
                take = jnp.logical_and(column < rows, use)
                values = jnp.where(take, crossed, values)
            found.append(values)
        return found

    def finish(edge):
        found = gathered(edge)
        frequency = freq_ref[0]
        scale = scale_ref[...]
        inverse_scale = 1.0 / scale
        for n in range(count):
            beside = jnp.concatenate([v[n * width : (n + 1) * width] for v in found], axis=0)
            inner = dot(lift_ref[...], beside) + dot(volume_ref[...], tile_ref[n])
            value = forcing_ref[n].astype(jnp.float32) - scale * inner
            for m in range(count):
                weight = table_ref[inst * count + n, inst * count + m] * frequency
                value -= weight * tile_ref[m].astype(jnp.float32)
            update = dot(inverse_ref[...], value.astype(jnp.bfloat16))
            out_ref[n] = tile_ref[n].astype(jnp.float32) + update * inverse_scale

    @pl.when(at_edge)
    def _():
        finish(True)

    @pl.when(jnp.logical_not(at_edge))
    def _():
        finish(False)


def update_kernel(peers, first, place_ref, freq_ref, table_ref, ready_ref, scale_ref, inverse_ref, *rest):
    others, out_ref = rest[: peers - 1], rest[-1]
    count = ready_ref.shape[0]
    tile = out_ref.shape[2]
    step = pl.program_id(0)
    here = pl.ds(pl.multiple_of(step * tile, tile), tile)
    there = pl.ds(pl.multiple_of(first + step * tile, tile), tile)
    inst = place_ref[1]
    factor = freq_ref[0] / scale_ref[:, there]
    values = [ready_ref[n, :, there] for n in range(count)]
    for d in range(1, peers):
        owner = lax.rem(inst - d + peers, peers)
        for m in range(count):
            moved = dot(inverse_ref[...], others[d - 1][m, :, here])
            for n in range(count):
                weight = table_ref[inst * count + n, owner * count + m]
                values[n] -= (weight * factor) * moved
    for n in range(count):
        out_ref[n] = values[n].astype(jnp.bfloat16)


def whole(array):
    return pl.BlockSpec(array.shape, lambda j: (0,) * array.ndim)


def body(solution, forcing, metric_scale, frequency, adjacency, partner, volume_matrix, trace_matrix, lift_matrix,
         block_inverse):
    current = solution[0]
    forcing_local = forcing[0]
    neighbours = adjacency[0]
    partner_rows = partner[0]
    count, dof, total = current.shape
    width = trace_matrix.shape[0] // 6
    iface_rows = partner_rows.shape[1]
    shards = lax.axis_size("space")
    peers = lax.axis_size("inst")
    section = lax.axis_index("row")
    place = jnp.stack([section, lax.axis_index("inst"), lax.axis_index("space")]).astype(jnp.int32)
    table = jnp.asarray(spectral_table(count * peers))
    smem = pl.BlockSpec(memory_space=pltpu.SMEM)
    bf16 = jnp.bfloat16

    with jax.named_scope("instances"):
        bounds = [(0, total)]
        arriving = [[lax.ppermute(current[:, :, first:last], "inst", [(i, (i + d) % peers) for i in range(peers)])
                     for d in range(1, peers)] for first, last in bounds]

    with jax.named_scope("ends"):
        up, down, cross = pl.pallas_call(
            ends_kernel,
            grid=(1,),
            out_shape=(jax.ShapeDtypeStruct((count, 2 * width, LAYER), bf16),
                       jax.ShapeDtypeStruct((count, 2 * width, LAYER), bf16),
                       jax.ShapeDtypeStruct((count, width, iface_rows), bf16)),
            in_specs=[smem,
                      pl.BlockSpec((count, dof, LANES), lambda j: (0, 0, 0)),
                      pl.BlockSpec((count, dof, LANES), lambda j: (0, 0, total // LANES - 1)),
                      whole(trace_matrix)],
            out_specs=(pl.BlockSpec((count, 2 * width, LAYER), lambda j: (0, 0, 0)),
                       pl.BlockSpec((count, 2 * width, LAYER), lambda j: (0, 0, 0)),
                       pl.BlockSpec((count, width, iface_rows), lambda j: (0, 0, 0))),
            compiler_params=pltpu.CompilerParams(vmem_limit_bytes=VMEM_LIMIT),
            cost_estimate=pl.CostEstimate(flops=8 * width * dof * LANES * 2 * count,
                                          bytes_accessed=1_000_000, transcendentals=0),
            name="ends",
        )(place, current, current, trace_matrix)

    with jax.named_scope("halo"):
        low = lax.ppermute(up, "space", [(i, (i + 1) % shards) for i in range(shards)])
        high = lax.ppermute(down, "space", [(i, (i - 1) % shards) for i in range(shards)])
    with jax.named_scope("interface"):
        pieces = [lax.ppermute(cross, ("space", "row"),
                               [(i * 2 + r, (i + d) % shards * 2 + 1 - r) for i in range(shards) for r in range(2)])
                  for d in range(shards)]

    tile = 256
    steps = total // tile
    by_tile = lambda *lead: pl.BlockSpec(lead + (tile,), lambda j: (0,) * len(lead) + (j,))
    with jax.named_scope("couple"):
        ready = pl.pallas_call(
            functools.partial(couple_kernel, shards),
            grid=(steps,),
            out_shape=jax.ShapeDtypeStruct((count, dof, total), jnp.float32),
            in_specs=[smem, smem, smem, by_tile(6), whole(partner_rows), whole(current), by_tile(count, dof),
                      by_tile(count, dof), by_tile(1), whole(trace_matrix), whole(lift_matrix),
                      whole(volume_matrix), whole(block_inverse), whole(low), whole(high)] + [whole(p) for p in pieces],
            out_specs=by_tile(count, dof),
            scratch_shapes=[pltpu.VMEM((6, count * width, total), bf16)],
            compiler_params=pltpu.CompilerParams(vmem_limit_bytes=VMEM_LIMIT),
            cost_estimate=pl.CostEstimate(
                flops=2 * count * total * (6 * width * dof * 2 + dof * dof + 6 * width * total),
                bytes_accessed=count * dof * total * 10, transcendentals=0),
            name="couple",
        )(place, frequency, table, neighbours, partner_rows, current, current, forcing_local, metric_scale,
          trace_matrix, lift_matrix, volume_matrix, block_inverse, low, high, *pieces)

    vmem = pl.BlockSpec(memory_space=pltpu.VMEM)
    with jax.named_scope("update"):
        result = None
        for (first, last), others in zip(bounds, arriving):
            more = [] if result is None else [result]
            result = pl.pallas_call(
                functools.partial(update_kernel, peers, first),
                grid=((last - first) // tile,),
                out_shape=jax.ShapeDtypeStruct((count, dof, total), bf16),
                in_specs=[smem, smem, smem] + [vmem] * (2 + peers) + [pl.BlockSpec(memory_space=pl.ANY)] * len(more),
                out_specs=pl.BlockSpec((count, dof, tile), lambda j, at=first // tile: (0, 0, at + j)),
                input_output_aliases={5 + peers: 0} if more else {},
                compiler_params=pltpu.CompilerParams(vmem_limit_bytes=VMEM_LIMIT),
                cost_estimate=pl.CostEstimate(flops=2 * count * (last - first) * dof * dof * (peers - 1),
                                              bytes_accessed=count * dof * (last - first) * 8, transcendentals=0),
                name="update",
            )(place, frequency, table, ready, metric_scale, block_inverse, *others, *more)
    return result[None]


def solution(mesh):
    in_specs = (
        P("row", "inst", None, ("groups", "space")),
        P("row", "inst", None, ("groups", "space")),
        P("row", ("groups", "space")),
        P(),
        P("row", None, ("groups", "space")),
        P("row", "inst", ("groups", "space")),
        P(),
        P(),
        P(),
        P(),
    )
    out_specs = P("row", "inst", None, ("groups", "space"))
    return jax.shard_map(body, mesh=mesh, in_specs=in_specs, out_specs=out_specs, check_vma=False)
```

```python
import functools

import jax
import jax.numpy as jnp
import numpy as np
from jax import lax
from jax.experimental import pallas as pl
from jax.experimental.pallas import tpu as pltpu
from jax.sharding import PartitionSpec as P

LAYER = 64
OPPOSITE = (1, 0, 3, 2, 5, 4)
LANES = 128
VMEM_LIMIT = 40 * 1024 * 1024


def spectral_table(instances):
    positions = np.arange(instances)
    distance = positions[:, None] - positions[None, :]
    parity = np.where(distance % 2 == 0, 1.0, -1.0)
    angles = np.pi * distance / instances
    sines = np.where(distance == 0, 1.0, np.sin(angles))
    cotangent = np.where(distance == 0, 0.0, np.cos(angles) / sines)
    return (0.5 * parity * cotangent).astype(np.float32)


def one_hot(picked, rows):
    numbers = lax.broadcasted_iota(jnp.int32, (rows, picked.shape[1]), 0)
    return jnp.where(numbers == picked, 1.0, 0.0).astype(jnp.bfloat16)


def dot(left, right):
    return jnp.dot(left, right, preferred_element_type=jnp.float32)


def ends_kernel(place_ref, first_ref, last_ref, trace_ref, up_ref, down_ref, cross_ref):
    width = trace_ref.shape[0] // 6
    section = place_ref[0]
    for n in range(first_ref.shape[0]):
        first = dot(trace_ref[...], first_ref[n]).astype(jnp.bfloat16)
        last = dot(trace_ref[4 * width :, :], last_ref[n]).astype(jnp.bfloat16)
        down_ref[n] = first[4 * width :, :LAYER]
        up_ref[n] = last[:, last.shape[1] - LAYER :]
        rows = cross_ref.shape[2]
        cross_ref[n] = jnp.where(section == 0, first[width : 2 * width, :rows], first[:width, :rows])


def couple_kernel(shards, place_ref, freq_ref, table_ref, adj_ref, partner_ref, all_ref, tile_ref, forcing_ref,
                  scale_ref, trace_ref, lift_ref, volume_ref, inverse_ref, low_ref, high_ref, *rest):
    pieces, (out_ref, traces) = rest[:shards], rest[shards:]
    step = pl.program_id(0)
    steps = pl.num_programs(0)
    count, dof, total = all_ref.shape
    width = trace_ref.shape[0] // 6
    tile = tile_ref.shape[2]
    section, inst, space = place_ref[0], place_ref[1], place_ref[2]

    @pl.when(step == 0)
    def _():
        for n in range(count):
            for c in range(total // tile):
                cols = slice(c * tile, (c + 1) * tile)
                made = dot(trace_ref[...], all_ref[n, :, cols]).astype(jnp.bfloat16)
                for f in range(6):
                    traces[f, n * width : (n + 1) * width, cols] = made[f * width : (f + 1) * width]

    column = lax.broadcasted_iota(jnp.int32, (1, tile), 1)
    at_edge = jnp.logical_or(step == 0, step == steps - 1)

    def gathered(edge):
        found = []
        for f in range(6):
            adj = adj_ref[f : f + 1, :]
            values = dot(traces[OPPOSITE[f]], one_hot(adj - LAYER, total))
            if edge and f >= 4:
                part = slice((5 - f) * width, (6 - f) * width)
                below = jnp.concatenate([low_ref[n, part, :] for n in range(count)], axis=0)
                above = jnp.concatenate([high_ref[n, part, :] for n in range(count)], axis=0)
                values += dot(below, one_hot(adj, LAYER))
                values += dot(above, one_hot(adj - (LAYER + total), LAYER))
            values = values.astype(jnp.bfloat16)
            if edge and f < 2:
                rows = partner_ref.shape[1]
                use = jnp.logical_and(step == 0, section == 1 - f)
                crossed = []
                for n in range(count):
                    wanted = partner_ref[n : n + 1, :]
                    arrived = jnp.zeros((width, rows), jnp.float32)
                    for d in range(shards):
                        source = lax.rem(space - d + shards, shards)
                        arrived += dot(pieces[d][n], one_hot(wanted - source * rows, rows))
                    crossed.append(arrived)
                crossed = jnp.concatenate(crossed, axis=0).astype(jnp.bfloat16)
                crossed = jnp.concatenate(
                    [crossed, jnp.zeros((count * width, tile - rows), jnp.bfloat16)], axis=1)
                take = jnp.logical_and(column < rows, use)
                values = jnp.where(take, crossed, values)
            found.append(values)
        return found

    def finish(edge):
        found = gathered(edge)
        frequency = freq_ref[0]
        scale = scale_ref[...]
        inverse_scale = 1.0 / scale
        for n in range(count):
            beside = jnp.concatenate([v[n * width : (n + 1) * width] for v in found], axis=0)
            inner = dot(lift_ref[...], beside) + dot(volume_ref[...], tile_ref[n])
            value = forcing_ref[n].astype(jnp.float32) - scale * inner
            for m in range(count):
                weight = table_ref[inst * count + n, inst * count + m] * frequency
                value -= weight * tile_ref[m].astype(jnp.float32)
            update = dot(inverse_ref[...], value.astype(jnp.bfloat16))
            out_ref[n] = tile_ref[n].astype(jnp.float32) + update * inverse_scale

    @pl.when(at_edge)
    def _():
        finish(True)

    @pl.when(jnp.logical_not(at_edge))
    def _():
        finish(False)


def update_kernel(peers, first, place_ref, freq_ref, table_ref, ready_ref, scale_ref, inverse_ref, *rest):
    others, out_ref = rest[: peers - 1], rest[-1]
    count = ready_ref.shape[0]
    tile = out_ref.shape[2]
    step = pl.program_id(0)
    here = pl.ds(pl.multiple_of(step * tile, tile), tile)
    there = pl.ds(pl.multiple_of(first + step * tile, tile), tile)
    inst = place_ref[1]
    factor = freq_ref[0] / scale_ref[:, there]
    values = [ready_ref[n, :, there] for n in range(count)]
    for d in range(1, peers):
        owner = lax.rem(inst - d + peers, peers)
        for m in range(count):
            moved = dot(inverse_ref[...], others[d - 1][m, :, here])
            for n in range(count):
                weight = table_ref[inst * count + n, owner * count + m]
                values[n] -= (weight * factor) * moved
    for n in range(count):
        out_ref[n] = values[n].astype(jnp.bfloat16)


def whole(array):
    return pl.BlockSpec(array.shape, lambda j: (0,) * array.ndim)


def body(solution, forcing, metric_scale, frequency, adjacency, partner, volume_matrix, trace_matrix, lift_matrix,
         block_inverse):
    current = solution[0]
    forcing_local = forcing[0]
    neighbours = adjacency[0]
    partner_rows = partner[0]
    count, dof, total = current.shape
    width = trace_matrix.shape[0] // 6
    iface_rows = partner_rows.shape[1]
    shards = lax.axis_size("space")
    peers = lax.axis_size("inst")
    section = lax.axis_index("row")
    place = jnp.stack([section, lax.axis_index("inst"), lax.axis_index("space")]).astype(jnp.int32)
    table = jnp.asarray(spectral_table(count * peers))
    smem = pl.BlockSpec(memory_space=pltpu.SMEM)
    bf16 = jnp.bfloat16

    with jax.named_scope("instances"):
        tile = 256
        bounds = [(0, tile), (tile, total - tile), (total - tile, total)]
        arriving = [[lax.ppermute(current[:, :, first:last], "inst", [(i, (i + d) % peers) for i in range(peers)])
                     for d in range(1, peers)] for first, last in bounds]

    with jax.named_scope("ends"):
        up, down, cross = pl.pallas_call(
            ends_kernel,
            grid=(1,),
            out_shape=(jax.ShapeDtypeStruct((count, 2 * width, LAYER), bf16),
                       jax.ShapeDtypeStruct((count, 2 * width, LAYER), bf16),
                       jax.ShapeDtypeStruct((count, width, iface_rows), bf16)),
            in_specs=[smem,
                      pl.BlockSpec((count, dof, LANES), lambda j: (0, 0, 0)),
                      pl.BlockSpec((count, dof, LANES), lambda j: (0, 0, total // LANES - 1)),
                      whole(trace_matrix)],
            out_specs=(pl.BlockSpec((count, 2 * width, LAYER), lambda j: (0, 0, 0)),
                       pl.BlockSpec((count, 2 * width, LAYER), lambda j: (0, 0, 0)),
                       pl.BlockSpec((count, width, iface_rows), lambda j: (0, 0, 0))),
            compiler_params=pltpu.CompilerParams(vmem_limit_bytes=VMEM_LIMIT),
            cost_estimate=pl.CostEstimate(flops=8 * width * dof * LANES * 2 * count,
                                          bytes_accessed=1_000_000, transcendentals=0),
            name="ends",
        )(place, current, current, trace_matrix)

    with jax.named_scope("halo"):
        low = lax.ppermute(up, "space", [(i, (i + 1) % shards) for i in range(shards)])
        high = lax.ppermute(down, "space", [(i, (i - 1) % shards) for i in range(shards)])
    with jax.named_scope("interface"):
        pieces = [lax.ppermute(cross, ("space", "row"),
                               [(i * 2 + r, (i + d) % shards * 2 + 1 - r) for i in range(shards) for r in range(2)])
                  for d in range(shards)]

    steps = total // tile
    by_tile = lambda *lead: pl.BlockSpec(lead + (tile,), lambda j: (0,) * len(lead) + (j,))
    with jax.named_scope("couple"):
        ready = pl.pallas_call(
            functools.partial(couple_kernel, shards),
            grid=(steps,),
            out_shape=jax.ShapeDtypeStruct((count, dof, total), jnp.float32),
            in_specs=[smem, smem, smem, by_tile(6), whole(partner_rows), whole(current), by_tile(count, dof),
                      by_tile(count, dof), by_tile(1), whole(trace_matrix), whole(lift_matrix),
                      whole(volume_matrix), whole(block_inverse), whole(low), whole(high)] + [whole(p) for p in pieces],
            out_specs=by_tile(count, dof),
            scratch_shapes=[pltpu.VMEM((6, count * width, total), bf16)],
            compiler_params=pltpu.CompilerParams(vmem_limit_bytes=VMEM_LIMIT),
            cost_estimate=pl.CostEstimate(
                flops=2 * count * total * (6 * width * dof * 2 + dof * dof + 6 * width * total),
                bytes_accessed=count * dof * total * 10, transcendentals=0),
            name="couple",
        )(place, frequency, table, neighbours, partner_rows, current, current, forcing_local, metric_scale,
          trace_matrix, lift_matrix, volume_matrix, block_inverse, low, high, *pieces)

    vmem = pl.BlockSpec(memory_space=pltpu.VMEM)
    with jax.named_scope("update"):
        result = None
        for (first, last), others in zip(bounds, arriving):
            more = [] if result is None else [result]
            result = pl.pallas_call(
                functools.partial(update_kernel, peers, first),
                grid=((last - first) // tile,),
                out_shape=jax.ShapeDtypeStruct((count, dof, total), bf16),
                in_specs=[smem, smem, smem] + [vmem] * (2 + peers) + [pl.BlockSpec(memory_space=pl.ANY)] * len(more),
                out_specs=pl.BlockSpec((count, dof, tile), lambda j, at=first // tile: (0, 0, at + j)),
                input_output_aliases={5 + peers: 0} if more else {},
                compiler_params=pltpu.CompilerParams(vmem_limit_bytes=VMEM_LIMIT),
                cost_estimate=pl.CostEstimate(flops=2 * count * (last - first) * dof * dof * (peers - 1),
                                              bytes_accessed=count * dof * (last - first) * 8, transcendentals=0),
                name="update",
            )(place, frequency, table, ready, metric_scale, block_inverse, *others, *more)
    return result[None]


def solution(mesh):
    in_specs = (
        P("row", "inst", None, ("groups", "space")),
        P("row", "inst", None, ("groups", "space")),
        P("row", ("groups", "space")),
        P(),
        P("row", None, ("groups", "space")),
        P("row", "inst", ("groups", "space")),
        P(),
        P(),
        P(),
        P(),
    )
    out_specs = P("row", "inst", None, ("groups", "space"))
    return jax.shard_map(body, mesh=mesh, in_specs=in_specs, out_specs=out_specs, check_vma=False)
```

```python
import functools

import jax
import jax.numpy as jnp
import numpy as np
from jax import lax
from jax.experimental import pallas as pl
from jax.experimental.pallas import tpu as pltpu
from jax.sharding import PartitionSpec as P

LAYER = 64
OPPOSITE = (1, 0, 3, 2, 5, 4)
LANES = 128
VMEM_LIMIT = 40 * 1024 * 1024


def spectral_table(instances):
    positions = np.arange(instances)
    distance = positions[:, None] - positions[None, :]
    parity = np.where(distance % 2 == 0, 1.0, -1.0)
    angles = np.pi * distance / instances
    sines = np.where(distance == 0, 1.0, np.sin(angles))
    cotangent = np.where(distance == 0, 0.0, np.cos(angles) / sines)
    return (0.5 * parity * cotangent).astype(np.float32)


def one_hot(picked, rows):
    numbers = lax.broadcasted_iota(jnp.int32, (rows, picked.shape[1]), 0)
    return jnp.where(numbers == picked, 1.0, 0.0).astype(jnp.bfloat16)


def dot(left, right):
    return jnp.dot(left, right, preferred_element_type=jnp.float32)


def ends_kernel(place_ref, first_ref, last_ref, trace_ref, up_ref, down_ref, cross_ref):
    width = trace_ref.shape[0] // 6
    section = place_ref[0]
    for n in range(first_ref.shape[0]):
        first = dot(trace_ref[...], first_ref[n]).astype(jnp.bfloat16)
        last = dot(trace_ref[4 * width :, :], last_ref[n]).astype(jnp.bfloat16)
        down_ref[n] = first[4 * width :, :LAYER]
        up_ref[n] = last[:, last.shape[1] - LAYER :]
        rows = cross_ref.shape[2]
        cross_ref[n] = jnp.where(section == 0, first[width : 2 * width, :rows], first[:width, :rows])


def couple_kernel(shards, peers, place_ref, freq_ref, table_ref, adj_ref, partner_ref, all_ref, tile_ref, forcing_ref,
                  scale_ref, trace_ref, lift_ref, volume_ref, inverse_ref, low_ref, high_ref, *rest):
    pieces, (out_ref, factor_ref, traces) = rest[:shards], rest[shards:]
    step = pl.program_id(0)
    steps = pl.num_programs(0)
    count, dof, total = all_ref.shape
    width = trace_ref.shape[0] // 6
    tile = tile_ref.shape[2]
    section, inst, space = place_ref[0], place_ref[1], place_ref[2]

    @pl.when(step == 0)
    def _():
        for n in range(count):
            for c in range(total // tile):
                cols = slice(c * tile, (c + 1) * tile)
                made = dot(trace_ref[...], all_ref[n, :, cols]).astype(jnp.bfloat16)
                for f in range(6):
                    traces[f, n * width : (n + 1) * width, cols] = made[f * width : (f + 1) * width]

    column = lax.broadcasted_iota(jnp.int32, (1, tile), 1)
    at_edge = jnp.logical_or(step == 0, step == steps - 1)

    def gathered(edge):
        found = []
        for f in range(6):
            adj = adj_ref[f : f + 1, :]
            values = dot(traces[OPPOSITE[f]], one_hot(adj - LAYER, total))
            if edge and f >= 4:
                part = slice((5 - f) * width, (6 - f) * width)
                below = jnp.concatenate([low_ref[n, part, :] for n in range(count)], axis=0)
                above = jnp.concatenate([high_ref[n, part, :] for n in range(count)], axis=0)
                values += dot(below, one_hot(adj, LAYER))
                values += dot(above, one_hot(adj - (LAYER + total), LAYER))
            values = values.astype(jnp.bfloat16)
            if edge and f < 2:
                rows = partner_ref.shape[1]
                use = jnp.logical_and(step == 0, section == 1 - f)
                crossed = []
                for n in range(count):
                    wanted = partner_ref[n : n + 1, :]
                    arrived = jnp.zeros((width, rows), jnp.float32)
                    for d in range(shards):
                        source = lax.rem(space - d + shards, shards)
                        arrived += dot(pieces[d][n], one_hot(wanted - source * rows, rows))
                    crossed.append(arrived)
                crossed = jnp.concatenate(crossed, axis=0).astype(jnp.bfloat16)
                crossed = jnp.concatenate(
                    [crossed, jnp.zeros((count * width, tile - rows), jnp.bfloat16)], axis=1)
                take = jnp.logical_and(column < rows, use)
                values = jnp.where(take, crossed, values)
            found.append(values)
        return found

    def finish(edge):
        found = gathered(edge)
        frequency = freq_ref[0]
        scale = scale_ref[...]
        inverse_scale = 1.0 / scale
        for n in range(count):
            for d in range(1, peers):
                owner = lax.rem(inst - d + peers, peers)
                for m in range(count):
                    weight = table_ref[inst * count + n, owner * count + m] * frequency
                    at = (n * (peers - 1) + d - 1) * count + m
                    factor_ref[at : at + 1, :] = weight * inverse_scale
        for n in range(count):
            beside = jnp.concatenate([v[n * width : (n + 1) * width] for v in found], axis=0)
            inner = dot(lift_ref[...], beside) + dot(volume_ref[...], tile_ref[n])
            value = forcing_ref[n].astype(jnp.float32) - scale * inner
            for m in range(count):
                weight = table_ref[inst * count + n, inst * count + m] * frequency
                value -= weight * tile_ref[m].astype(jnp.float32)
            update = dot(inverse_ref[...], value.astype(jnp.bfloat16))
            out_ref[n] = tile_ref[n].astype(jnp.float32) + update * inverse_scale

    @pl.when(at_edge)
    def _():
        finish(True)

    @pl.when(jnp.logical_not(at_edge))
    def _():
        finish(False)


def update_kernel(tile, ready_ref, factor_ref, inverse_ref, *rest):
    others, (out_ref, made, sems) = rest[:-3], rest[-3:]
    count, dof, total = ready_ref.shape
    copies = []
    for t in range(total // tile):
        cols = slice(t * tile, (t + 1) * tile)
        moved = [dot(inverse_ref[...], other[m, :, cols]) for other in others for m in range(count)]
        for n in range(count):
            value = ready_ref[n, :, cols]
            for k, part in enumerate(moved):
                at = n * len(moved) + k
                value -= factor_ref[at : at + 1, cols] * part
            made[t, n] = value.astype(jnp.bfloat16)
        copy = pltpu.make_async_copy(made.at[t], out_ref.at[:, :, cols], sems.at[t])
        copy.start()
        copies.append(copy)
    for copy in copies:
        copy.wait()


def whole(array):
    return pl.BlockSpec(array.shape, lambda j: (0,) * array.ndim)


def body(solution, forcing, metric_scale, frequency, adjacency, partner, volume_matrix, trace_matrix, lift_matrix,
         block_inverse):
    current = solution[0]
    forcing_local = forcing[0]
    neighbours = adjacency[0]
    partner_rows = partner[0]
    count, dof, total = current.shape
    width = trace_matrix.shape[0] // 6
    iface_rows = partner_rows.shape[1]
    shards = lax.axis_size("space")
    peers = lax.axis_size("inst")
    section = lax.axis_index("row")
    place = jnp.stack([section, lax.axis_index("inst"), lax.axis_index("space")]).astype(jnp.int32)
    table = jnp.asarray(spectral_table(count * peers))
    smem = pl.BlockSpec(memory_space=pltpu.SMEM)
    bf16 = jnp.bfloat16

    with jax.named_scope("instances"):
        others = [lax.ppermute(current, "inst", [(i, (i + d) % peers) for i in range(peers)])
                  for d in range(1, peers)]

    with jax.named_scope("ends"):
        up, down, cross = pl.pallas_call(
            ends_kernel,
            grid=(1,),
            out_shape=(jax.ShapeDtypeStruct((count, 2 * width, LAYER), bf16),
                       jax.ShapeDtypeStruct((count, 2 * width, LAYER), bf16),
                       jax.ShapeDtypeStruct((count, width, iface_rows), bf16)),
            in_specs=[smem,
                      pl.BlockSpec((count, dof, LANES), lambda j: (0, 0, 0)),
                      pl.BlockSpec((count, dof, LANES), lambda j: (0, 0, total // LANES - 1)),
                      whole(trace_matrix)],
            out_specs=(pl.BlockSpec((count, 2 * width, LAYER), lambda j: (0, 0, 0)),
                       pl.BlockSpec((count, 2 * width, LAYER), lambda j: (0, 0, 0)),
                       pl.BlockSpec((count, width, iface_rows), lambda j: (0, 0, 0))),
            compiler_params=pltpu.CompilerParams(vmem_limit_bytes=VMEM_LIMIT),
            cost_estimate=pl.CostEstimate(flops=8 * width * dof * LANES * 2 * count,
                                          bytes_accessed=1_000_000, transcendentals=0),
            name="ends",
        )(place, current, current, trace_matrix)

    with jax.named_scope("halo"):
        low = lax.ppermute(up, "space", [(i, (i + 1) % shards) for i in range(shards)])
        high = lax.ppermute(down, "space", [(i, (i - 1) % shards) for i in range(shards)])
    with jax.named_scope("interface"):
        pieces = [lax.ppermute(cross, ("space", "row"),
                               [(i * 2 + r, (i + d) % shards * 2 + 1 - r) for i in range(shards) for r in range(2)])
                  for d in range(shards)]

    tile = 256
    steps = total // tile
    by_tile = lambda *lead: pl.BlockSpec(lead + (tile,), lambda j: (0,) * len(lead) + (j,))
    with jax.named_scope("couple"):
        ready, factors = pl.pallas_call(
            functools.partial(couple_kernel, shards, peers),
            grid=(steps,),
            out_shape=(jax.ShapeDtypeStruct((count, dof, total), jnp.float32),
                       jax.ShapeDtypeStruct((count * count * (peers - 1), total), jnp.float32)),
            in_specs=[smem, smem, smem, by_tile(6), whole(partner_rows), whole(current), by_tile(count, dof),
                      by_tile(count, dof), by_tile(1), whole(trace_matrix), whole(lift_matrix),
                      whole(volume_matrix), whole(block_inverse), whole(low), whole(high)] + [whole(p) for p in pieces],
            out_specs=(by_tile(count, dof), by_tile(count * count * (peers - 1))),
            scratch_shapes=[pltpu.VMEM((6, count * width, total), bf16)],
            compiler_params=pltpu.CompilerParams(vmem_limit_bytes=VMEM_LIMIT),
            cost_estimate=pl.CostEstimate(
                flops=2 * count * total * (6 * width * dof * 2 + dof * dof + 6 * width * total),
                bytes_accessed=count * dof * total * 10, transcendentals=0),
            name="couple",
        )(place, frequency, table, neighbours, partner_rows, current, current, forcing_local, metric_scale,
          trace_matrix, lift_matrix, volume_matrix, block_inverse, low, high, *pieces)

    vmem = pl.BlockSpec(memory_space=pltpu.VMEM)
    with jax.named_scope("update"):
        result = pl.pallas_call(
            functools.partial(update_kernel, tile),
            out_shape=jax.ShapeDtypeStruct((count, dof, total), bf16),
            in_specs=[vmem] * (2 + peers),
            out_specs=pl.BlockSpec(memory_space=pl.ANY),
            scratch_shapes=[pltpu.VMEM((steps, count, dof, tile), bf16), pltpu.SemaphoreType.DMA((steps,))],
            compiler_params=pltpu.CompilerParams(vmem_limit_bytes=VMEM_LIMIT),
            cost_estimate=pl.CostEstimate(flops=2 * count * total * dof * dof * (peers - 1),
                                          bytes_accessed=count * dof * total * 8, transcendentals=0),
            name="update",
        )(ready, factors, block_inverse, *others)
    return result[None]


def solution(mesh):
    in_specs = (
        P("row", "inst", None, ("groups", "space")),
        P("row", "inst", None, ("groups", "space")),
        P("row", ("groups", "space")),
        P(),
        P("row", None, ("groups", "space")),
        P("row", "inst", ("groups", "space")),
        P(),
        P(),
        P(),
        P(),
    )
    out_specs = P("row", "inst", None, ("groups", "space"))
    return jax.shard_map(body, mesh=mesh, in_specs=in_specs, out_specs=out_specs, check_vma=False)
```

```python
import functools

import jax
import jax.numpy as jnp
import numpy as np
from jax import lax
from jax.experimental import pallas as pl
from jax.experimental.pallas import tpu as pltpu
from jax.sharding import PartitionSpec as P

LAYER = 64
OPPOSITE = (1, 0, 3, 2, 5, 4)
LANES = 128
VMEM_LIMIT = 40 * 1024 * 1024


def spectral_table(instances):
    positions = np.arange(instances)
    distance = positions[:, None] - positions[None, :]
    parity = np.where(distance % 2 == 0, 1.0, -1.0)
    angles = np.pi * distance / instances
    sines = np.where(distance == 0, 1.0, np.sin(angles))
    cotangent = np.where(distance == 0, 0.0, np.cos(angles) / sines)
    return (0.5 * parity * cotangent).astype(np.float32)


def one_hot(picked, rows):
    numbers = lax.broadcasted_iota(jnp.int32, (rows, picked.shape[1]), 0)
    return jnp.where(numbers == picked, 1.0, 0.0).astype(jnp.bfloat16)


def dot(left, right):
    return jnp.dot(left, right, preferred_element_type=jnp.float32)


def ends_kernel(place_ref, first_ref, last_ref, trace_ref, up_ref, down_ref, cross_ref):
    width = trace_ref.shape[0] // 6
    section = place_ref[0]
    for n in range(first_ref.shape[0]):
        first = dot(trace_ref[...], first_ref[n]).astype(jnp.bfloat16)
        last = dot(trace_ref[4 * width :, :], last_ref[n]).astype(jnp.bfloat16)
        down_ref[n] = first[4 * width :, :LAYER]
        up_ref[n] = last[:, last.shape[1] - LAYER :]
        rows = cross_ref.shape[2]
        cross_ref[n] = jnp.where(section == 0, first[width : 2 * width, :rows], first[:width, :rows])


def couple_kernel(shards, peers, place_ref, freq_ref, table_ref, adj_ref, partner_ref, all_ref, tile_ref, forcing_ref,
                  scale_ref, trace_ref, lift_ref, volume_ref, inverse_ref, low_ref, high_ref, *rest):
    pieces, (out_ref, factor_ref, traces) = rest[:shards], rest[shards:]
    step = pl.program_id(0)
    steps = pl.num_programs(0)
    count, dof, total = all_ref.shape
    width = trace_ref.shape[0] // 6
    tile = tile_ref.shape[2]
    section, inst, space = place_ref[0], place_ref[1], place_ref[2]

    @pl.when(step == 0)
    def _():
        for n in range(count):
            for c in range(total // tile):
                cols = slice(c * tile, (c + 1) * tile)
                made = dot(trace_ref[...], all_ref[n, :, cols]).astype(jnp.bfloat16)
                for f in range(6):
                    traces[f, n * width : (n + 1) * width, cols] = made[f * width : (f + 1) * width]

    column = lax.broadcasted_iota(jnp.int32, (1, tile), 1)
    at_edge = jnp.logical_or(step == 0, step == steps - 1)

    def gathered(edge):
        found = []
        for f in range(6):
            adj = adj_ref[f : f + 1, :]
            values = dot(traces[OPPOSITE[f]], one_hot(adj - LAYER, total))
            if edge and f >= 4:
                part = slice((5 - f) * width, (6 - f) * width)
                below = jnp.concatenate([low_ref[n, part, :] for n in range(count)], axis=0)
                above = jnp.concatenate([high_ref[n, part, :] for n in range(count)], axis=0)
                values += dot(below, one_hot(adj, LAYER))
                values += dot(above, one_hot(adj - (LAYER + total), LAYER))
            values = values.astype(jnp.bfloat16)
            if edge and f < 2:
                rows = partner_ref.shape[1]
                use = jnp.logical_and(step == 0, section == 1 - f)
                crossed = []
                for n in range(count):
                    wanted = partner_ref[n : n + 1, :]
                    arrived = jnp.zeros((width, rows), jnp.float32)
                    for d in range(shards):
                        source = lax.rem(space - d + shards, shards)
                        arrived += dot(pieces[d][n], one_hot(wanted - source * rows, rows))
                    crossed.append(arrived)
                crossed = jnp.concatenate(crossed, axis=0).astype(jnp.bfloat16)
                crossed = jnp.concatenate(
                    [crossed, jnp.zeros((count * width, tile - rows), jnp.bfloat16)], axis=1)
                take = jnp.logical_and(column < rows, use)
                values = jnp.where(take, crossed, values)
            found.append(values)
        return found

    def finish(edge):
        found = gathered(edge)
        frequency = freq_ref[0]
        scale = scale_ref[...]
        inverse_scale = 1.0 / scale
        for n in range(count):
            for d in range(1, peers):
                owner = lax.rem(inst - d + peers, peers)
                for m in range(count):
                    weight = table_ref[inst * count + n, owner * count + m] * frequency
                    at = (n * (peers - 1) + d - 1) * count + m
                    factor_ref[at : at + 1, :] = weight * inverse_scale
        for n in range(count):
            beside = jnp.concatenate([v[n * width : (n + 1) * width] for v in found], axis=0)
            inner = dot(lift_ref[...], beside) + dot(volume_ref[...], tile_ref[n])
            value = forcing_ref[n].astype(jnp.float32) - scale * inner
            for m in range(count):
                weight = table_ref[inst * count + n, inst * count + m] * frequency
                value -= weight * tile_ref[m].astype(jnp.float32)
            update = dot(inverse_ref[...], value.astype(jnp.bfloat16))
            out_ref[n] = tile_ref[n].astype(jnp.float32) + update * inverse_scale

    @pl.when(at_edge)
    def _():
        finish(True)

    @pl.when(jnp.logical_not(at_edge))
    def _():
        finish(False)


def update_kernel(tile, place_ref, ready_ref, factor_ref, inverse_ref, all_ref, out_ref, taken, made, in_sems, sems):
    count, dof, total = ready_ref.shape
    peers = all_ref.shape[0]
    steps = total // tile
    loads = []
    for t in range(steps):
        cols = slice(t * tile, (t + 1) * tile)
        for d in range(1, peers):
            owner = lax.rem(place_ref[1] - d + peers, peers)
            load = pltpu.make_async_copy(all_ref.at[owner, :, :, cols], taken.at[t, d - 1], in_sems.at[t, d - 1])
            load.start()
            loads.append(load)
    copies = []
    for t in range(steps):
        cols = slice(t * tile, (t + 1) * tile)
        for load in loads[t * (peers - 1) : (t + 1) * (peers - 1)]:
            load.wait()
        moved = [dot(inverse_ref[...], taken[t, d, m]) for d in range(peers - 1) for m in range(count)]
        for n in range(count):
            value = ready_ref[n, :, cols]
            for k, part in enumerate(moved):
                at = n * len(moved) + k
                value -= factor_ref[at : at + 1, cols] * part
            made[t, n] = value.astype(jnp.bfloat16)
        copy = pltpu.make_async_copy(made.at[t], out_ref.at[:, :, cols], sems.at[t])
        copy.start()
        copies.append(copy)
    for copy in copies:
        copy.wait()


def whole(array):
    return pl.BlockSpec(array.shape, lambda j: (0,) * array.ndim)


def body(solution, forcing, metric_scale, frequency, adjacency, partner, volume_matrix, trace_matrix, lift_matrix,
         block_inverse):
    current = solution[0]
    forcing_local = forcing[0]
    neighbours = adjacency[0]
    partner_rows = partner[0]
    count, dof, total = current.shape
    width = trace_matrix.shape[0] // 6
    iface_rows = partner_rows.shape[1]
    shards = lax.axis_size("space")
    peers = lax.axis_size("inst")
    section = lax.axis_index("row")
    place = jnp.stack([section, lax.axis_index("inst"), lax.axis_index("space")]).astype(jnp.int32)
    table = jnp.asarray(spectral_table(count * peers))
    smem = pl.BlockSpec(memory_space=pltpu.SMEM)
    bf16 = jnp.bfloat16

    with jax.named_scope("instances"):
        gathered = lax.all_gather(current, "inst")

    with jax.named_scope("ends"):
        up, down, cross = pl.pallas_call(
            ends_kernel,
            grid=(1,),
            out_shape=(jax.ShapeDtypeStruct((count, 2 * width, LAYER), bf16),
                       jax.ShapeDtypeStruct((count, 2 * width, LAYER), bf16),
                       jax.ShapeDtypeStruct((count, width, iface_rows), bf16)),
            in_specs=[smem,
                      pl.BlockSpec((count, dof, LANES), lambda j: (0, 0, 0)),
                      pl.BlockSpec((count, dof, LANES), lambda j: (0, 0, total // LANES - 1)),
                      whole(trace_matrix)],
            out_specs=(pl.BlockSpec((count, 2 * width, LAYER), lambda j: (0, 0, 0)),
                       pl.BlockSpec((count, 2 * width, LAYER), lambda j: (0, 0, 0)),
                       pl.BlockSpec((count, width, iface_rows), lambda j: (0, 0, 0))),
            compiler_params=pltpu.CompilerParams(vmem_limit_bytes=VMEM_LIMIT),
            cost_estimate=pl.CostEstimate(flops=8 * width * dof * LANES * 2 * count,
                                          bytes_accessed=1_000_000, transcendentals=0),
            name="ends",
        )(place, current, current, trace_matrix)

    with jax.named_scope("halo"):
        low = lax.ppermute(up, "space", [(i, (i + 1) % shards) for i in range(shards)])
        high = lax.ppermute(down, "space", [(i, (i - 1) % shards) for i in range(shards)])
    with jax.named_scope("interface"):
        pieces = [lax.ppermute(cross, ("space", "row"),
                               [(i * 2 + r, (i + d) % shards * 2 + 1 - r) for i in range(shards) for r in range(2)])
                  for d in range(shards)]

    tile = 256
    steps = total // tile
    by_tile = lambda *lead: pl.BlockSpec(lead + (tile,), lambda j: (0,) * len(lead) + (j,))
    with jax.named_scope("couple"):
        ready, factors = pl.pallas_call(
            functools.partial(couple_kernel, shards, peers),
            grid=(steps,),
            out_shape=(jax.ShapeDtypeStruct((count, dof, total), jnp.float32),
                       jax.ShapeDtypeStruct((count * count * (peers - 1), total), jnp.float32)),
            in_specs=[smem, smem, smem, by_tile(6), whole(partner_rows), whole(current), by_tile(count, dof),
                      by_tile(count, dof), by_tile(1), whole(trace_matrix), whole(lift_matrix),
                      whole(volume_matrix), whole(block_inverse), whole(low), whole(high)] + [whole(p) for p in pieces],
            out_specs=(by_tile(count, dof), by_tile(count * count * (peers - 1))),
            scratch_shapes=[pltpu.VMEM((6, count * width, total), bf16)],
            compiler_params=pltpu.CompilerParams(vmem_limit_bytes=VMEM_LIMIT),
            cost_estimate=pl.CostEstimate(
                flops=2 * count * total * (6 * width * dof * 2 + dof * dof + 6 * width * total),
                bytes_accessed=count * dof * total * 10, transcendentals=0),
            name="couple",
        )(place, frequency, table, neighbours, partner_rows, current, current, forcing_local, metric_scale,
          trace_matrix, lift_matrix, volume_matrix, block_inverse, low, high, *pieces)

    vmem = pl.BlockSpec(memory_space=pltpu.VMEM)
    with jax.named_scope("update"):
        result = pl.pallas_call(
            functools.partial(update_kernel, tile),
            out_shape=jax.ShapeDtypeStruct((count, dof, total), bf16),
            in_specs=[smem, vmem, vmem, vmem, pl.BlockSpec(memory_space=pl.ANY)],
            out_specs=pl.BlockSpec(memory_space=pl.ANY),
            scratch_shapes=[pltpu.VMEM((steps, peers - 1, count, dof, tile), bf16),
                            pltpu.VMEM((steps, count, dof, tile), bf16),
                            pltpu.SemaphoreType.DMA((steps, peers - 1)), pltpu.SemaphoreType.DMA((steps,))],
            compiler_params=pltpu.CompilerParams(vmem_limit_bytes=VMEM_LIMIT),
            cost_estimate=pl.CostEstimate(flops=2 * count * total * dof * dof * (peers - 1),
                                          bytes_accessed=count * dof * total * 8, transcendentals=0),
            name="update",
        )(place, ready, factors, block_inverse, gathered)
    return result[None]


def solution(mesh):
    in_specs = (
        P("row", "inst", None, ("groups", "space")),
        P("row", "inst", None, ("groups", "space")),
        P("row", ("groups", "space")),
        P(),
        P("row", None, ("groups", "space")),
        P("row", "inst", ("groups", "space")),
        P(),
        P(),
        P(),
        P(),
    )
    out_specs = P("row", "inst", None, ("groups", "space"))
    return jax.shard_map(body, mesh=mesh, in_specs=in_specs, out_specs=out_specs, check_vma=False)
```

```python
import functools

import jax
import jax.numpy as jnp
import numpy as np
from jax import lax
from jax.experimental import pallas as pl
from jax.experimental.pallas import tpu as pltpu
from jax.sharding import PartitionSpec as P

LAYER = 64
OPPOSITE = (1, 0, 3, 2, 5, 4)
LANES = 128
VMEM_LIMIT = 40 * 1024 * 1024


def spectral_table(instances):
    positions = np.arange(instances)
    distance = positions[:, None] - positions[None, :]
    parity = np.where(distance % 2 == 0, 1.0, -1.0)
    angles = np.pi * distance / instances
    sines = np.where(distance == 0, 1.0, np.sin(angles))
    cotangent = np.where(distance == 0, 0.0, np.cos(angles) / sines)
    return (0.5 * parity * cotangent).astype(np.float32)


def one_hot(picked, rows):
    numbers = lax.broadcasted_iota(jnp.int32, (rows, picked.shape[1]), 0)
    return jnp.where(numbers == picked, 1.0, 0.0).astype(jnp.bfloat16)


def dot(left, right):
    return jnp.dot(left, right, preferred_element_type=jnp.float32)


def ends_kernel(place_ref, first_ref, last_ref, trace_ref, up_ref, down_ref, cross_ref):
    width = trace_ref.shape[0] // 6
    section = place_ref[0]
    for n in range(first_ref.shape[0]):
        first = dot(trace_ref[...], first_ref[n]).astype(jnp.bfloat16)
        last = dot(trace_ref[4 * width :, :], last_ref[n]).astype(jnp.bfloat16)
        down_ref[n] = first[4 * width :, :LAYER]
        up_ref[n] = last[:, last.shape[1] - LAYER :]
        rows = cross_ref.shape[2]
        cross_ref[n] = jnp.where(section == 0, first[width : 2 * width, :rows], first[:width, :rows])


def couple_kernel(shards, peers, place_ref, freq_ref, table_ref, adj_ref, partner_ref, all_ref, tile_ref, forcing_ref,
                  scale_ref, trace_ref, lift_ref, volume_ref, inverse_ref, low_ref, high_ref, *rest):
    pieces, (out_ref, factor_ref, traces) = rest[:shards], rest[shards:]
    step = pl.program_id(0)
    steps = pl.num_programs(0)
    count, dof, total = all_ref.shape
    width = trace_ref.shape[0] // 6
    tile = tile_ref.shape[2]
    section, inst, space = place_ref[0], place_ref[1], place_ref[2]

    @pl.when(step == 0)
    def _():
        for n in range(count):
            for c in range(total // tile):
                cols = slice(c * tile, (c + 1) * tile)
                made = dot(trace_ref[...], all_ref[n, :, cols]).astype(jnp.bfloat16)
                for f in range(6):
                    traces[f, n * width : (n + 1) * width, cols] = made[f * width : (f + 1) * width]

    column = lax.broadcasted_iota(jnp.int32, (1, tile), 1)
    at_edge = jnp.logical_or(step == 0, step == steps - 1)

    def gathered(edge):
        found = []
        for f in range(6):
            adj = adj_ref[f : f + 1, :]
            values = dot(traces[OPPOSITE[f]], one_hot(adj - LAYER, total))
            if edge and f >= 4:
                part = slice((5 - f) * width, (6 - f) * width)
                below = jnp.concatenate([low_ref[n, part, :] for n in range(count)], axis=0)
                above = jnp.concatenate([high_ref[n, part, :] for n in range(count)], axis=0)
                values += dot(below, one_hot(adj, LAYER))
                values += dot(above, one_hot(adj - (LAYER + total), LAYER))
            values = values.astype(jnp.bfloat16)
            if edge and f < 2:
                rows = partner_ref.shape[1]
                use = jnp.logical_and(step == 0, section == 1 - f)
                crossed = []
                for n in range(count):
                    wanted = partner_ref[n : n + 1, :]
                    arrived = jnp.zeros((width, rows), jnp.float32)
                    for d in range(shards):
                        source = lax.rem(space - d + shards, shards)
                        arrived += dot(pieces[d][n], one_hot(wanted - source * rows, rows))
                    crossed.append(arrived)
                crossed = jnp.concatenate(crossed, axis=0).astype(jnp.bfloat16)
                crossed = jnp.concatenate(
                    [crossed, jnp.zeros((count * width, tile - rows), jnp.bfloat16)], axis=1)
                take = jnp.logical_and(column < rows, use)
                values = jnp.where(take, crossed, values)
            found.append(values)
        return found

    def finish(edge):
        found = gathered(edge)
        frequency = freq_ref[0]
        scale = scale_ref[...]
        inverse_scale = 1.0 / scale
        for n in range(count):
            for d in range(1, peers):
                owner = lax.rem(inst - d + peers, peers)
                for m in range(count):
                    weight = table_ref[inst * count + n, owner * count + m] * frequency
                    at = (n * (peers - 1) + d - 1) * count + m
                    factor_ref[at : at + 1, :] = weight * inverse_scale
        for n in range(count):
            beside = jnp.concatenate([v[n * width : (n + 1) * width] for v in found], axis=0)
            inner = dot(lift_ref[...], beside) + dot(volume_ref[...], tile_ref[n])
            value = forcing_ref[n].astype(jnp.float32) - scale * inner
            for m in range(count):
                weight = table_ref[inst * count + n, inst * count + m] * frequency
                value -= weight * tile_ref[m].astype(jnp.float32)
            update = dot(inverse_ref[...], value.astype(jnp.bfloat16))
            out_ref[n] = tile_ref[n].astype(jnp.float32) + update * inverse_scale

    @pl.when(at_edge)
    def _():
        finish(True)

    @pl.when(jnp.logical_not(at_edge))
    def _():
        finish(False)


def update_kernel(tile, parts, ready_ref, factor_ref, inverse_ref, *rest):
    others, (out_ref, made, sems) = rest[:-3], rest[-3:]
    count, dof, total = ready_ref.shape
    copies = []
    for p in range(parts):
        whole_part = slice(p * total // parts, (p + 1) * total // parts)
        for start in range(whole_part.start, whole_part.stop, tile):
            cols = slice(start, start + tile)
            moved = [dot(inverse_ref[...], other[m, :, cols]) for other in others for m in range(count)]
            for n in range(count):
                value = ready_ref[n, :, cols]
                for k, part in enumerate(moved):
                    at = n * len(moved) + k
                    value -= factor_ref[at : at + 1, cols] * part
                made[n, :, cols] = value.astype(jnp.bfloat16)
        copy = pltpu.make_async_copy(made.at[:, :, whole_part], out_ref.at[:, :, whole_part], sems.at[p])
        copy.start()
        copies.append(copy)
    for copy in copies:
        copy.wait()


def whole(array):
    return pl.BlockSpec(array.shape, lambda j: (0,) * array.ndim)


def body(solution, forcing, metric_scale, frequency, adjacency, partner, volume_matrix, trace_matrix, lift_matrix,
         block_inverse):
    current = solution[0]
    forcing_local = forcing[0]
    neighbours = adjacency[0]
    partner_rows = partner[0]
    count, dof, total = current.shape
    width = trace_matrix.shape[0] // 6
    iface_rows = partner_rows.shape[1]
    shards = lax.axis_size("space")
    peers = lax.axis_size("inst")
    section = lax.axis_index("row")
    place = jnp.stack([section, lax.axis_index("inst"), lax.axis_index("space")]).astype(jnp.int32)
    table = jnp.asarray(spectral_table(count * peers))
    smem = pl.BlockSpec(memory_space=pltpu.SMEM)
    bf16 = jnp.bfloat16

    with jax.named_scope("instances"):
        others = [lax.ppermute(current, "inst", [(i, (i + d) % peers) for i in range(peers)])
                  for d in range(1, peers)]

    with jax.named_scope("ends"):
        up, down, cross = pl.pallas_call(
            ends_kernel,
            grid=(1,),
            out_shape=(jax.ShapeDtypeStruct((count, 2 * width, LAYER), bf16),
                       jax.ShapeDtypeStruct((count, 2 * width, LAYER), bf16),
                       jax.ShapeDtypeStruct((count, width, iface_rows), bf16)),
            in_specs=[smem,
                      pl.BlockSpec((count, dof, LANES), lambda j: (0, 0, 0)),
                      pl.BlockSpec((count, dof, LANES), lambda j: (0, 0, total // LANES - 1)),
                      whole(trace_matrix)],
            out_specs=(pl.BlockSpec((count, 2 * width, LAYER), lambda j: (0, 0, 0)),
                       pl.BlockSpec((count, 2 * width, LAYER), lambda j: (0, 0, 0)),
                       pl.BlockSpec((count, width, iface_rows), lambda j: (0, 0, 0))),
            compiler_params=pltpu.CompilerParams(vmem_limit_bytes=VMEM_LIMIT),
            cost_estimate=pl.CostEstimate(flops=8 * width * dof * LANES * 2 * count,
                                          bytes_accessed=1_000_000, transcendentals=0),
            name="ends",
        )(place, current, current, trace_matrix)

    with jax.named_scope("halo"):
        low = lax.ppermute(up, "space", [(i, (i + 1) % shards) for i in range(shards)])
        high = lax.ppermute(down, "space", [(i, (i - 1) % shards) for i in range(shards)])
    with jax.named_scope("interface"):
        pieces = [lax.ppermute(cross, ("space", "row"),
                               [(i * 2 + r, (i + d) % shards * 2 + 1 - r) for i in range(shards) for r in range(2)])
                  for d in range(shards)]

    tile = 256
    steps = total // tile
    by_tile = lambda *lead: pl.BlockSpec(lead + (tile,), lambda j: (0,) * len(lead) + (j,))
    with jax.named_scope("couple"):
        ready, factors = pl.pallas_call(
            functools.partial(couple_kernel, shards, peers),
            grid=(steps,),
            out_shape=(jax.ShapeDtypeStruct((count, dof, total), jnp.float32),
                       jax.ShapeDtypeStruct((count * count * (peers - 1), total), jnp.float32)),
            in_specs=[smem, smem, smem, by_tile(6), whole(partner_rows), whole(current), by_tile(count, dof),
                      by_tile(count, dof), by_tile(1), whole(trace_matrix), whole(lift_matrix),
                      whole(volume_matrix), whole(block_inverse), whole(low), whole(high)] + [whole(p) for p in pieces],
            out_specs=(by_tile(count, dof), by_tile(count * count * (peers - 1))),
            scratch_shapes=[pltpu.VMEM((6, count * width, total), bf16)],
            compiler_params=pltpu.CompilerParams(vmem_limit_bytes=VMEM_LIMIT),
            cost_estimate=pl.CostEstimate(
                flops=2 * count * total * (6 * width * dof * 2 + dof * dof + 6 * width * total),
                bytes_accessed=count * dof * total * 10, transcendentals=0),
            name="couple",
        )(place, frequency, table, neighbours, partner_rows, current, current, forcing_local, metric_scale,
          trace_matrix, lift_matrix, volume_matrix, block_inverse, low, high, *pieces)

    vmem = pl.BlockSpec(memory_space=pltpu.VMEM)
    parts = 2
    with jax.named_scope("update"):
        result = pl.pallas_call(
            functools.partial(update_kernel, tile, parts),
            out_shape=jax.ShapeDtypeStruct((count, dof, total), bf16),
            in_specs=[vmem] * (2 + peers),
            out_specs=pl.BlockSpec(memory_space=pl.ANY),
            scratch_shapes=[pltpu.VMEM((count, dof, total), bf16), pltpu.SemaphoreType.DMA((parts,))],
            compiler_params=pltpu.CompilerParams(vmem_limit_bytes=VMEM_LIMIT),
            cost_estimate=pl.CostEstimate(flops=2 * count * total * dof * dof * (peers - 1),
                                          bytes_accessed=count * dof * total * 8, transcendentals=0),
            name="update",
        )(ready, factors, block_inverse, *others)
    return result[None]


def solution(mesh):
    in_specs = (
        P("row", "inst", None, ("groups", "space")),
        P("row", "inst", None, ("groups", "space")),
        P("row", ("groups", "space")),
        P(),
        P("row", None, ("groups", "space")),
        P("row", "inst", ("groups", "space")),
        P(),
        P(),
        P(),
        P(),
    )
    out_specs = P("row", "inst", None, ("groups", "space"))
    return jax.shard_map(body, mesh=mesh, in_specs=in_specs, out_specs=out_specs, check_vma=False)
```

```python
import functools

import jax
import jax.numpy as jnp
import numpy as np
from jax import lax
from jax.experimental import pallas as pl
from jax.experimental.pallas import tpu as pltpu
from jax.sharding import PartitionSpec as P

LAYER = 64
OPPOSITE = (1, 0, 3, 2, 5, 4)
LANES = 128
VMEM_LIMIT = 40 * 1024 * 1024


def spectral_table(instances):
    positions = np.arange(instances)
    distance = positions[:, None] - positions[None, :]
    parity = np.where(distance % 2 == 0, 1.0, -1.0)
    angles = np.pi * distance / instances
    sines = np.where(distance == 0, 1.0, np.sin(angles))
    cotangent = np.where(distance == 0, 0.0, np.cos(angles) / sines)
    return (0.5 * parity * cotangent).astype(np.float32)


def one_hot(picked, rows):
    numbers = lax.broadcasted_iota(jnp.int32, (rows, picked.shape[1]), 0)
    return jnp.where(numbers == picked, 1.0, 0.0).astype(jnp.bfloat16)


def dot(left, right):
    return jnp.dot(left, right, preferred_element_type=jnp.float32)


def ends_kernel(place_ref, first_ref, last_ref, trace_ref, up_ref, down_ref, cross_ref):
    width = trace_ref.shape[0] // 6
    section = place_ref[0]
    for n in range(first_ref.shape[0]):
        first = dot(trace_ref[...], first_ref[n]).astype(jnp.bfloat16)
        last = dot(trace_ref[4 * width :, :], last_ref[n]).astype(jnp.bfloat16)
        down_ref[n] = first[4 * width :, :LAYER]
        up_ref[n] = last[:, last.shape[1] - LAYER :]
        rows = cross_ref.shape[2]
        cross_ref[n] = jnp.where(section == 0, first[width : 2 * width, :rows], first[:width, :rows])


def couple_kernel(shards, peers, place_ref, freq_ref, table_ref, adj_ref, partner_ref, all_ref, tile_ref, forcing_ref,
                  scale_ref, trace_ref, lift_ref, volume_ref, inverse_ref, low_ref, high_ref, *rest):
    pieces, (out_ref, factor_ref, traces) = rest[:shards], rest[shards:]
    step = pl.program_id(0)
    steps = pl.num_programs(0)
    count, dof, total = all_ref.shape
    width = trace_ref.shape[0] // 6
    tile = tile_ref.shape[2]
    section, inst, space = place_ref[0], place_ref[1], place_ref[2]

    @pl.when(step == 0)
    def _():
        for n in range(count):
            for c in range(total // tile):
                cols = slice(c * tile, (c + 1) * tile)
                made = dot(trace_ref[...], all_ref[n, :, cols]).astype(jnp.bfloat16)
                for f in range(6):
                    traces[f, n * width : (n + 1) * width, cols] = made[f * width : (f + 1) * width]

    column = lax.broadcasted_iota(jnp.int32, (1, tile), 1)
    at_edge = jnp.logical_or(step == 0, step == steps - 1)

    def gathered(edge):
        found = []
        for f in range(6):
            adj = adj_ref[f : f + 1, :]
            values = dot(traces[OPPOSITE[f]], one_hot(adj - LAYER, total))
            if edge and f >= 4:
                part = slice((5 - f) * width, (6 - f) * width)
                below = jnp.concatenate([low_ref[n, part, :] for n in range(count)], axis=0)
                above = jnp.concatenate([high_ref[n, part, :] for n in range(count)], axis=0)
                values += dot(below, one_hot(adj, LAYER))
                values += dot(above, one_hot(adj - (LAYER + total), LAYER))
            values = values.astype(jnp.bfloat16)
            if edge and f < 2:
                rows = partner_ref.shape[1]
                use = jnp.logical_and(step == 0, section == 1 - f)
                crossed = []
                for n in range(count):
                    wanted = partner_ref[n : n + 1, :]
                    arrived = jnp.zeros((width, rows), jnp.float32)
                    for d in range(shards):
                        source = lax.rem(space - d + shards, shards)
                        arrived += dot(pieces[d][n], one_hot(wanted - source * rows, rows))
                    crossed.append(arrived)
                crossed = jnp.concatenate(crossed, axis=0).astype(jnp.bfloat16)
                crossed = jnp.concatenate(
                    [crossed, jnp.zeros((count * width, tile - rows), jnp.bfloat16)], axis=1)
                take = jnp.logical_and(column < rows, use)
                values = jnp.where(take, crossed, values)
            found.append(values)
        return found

    def finish(edge):
        found = gathered(edge)
        frequency = freq_ref[0]
        scale = scale_ref[...]
        inverse_scale = 1.0 / scale
        for n in range(count):
            for d in range(1, peers):
                owner = lax.rem(inst - d + peers, peers)
                for m in range(count):
                    instance = lax.rem(inst + m, count) if paired(peers, count) else m
                    weight = table_ref[inst * count + n, owner * count + instance] * frequency
                    at = (n * (peers - 1) + d - 1) * count + m
                    factor_ref[at : at + 1, :] = weight * inverse_scale
        for n in range(count):
            beside = jnp.concatenate([v[n * width : (n + 1) * width] for v in found], axis=0)
            inner = dot(lift_ref[...], beside) + dot(volume_ref[...], tile_ref[n])
            value = forcing_ref[n].astype(jnp.float32) - scale * inner
            for m in range(count):
                weight = table_ref[inst * count + n, inst * count + m] * frequency
                value -= weight * tile_ref[m].astype(jnp.float32)
            update = dot(inverse_ref[...], value.astype(jnp.bfloat16))
            out_ref[n] = tile_ref[n].astype(jnp.float32) + update * inverse_scale

    @pl.when(at_edge)
    def _():
        finish(True)

    @pl.when(jnp.logical_not(at_edge))
    def _():
        finish(False)


def fold_kernel(tile, place_ref, ready_ref, factor_ref, inverse_ref, other_ref, out_ref):
    count, dof, total = ready_ref.shape
    slot = 1 - place_ref[1]
    for t in range(total // tile):
        cols = slice(t * tile, (t + 1) * tile)
        moved = dot(inverse_ref[...], other_ref[slot, :, cols])
        for n in range(count):
            at = n * count
            out_ref[n, :, cols] = ready_ref[n, :, cols] - factor_ref[at : at + 1, cols] * moved


def update_kernel(tile, place_ref, ready_ref, factor_ref, inverse_ref, other_ref, out_ref, made, sems):
    count, dof, total = ready_ref.shape
    slot = place_ref[1]
    copies = []
    for t in range(total // tile):
        cols = slice(t * tile, (t + 1) * tile)
        moved = dot(inverse_ref[...], other_ref[slot, :, cols])
        for n in range(count):
            at = n * count + 1
            made[t, n] = (ready_ref[n, :, cols] - factor_ref[at : at + 1, cols] * moved).astype(jnp.bfloat16)
        copy = pltpu.make_async_copy(made.at[t], out_ref.at[:, :, cols], sems.at[t])
        copy.start()
        copies.append(copy)
    for copy in copies:
        copy.wait()


def ring_update_kernel(tile, ready_ref, factor_ref, inverse_ref, *rest):
    others, (out_ref, made, sems) = rest[:-3], rest[-3:]
    count, dof, total = ready_ref.shape
    copies = []
    for t in range(total // tile):
        cols = slice(t * tile, (t + 1) * tile)
        moved = [dot(inverse_ref[...], other[m, :, cols]) for other in others for m in range(count)]
        for n in range(count):
            value = ready_ref[n, :, cols]
            for k, part in enumerate(moved):
                at = n * len(moved) + k
                value -= factor_ref[at : at + 1, cols] * part
            made[t, n] = value.astype(jnp.bfloat16)
        copy = pltpu.make_async_copy(made.at[t], out_ref.at[:, :, cols], sems.at[t])
        copy.start()
        copies.append(copy)
    for copy in copies:
        copy.wait()


def paired(peers, count):
    return peers == 2 and count == 2


def whole(array):
    return pl.BlockSpec(array.shape, lambda j: (0,) * array.ndim)


def body(solution, forcing, metric_scale, frequency, adjacency, partner, volume_matrix, trace_matrix, lift_matrix,
         block_inverse):
    current = solution[0]
    forcing_local = forcing[0]
    neighbours = adjacency[0]
    partner_rows = partner[0]
    count, dof, total = current.shape
    width = trace_matrix.shape[0] // 6
    iface_rows = partner_rows.shape[1]
    shards = lax.axis_size("space")
    peers = lax.axis_size("inst")
    section = lax.axis_index("row")
    place = jnp.stack([section, lax.axis_index("inst"), lax.axis_index("space")]).astype(jnp.int32)
    table = jnp.asarray(spectral_table(count * peers))
    smem = pl.BlockSpec(memory_space=pltpu.SMEM)
    bf16 = jnp.bfloat16

    with jax.named_scope("instances"):
        if paired(peers, count):
            others = [lax.all_to_all(current, "inst", split_axis=0, concat_axis=0, tiled=True, axis_index_groups=order)
                      for order in ([[0, 1]], [[1, 0]])]
        else:
            others = [lax.ppermute(current, "inst", [(i, (i + d) % peers) for i in range(peers)])
                      for d in range(1, peers)]

    with jax.named_scope("ends"):
        up, down, cross = pl.pallas_call(
            ends_kernel,
            grid=(1,),
            out_shape=(jax.ShapeDtypeStruct((count, 2 * width, LAYER), bf16),
                       jax.ShapeDtypeStruct((count, 2 * width, LAYER), bf16),
                       jax.ShapeDtypeStruct((count, width, iface_rows), bf16)),
            in_specs=[smem,
                      pl.BlockSpec((count, dof, LANES), lambda j: (0, 0, 0)),
                      pl.BlockSpec((count, dof, LANES), lambda j: (0, 0, total // LANES - 1)),
                      whole(trace_matrix)],
            out_specs=(pl.BlockSpec((count, 2 * width, LAYER), lambda j: (0, 0, 0)),
                       pl.BlockSpec((count, 2 * width, LAYER), lambda j: (0, 0, 0)),
                       pl.BlockSpec((count, width, iface_rows), lambda j: (0, 0, 0))),
            compiler_params=pltpu.CompilerParams(vmem_limit_bytes=VMEM_LIMIT),
            cost_estimate=pl.CostEstimate(flops=8 * width * dof * LANES * 2 * count,
                                          bytes_accessed=1_000_000, transcendentals=0),
            name="ends",
        )(place, current, current, trace_matrix)

    with jax.named_scope("halo"):
        low = lax.ppermute(up, "space", [(i, (i + 1) % shards) for i in range(shards)])
        high = lax.ppermute(down, "space", [(i, (i - 1) % shards) for i in range(shards)])
    with jax.named_scope("interface"):
        pieces = [lax.ppermute(cross, ("space", "row"),
                               [(i * 2 + r, (i + d) % shards * 2 + 1 - r) for i in range(shards) for r in range(2)])
                  for d in range(shards)]

    tile = 256
    steps = total // tile
    by_tile = lambda *lead: pl.BlockSpec(lead + (tile,), lambda j: (0,) * len(lead) + (j,))
    with jax.named_scope("couple"):
        ready, factors = pl.pallas_call(
            functools.partial(couple_kernel, shards, peers),
            grid=(steps,),
            out_shape=(jax.ShapeDtypeStruct((count, dof, total), jnp.float32),
                       jax.ShapeDtypeStruct((count * count * (peers - 1), total), jnp.float32)),
            in_specs=[smem, smem, smem, by_tile(6), whole(partner_rows), whole(current), by_tile(count, dof),
                      by_tile(count, dof), by_tile(1), whole(trace_matrix), whole(lift_matrix),
                      whole(volume_matrix), whole(block_inverse), whole(low), whole(high)] + [whole(p) for p in pieces],
            out_specs=(by_tile(count, dof), by_tile(count * count * (peers - 1))),
            scratch_shapes=[pltpu.VMEM((6, count * width, total), bf16)],
            compiler_params=pltpu.CompilerParams(vmem_limit_bytes=VMEM_LIMIT),
            cost_estimate=pl.CostEstimate(
                flops=2 * count * total * (6 * width * dof * 2 + dof * dof + 6 * width * total),
                bytes_accessed=count * dof * total * 10, transcendentals=0),
            name="couple",
        )(place, frequency, table, neighbours, partner_rows, current, current, forcing_local, metric_scale,
          trace_matrix, lift_matrix, volume_matrix, block_inverse, low, high, *pieces)

    vmem = pl.BlockSpec(memory_space=pltpu.VMEM)
    half = pl.CostEstimate(flops=count * total * dof * dof, bytes_accessed=count * dof * total * 4, transcendentals=0)
    with jax.named_scope("update"):
        if paired(peers, count):
            folded = pl.pallas_call(
                functools.partial(fold_kernel, tile),
                out_shape=jax.ShapeDtypeStruct((count, dof, total), jnp.float32),
                in_specs=[smem] + [vmem] * 4,
                out_specs=vmem,
                input_output_aliases={1: 0},
                compiler_params=pltpu.CompilerParams(vmem_limit_bytes=VMEM_LIMIT),
                cost_estimate=half,
                name="fold",
            )(place, ready, factors, block_inverse, others[0])
            kernel, operands = update_kernel, (place, folded, factors, block_inverse, others[1])
        else:
            kernel, operands = ring_update_kernel, (ready, factors, block_inverse, *others)
        result = pl.pallas_call(
            functools.partial(kernel, tile),
            out_shape=jax.ShapeDtypeStruct((count, dof, total), bf16),
            in_specs=([smem] + [vmem] * 4) if paired(peers, count) else [vmem] * (2 + peers),
            out_specs=pl.BlockSpec(memory_space=pl.ANY),
            scratch_shapes=[pltpu.VMEM((steps, count, dof, tile), bf16), pltpu.SemaphoreType.DMA((steps,))],
            compiler_params=pltpu.CompilerParams(vmem_limit_bytes=VMEM_LIMIT),
            cost_estimate=half,
            name="update",
        )(*operands)
    return result[None]


def solution(mesh):
    in_specs = (
        P("row", "inst", None, ("groups", "space")),
        P("row", "inst", None, ("groups", "space")),
        P("row", ("groups", "space")),
        P(),
        P("row", None, ("groups", "space")),
        P("row", "inst", ("groups", "space")),
        P(),
        P(),
        P(),
        P(),
    )
    out_specs = P("row", "inst", None, ("groups", "space"))
    return jax.shard_map(body, mesh=mesh, in_specs=in_specs, out_specs=out_specs, check_vma=False)
```

```python
import functools

import jax
import jax.numpy as jnp
import numpy as np
from jax import lax
from jax.experimental import pallas as pl
from jax.experimental.pallas import tpu as pltpu
from jax.sharding import PartitionSpec as P

LAYER = 64
OPPOSITE = (1, 0, 3, 2, 5, 4)
LANES = 128
VMEM_LIMIT = 40 * 1024 * 1024


def spectral_table(instances):
    positions = np.arange(instances)
    distance = positions[:, None] - positions[None, :]
    parity = np.where(distance % 2 == 0, 1.0, -1.0)
    angles = np.pi * distance / instances
    sines = np.where(distance == 0, 1.0, np.sin(angles))
    cotangent = np.where(distance == 0, 0.0, np.cos(angles) / sines)
    return (0.5 * parity * cotangent).astype(np.float32)


def one_hot(picked, rows):
    numbers = lax.broadcasted_iota(jnp.int32, (rows, picked.shape[1]), 0)
    return jnp.where(numbers == picked, 1.0, 0.0).astype(jnp.bfloat16)


def dot(left, right):
    return jnp.dot(left, right, preferred_element_type=jnp.float32)


def ends_kernel(place_ref, first_ref, last_ref, trace_ref, up_ref, down_ref, cross_ref):
    width = trace_ref.shape[0] // 6
    section = place_ref[0]
    for n in range(first_ref.shape[0]):
        first = dot(trace_ref[...], first_ref[n]).astype(jnp.bfloat16)
        last = dot(trace_ref[4 * width :, :], last_ref[n]).astype(jnp.bfloat16)
        down_ref[n] = first[4 * width :, :LAYER]
        up_ref[n] = last[:, last.shape[1] - LAYER :]
        rows = cross_ref.shape[2]
        cross_ref[n] = jnp.where(section == 0, first[width : 2 * width, :rows], first[:width, :rows])


def couple_kernel(shards, peers, place_ref, freq_ref, table_ref, adj_ref, partner_ref, all_ref, tile_ref, forcing_ref,
                  scale_ref, trace_ref, lift_ref, volume_ref, inverse_ref, low_ref, high_ref, *rest):
    pieces, (out_ref, factor_ref, traces) = rest[:shards], rest[shards:]
    step = pl.program_id(0)
    steps = pl.num_programs(0)
    count, dof, total = all_ref.shape
    width = trace_ref.shape[0] // 6
    tile = tile_ref.shape[2]
    section, inst, space = place_ref[0], place_ref[1], place_ref[2]

    @pl.when(step == 0)
    def _():
        for n in range(count):
            for c in range(total // tile):
                cols = slice(c * tile, (c + 1) * tile)
                made = dot(trace_ref[...], all_ref[n, :, cols]).astype(jnp.bfloat16)
                for f in range(6):
                    traces[f, n * width : (n + 1) * width, cols] = made[f * width : (f + 1) * width]

    column = lax.broadcasted_iota(jnp.int32, (1, tile), 1)
    at_edge = jnp.logical_or(step == 0, step == steps - 1)

    def gathered(edge):
        found = []
        for f in range(6):
            adj = adj_ref[f : f + 1, :]
            values = dot(traces[OPPOSITE[f]], one_hot(adj - LAYER, total))
            if edge and f >= 4:
                part = slice((5 - f) * width, (6 - f) * width)
                below = jnp.concatenate([low_ref[n, part, :] for n in range(count)], axis=0)
                above = jnp.concatenate([high_ref[n, part, :] for n in range(count)], axis=0)
                values += dot(below, one_hot(adj, LAYER))
                values += dot(above, one_hot(adj - (LAYER + total), LAYER))
            values = values.astype(jnp.bfloat16)
            if edge and f < 2:
                rows = partner_ref.shape[1]
                use = jnp.logical_and(step == 0, section == 1 - f)
                crossed = []
                for n in range(count):
                    wanted = partner_ref[n : n + 1, :]
                    arrived = jnp.zeros((width, rows), jnp.float32)
                    for d in range(shards):
                        source = lax.rem(space - d + shards, shards)
                        arrived += dot(pieces[d][n], one_hot(wanted - source * rows, rows))
                    crossed.append(arrived)
                crossed = jnp.concatenate(crossed, axis=0).astype(jnp.bfloat16)
                crossed = jnp.concatenate(
                    [crossed, jnp.zeros((count * width, tile - rows), jnp.bfloat16)], axis=1)
                take = jnp.logical_and(column < rows, use)
                values = jnp.where(take, crossed, values)
            found.append(values)
        return found

    def finish(edge):
        found = gathered(edge)
        frequency = freq_ref[0]
        scale = scale_ref[...]
        inverse_scale = 1.0 / scale
        for n in range(count):
            for d in range(1, peers):
                owner = lax.rem(inst - d + peers, peers)
                for m in range(count):
                    weight = table_ref[inst * count + n, owner * count + m] * frequency
                    at = (n * (peers - 1) + d - 1) * count + m
                    factor_ref[at : at + 1, :] = weight * inverse_scale
        for n in range(count):
            beside = jnp.concatenate([v[n * width : (n + 1) * width] for v in found], axis=0)
            inner = dot(lift_ref[...], beside) + dot(volume_ref[...], tile_ref[n])
            value = forcing_ref[n].astype(jnp.float32) - scale * inner
            for m in range(count):
                weight = table_ref[inst * count + n, inst * count + m] * frequency
                value -= weight * tile_ref[m].astype(jnp.float32)
            update = dot(inverse_ref[...], value.astype(jnp.bfloat16))
            out_ref[n] = tile_ref[n].astype(jnp.float32) + update * inverse_scale

    @pl.when(at_edge)
    def _():
        finish(True)

    @pl.when(jnp.logical_not(at_edge))
    def _():
        finish(False)


def update_kernel(cuts, ready_ref, factor_ref, inverse_ref, *rest):
    others, (out_ref, made, sems) = rest[:-3], rest[-3:]
    count = ready_ref.shape[0]
    copies = []
    for t, (first, last) in enumerate(zip(cuts[:-1], cuts[1:])):
        cols = slice(first, last)
        moved = [dot(inverse_ref[...], other[m, :, cols]) for other in others for m in range(count)]
        for n in range(count):
            value = ready_ref[n, :, cols]
            for k, part in enumerate(moved):
                at = n * len(moved) + k
                value -= factor_ref[at : at + 1, cols] * part
            made[n, :, cols] = value.astype(jnp.bfloat16)
            copy = pltpu.make_async_copy(made.at[n, :, cols], out_ref.at[n, :, cols], sems.at[t, n])
            copy.start()
            copies.append(copy)
    for copy in copies:
        copy.wait()


def whole(array):
    return pl.BlockSpec(array.shape, lambda j: (0,) * array.ndim)


def body(solution, forcing, metric_scale, frequency, adjacency, partner, volume_matrix, trace_matrix, lift_matrix,
         block_inverse):
    current = solution[0]
    forcing_local = forcing[0]
    neighbours = adjacency[0]
    partner_rows = partner[0]
    count, dof, total = current.shape
    width = trace_matrix.shape[0] // 6
    iface_rows = partner_rows.shape[1]
    shards = lax.axis_size("space")
    peers = lax.axis_size("inst")
    section = lax.axis_index("row")
    place = jnp.stack([section, lax.axis_index("inst"), lax.axis_index("space")]).astype(jnp.int32)
    table = jnp.asarray(spectral_table(count * peers))
    smem = pl.BlockSpec(memory_space=pltpu.SMEM)
    bf16 = jnp.bfloat16

    with jax.named_scope("instances"):
        others = [lax.ppermute(current, "inst", [(i, (i + d) % peers) for i in range(peers)])
                  for d in range(1, peers)]

    with jax.named_scope("ends"):
        up, down, cross = pl.pallas_call(
            ends_kernel,
            grid=(1,),
            out_shape=(jax.ShapeDtypeStruct((count, 2 * width, LAYER), bf16),
                       jax.ShapeDtypeStruct((count, 2 * width, LAYER), bf16),
                       jax.ShapeDtypeStruct((count, width, iface_rows), bf16)),
            in_specs=[smem,
                      pl.BlockSpec((count, dof, LANES), lambda j: (0, 0, 0)),
                      pl.BlockSpec((count, dof, LANES), lambda j: (0, 0, total // LANES - 1)),
                      whole(trace_matrix)],
            out_specs=(pl.BlockSpec((count, 2 * width, LAYER), lambda j: (0, 0, 0)),
                       pl.BlockSpec((count, 2 * width, LAYER), lambda j: (0, 0, 0)),
                       pl.BlockSpec((count, width, iface_rows), lambda j: (0, 0, 0))),
            compiler_params=pltpu.CompilerParams(vmem_limit_bytes=VMEM_LIMIT),
            cost_estimate=pl.CostEstimate(flops=8 * width * dof * LANES * 2 * count,
                                          bytes_accessed=1_000_000, transcendentals=0),
            name="ends",
        )(place, current, current, trace_matrix)

    with jax.named_scope("halo"):
        low = lax.ppermute(up, "space", [(i, (i + 1) % shards) for i in range(shards)])
        high = lax.ppermute(down, "space", [(i, (i - 1) % shards) for i in range(shards)])
    with jax.named_scope("interface"):
        pieces = [lax.ppermute(cross, ("space", "row"),
                               [(i * 2 + r, (i + d) % shards * 2 + 1 - r) for i in range(shards) for r in range(2)])
                  for d in range(shards)]

    tile = 256
    steps = total // tile
    by_tile = lambda *lead: pl.BlockSpec(lead + (tile,), lambda j: (0,) * len(lead) + (j,))
    with jax.named_scope("couple"):
        ready, factors = pl.pallas_call(
            functools.partial(couple_kernel, shards, peers),
            grid=(steps,),
            out_shape=(jax.ShapeDtypeStruct((count, dof, total), jnp.float32),
                       jax.ShapeDtypeStruct((count * count * (peers - 1), total), jnp.float32)),
            in_specs=[smem, smem, smem, by_tile(6), whole(partner_rows), whole(current), by_tile(count, dof),
                      by_tile(count, dof), by_tile(1), whole(trace_matrix), whole(lift_matrix),
                      whole(volume_matrix), whole(block_inverse), whole(low), whole(high)] + [whole(p) for p in pieces],
            out_specs=(by_tile(count, dof), by_tile(count * count * (peers - 1))),
            scratch_shapes=[pltpu.VMEM((6, count * width, total), bf16)],
            compiler_params=pltpu.CompilerParams(vmem_limit_bytes=VMEM_LIMIT),
            cost_estimate=pl.CostEstimate(
                flops=2 * count * total * (6 * width * dof * 2 + dof * dof + 6 * width * total),
                bytes_accessed=count * dof * total * 10, transcendentals=0),
            name="couple",
        )(place, frequency, table, neighbours, partner_rows, current, current, forcing_local, metric_scale,
          trace_matrix, lift_matrix, volume_matrix, block_inverse, low, high, *pieces)

    vmem = pl.BlockSpec(memory_space=pltpu.VMEM)
    cuts = [0] + list(range(tile // 2, total, tile)) + [total]
    with jax.named_scope("update"):
        result = pl.pallas_call(
            functools.partial(update_kernel, cuts),
            out_shape=jax.ShapeDtypeStruct((count, dof, total), bf16),
            in_specs=[vmem] * (2 + peers),
            out_specs=pl.BlockSpec(memory_space=pl.ANY),
            scratch_shapes=[pltpu.VMEM((count, dof, total), bf16),
                            pltpu.SemaphoreType.DMA((len(cuts) - 1, count))],
            compiler_params=pltpu.CompilerParams(vmem_limit_bytes=VMEM_LIMIT),
            cost_estimate=pl.CostEstimate(flops=2 * count * total * dof * dof * (peers - 1),
                                          bytes_accessed=count * dof * total * 8, transcendentals=0),
            name="update",
        )(ready, factors, block_inverse, *others)
    return result[None]


def solution(mesh):
    in_specs = (
        P("row", "inst", None, ("groups", "space")),
        P("row", "inst", None, ("groups", "space")),
        P("row", ("groups", "space")),
        P(),
        P("row", None, ("groups", "space")),
        P("row", "inst", ("groups", "space")),
        P(),
        P(),
        P(),
        P(),
    )
    out_specs = P("row", "inst", None, ("groups", "space"))
    return jax.shard_map(body, mesh=mesh, in_specs=in_specs, out_specs=out_specs, check_vma=False)
```

```python
import functools

import jax
import jax.numpy as jnp
import numpy as np
from jax import lax
from jax.experimental import pallas as pl
from jax.experimental.pallas import tpu as pltpu
from jax.sharding import PartitionSpec as P

LAYER = 64
OPPOSITE = (1, 0, 3, 2, 5, 4)
LANES = 128
STRIP = 32
VMEM_LIMIT = 40 * 1024 * 1024


def spectral_table(instances):
    positions = np.arange(instances)
    distance = positions[:, None] - positions[None, :]
    parity = np.where(distance % 2 == 0, 1.0, -1.0)
    angles = np.pi * distance / instances
    sines = np.where(distance == 0, 1.0, np.sin(angles))
    cotangent = np.where(distance == 0, 0.0, np.cos(angles) / sines)
    return (0.5 * parity * cotangent).astype(np.float32)


def one_hot(picked, rows):
    numbers = lax.broadcasted_iota(jnp.int32, (rows, picked.shape[1]), 0)
    return jnp.where(numbers == picked, 1.0, 0.0).astype(jnp.bfloat16)


def dot(left, right):
    return jnp.dot(left, right, preferred_element_type=jnp.float32)


def ends_kernel(place_ref, first_ref, last_ref, trace_ref, up_ref, down_ref, cross_ref):
    width = trace_ref.shape[0] // 6
    section = place_ref[0]
    for n in range(first_ref.shape[0]):
        first = dot(trace_ref[...], first_ref[n]).astype(jnp.bfloat16)
        last = dot(trace_ref[4 * width :, :], last_ref[n]).astype(jnp.bfloat16)
        down_ref[n] = first[4 * width :, :LAYER]
        up_ref[n] = last[:, last.shape[1] - LAYER :]
        rows = cross_ref.shape[2]
        cross_ref[n] = jnp.where(section == 0, first[width : 2 * width, :rows], first[:width, :rows])


def couple_kernel(shards, peers, place_ref, freq_ref, table_ref, adj_ref, partner_ref, all_ref, tile_ref, forcing_ref,
                  scale_ref, trace_ref, lift_ref, volume_ref, inverse_ref, low_ref, high_ref, *rest):
    pieces, (out_ref, factor_ref, traces) = rest[:shards], rest[shards:]
    step = pl.program_id(0)
    steps = pl.num_programs(0)
    count, dof, total = all_ref.shape
    width = trace_ref.shape[0] // 6
    tile = tile_ref.shape[2]
    section, inst, space = place_ref[0], place_ref[1], place_ref[2]

    @pl.when(step == 0)
    def _():
        for n in range(count):
            for c in range(total // tile):
                cols = slice(c * tile, (c + 1) * tile)
                made = dot(trace_ref[...], all_ref[n, :, cols]).astype(jnp.bfloat16)
                for f in range(6):
                    traces[f, n * width : (n + 1) * width, cols] = made[f * width : (f + 1) * width]

    column = lax.broadcasted_iota(jnp.int32, (1, tile), 1)
    at_edge = jnp.logical_or(step == 0, step == steps - 1)

    def gathered(edge):
        found = []
        for f in range(6):
            adj = adj_ref[f : f + 1, :]
            values = dot(traces[OPPOSITE[f]], one_hot(adj - LAYER, total))
            if edge and f >= 4:
                part = slice((5 - f) * width, (6 - f) * width)
                below = jnp.concatenate([low_ref[n, part, :] for n in range(count)], axis=0)
                above = jnp.concatenate([high_ref[n, part, :] for n in range(count)], axis=0)
                values += dot(below, one_hot(adj, LAYER))
                values += dot(above, one_hot(adj - (LAYER + total), LAYER))
            values = values.astype(jnp.bfloat16)
            if edge and f < 2:
                rows = partner_ref.shape[1]
                use = jnp.logical_and(step == 0, section == 1 - f)
                crossed = []
                for n in range(count):
                    wanted = partner_ref[n : n + 1, :]
                    arrived = jnp.zeros((width, rows), jnp.float32)
                    for d in range(shards):
                        source = lax.rem(space - d + shards, shards)
                        arrived += dot(pieces[d][n], one_hot(wanted - source * rows, rows))
                    crossed.append(arrived)
                crossed = jnp.concatenate(crossed, axis=0).astype(jnp.bfloat16)
                crossed = jnp.concatenate(
                    [crossed, jnp.zeros((count * width, tile - rows), jnp.bfloat16)], axis=1)
                take = jnp.logical_and(column < rows, use)
                values = jnp.where(take, crossed, values)
            found.append(values)
        return found

    def finish(edge):
        found = gathered(edge)
        frequency = freq_ref[0]
        scale = scale_ref[...]
        inverse_scale = 1.0 / scale
        for n in range(count):
            for d in range(1, peers):
                owner = lax.rem(inst - d + peers, peers)
                for m in range(count):
                    weight = table_ref[inst * count + n, owner * count + m] * frequency
                    at = (n * (peers - 1) + d - 1) * count + m
                    factor_ref[at : at + 1, :] = weight * inverse_scale
        for n in range(count):
            beside = jnp.concatenate([v[n * width : (n + 1) * width] for v in found], axis=0)
            inner = dot(lift_ref[...], beside) + dot(volume_ref[...], tile_ref[n])
            value = forcing_ref[n].astype(jnp.float32) - scale * inner
            for m in range(count):
                weight = table_ref[inst * count + n, inst * count + m] * frequency
                value -= weight * tile_ref[m].astype(jnp.float32)
            update = dot(inverse_ref[...], value.astype(jnp.bfloat16))
            out_ref[n] = tile_ref[n].astype(jnp.float32) + update * inverse_scale

    @pl.when(at_edge)
    def _():
        finish(True)

    @pl.when(jnp.logical_not(at_edge))
    def _():
        finish(False)


def update_kernel(tile, ready_ref, factor_ref, inverse_ref, *rest):
    others, (out_ref, made, moved, sems) = rest[:-4], rest[-4:]
    count, dof, total = ready_ref.shape
    products = len(others) * count
    copies = []
    for t in range(total // tile):
        cols = slice(t * tile, (t + 1) * tile)
        for k in range(products):
            moved[t % 2, k] = dot(inverse_ref[...], others[k // count][k % count, :, cols])
        factors = [[factor_ref[n * products + k : n * products + k + 1, cols] for k in range(products)]
                   for n in range(count)]
        for strip in range(0, dof, STRIP):
            rows = slice(strip, strip + STRIP)
            parts = [moved[t % 2, k, rows, :] for k in range(products)]
            for n in range(count):
                value = ready_ref[n, rows, cols]
                for factor, part in zip(factors[n], parts):
                    value -= factor * part
                made[t, n, rows, :] = value.astype(jnp.bfloat16)
        copy = pltpu.make_async_copy(made.at[t], out_ref.at[:, :, cols], sems.at[t])
        copy.start()
        copies.append(copy)
    for copy in copies:
        copy.wait()


def whole(array):
    return pl.BlockSpec(array.shape, lambda j: (0,) * array.ndim)


def body(solution, forcing, metric_scale, frequency, adjacency, partner, volume_matrix, trace_matrix, lift_matrix,
         block_inverse):
    current = solution[0]
    forcing_local = forcing[0]
    neighbours = adjacency[0]
    partner_rows = partner[0]
    count, dof, total = current.shape
    width = trace_matrix.shape[0] // 6
    iface_rows = partner_rows.shape[1]
    shards = lax.axis_size("space")
    peers = lax.axis_size("inst")
    section = lax.axis_index("row")
    place = jnp.stack([section, lax.axis_index("inst"), lax.axis_index("space")]).astype(jnp.int32)
    table = jnp.asarray(spectral_table(count * peers))
    smem = pl.BlockSpec(memory_space=pltpu.SMEM)
    bf16 = jnp.bfloat16

    with jax.named_scope("instances"):
        others = [lax.ppermute(current, "inst", [(i, (i + d) % peers) for i in range(peers)])
                  for d in range(1, peers)]

    with jax.named_scope("ends"):
        up, down, cross = pl.pallas_call(
            ends_kernel,
            grid=(1,),
            out_shape=(jax.ShapeDtypeStruct((count, 2 * width, LAYER), bf16),
                       jax.ShapeDtypeStruct((count, 2 * width, LAYER), bf16),
                       jax.ShapeDtypeStruct((count, width, iface_rows), bf16)),
            in_specs=[smem,
                      pl.BlockSpec((count, dof, LANES), lambda j: (0, 0, 0)),
                      pl.BlockSpec((count, dof, LANES), lambda j: (0, 0, total // LANES - 1)),
                      whole(trace_matrix)],
            out_specs=(pl.BlockSpec((count, 2 * width, LAYER), lambda j: (0, 0, 0)),
                       pl.BlockSpec((count, 2 * width, LAYER), lambda j: (0, 0, 0)),
                       pl.BlockSpec((count, width, iface_rows), lambda j: (0, 0, 0))),
            compiler_params=pltpu.CompilerParams(vmem_limit_bytes=VMEM_LIMIT),
            cost_estimate=pl.CostEstimate(flops=8 * width * dof * LANES * 2 * count,
                                          bytes_accessed=1_000_000, transcendentals=0),
            name="ends",
        )(place, current, current, trace_matrix)

    with jax.named_scope("halo"):
        low = lax.ppermute(up, "space", [(i, (i + 1) % shards) for i in range(shards)])
        high = lax.ppermute(down, "space", [(i, (i - 1) % shards) for i in range(shards)])
    with jax.named_scope("interface"):
        pieces = [lax.ppermute(cross, ("space", "row"),
                               [(i * 2 + r, (i + d) % shards * 2 + 1 - r) for i in range(shards) for r in range(2)])
                  for d in range(shards)]

    tile = 256
    steps = total // tile
    by_tile = lambda *lead: pl.BlockSpec(lead + (tile,), lambda j: (0,) * len(lead) + (j,))
    with jax.named_scope("couple"):
        ready, factors = pl.pallas_call(
            functools.partial(couple_kernel, shards, peers),
            grid=(steps,),
            out_shape=(jax.ShapeDtypeStruct((count, dof, total), jnp.float32),
                       jax.ShapeDtypeStruct((count * count * (peers - 1), total), jnp.float32)),
            in_specs=[smem, smem, smem, by_tile(6), whole(partner_rows), whole(current), by_tile(count, dof),
                      by_tile(count, dof), by_tile(1), whole(trace_matrix), whole(lift_matrix),
                      whole(volume_matrix), whole(block_inverse), whole(low), whole(high)] + [whole(p) for p in pieces],
            out_specs=(by_tile(count, dof), by_tile(count * count * (peers - 1))),
            scratch_shapes=[pltpu.VMEM((6, count * width, total), bf16)],
            compiler_params=pltpu.CompilerParams(vmem_limit_bytes=VMEM_LIMIT),
            cost_estimate=pl.CostEstimate(
                flops=2 * count * total * (6 * width * dof * 2 + dof * dof + 6 * width * total),
                bytes_accessed=count * dof * total * 10, transcendentals=0),
            name="couple",
        )(place, frequency, table, neighbours, partner_rows, current, current, forcing_local, metric_scale,
          trace_matrix, lift_matrix, volume_matrix, block_inverse, low, high, *pieces)

    vmem = pl.BlockSpec(memory_space=pltpu.VMEM)
    with jax.named_scope("update"):
        result = pl.pallas_call(
            functools.partial(update_kernel, tile),
            out_shape=jax.ShapeDtypeStruct((count, dof, total), bf16),
            in_specs=[vmem] * (2 + peers),
            out_specs=pl.BlockSpec(memory_space=pl.ANY),
            scratch_shapes=[pltpu.VMEM((steps, count, dof, tile), bf16),
                            pltpu.VMEM((2, (peers - 1) * count, dof, tile), jnp.float32),
                            pltpu.SemaphoreType.DMA((steps,))],
            compiler_params=pltpu.CompilerParams(vmem_limit_bytes=VMEM_LIMIT),
            cost_estimate=pl.CostEstimate(flops=2 * count * total * dof * dof * (peers - 1),
                                          bytes_accessed=count * dof * total * 8, transcendentals=0),
            name="update",
        )(ready, factors, block_inverse, *others)
    return result[None]


def solution(mesh):
    in_specs = (
        P("row", "inst", None, ("groups", "space")),
        P("row", "inst", None, ("groups", "space")),
        P("row", ("groups", "space")),
        P(),
        P("row", None, ("groups", "space")),
        P("row", "inst", ("groups", "space")),
        P(),
        P(),
        P(),
        P(),
    )
    out_specs = P("row", "inst", None, ("groups", "space"))
    return jax.shard_map(body, mesh=mesh, in_specs=in_specs, out_specs=out_specs, check_vma=False)
```

```python
import functools

import jax
import jax.numpy as jnp
import numpy as np
from jax import lax
from jax.experimental import pallas as pl
from jax.experimental.pallas import tpu as pltpu
from jax.sharding import PartitionSpec as P

LAYER = 64
OPPOSITE = (1, 0, 3, 2, 5, 4)
LANES = 128
VMEM_LIMIT = 40 * 1024 * 1024


def spectral_table(instances):
    positions = np.arange(instances)
    distance = positions[:, None] - positions[None, :]
    parity = np.where(distance % 2 == 0, 1.0, -1.0)
    angles = np.pi * distance / instances
    sines = np.where(distance == 0, 1.0, np.sin(angles))
    cotangent = np.where(distance == 0, 0.0, np.cos(angles) / sines)
    return (0.5 * parity * cotangent).astype(np.float32)


def one_hot(picked, rows):
    numbers = lax.broadcasted_iota(jnp.int32, (rows, picked.shape[1]), 0)
    return jnp.where(numbers == picked, 1.0, 0.0).astype(jnp.bfloat16)


def dot(left, right):
    return jnp.dot(left, right, preferred_element_type=jnp.float32)


def ends_kernel(place_ref, first_ref, last_ref, trace_ref, up_ref, down_ref, cross_ref):
    width = trace_ref.shape[0] // 6
    section = place_ref[0]
    for n in range(first_ref.shape[0]):
        first = dot(trace_ref[...], first_ref[n]).astype(jnp.bfloat16)
        last = dot(trace_ref[4 * width :, :], last_ref[n]).astype(jnp.bfloat16)
        down_ref[n] = first[4 * width :, :LAYER]
        up_ref[n] = last[:, last.shape[1] - LAYER :]
        rows = cross_ref.shape[2]
        cross_ref[n] = jnp.where(section == 0, first[width : 2 * width, :rows], first[:width, :rows])


def couple_kernel(shards, peers, place_ref, freq_ref, table_ref, adj_ref, partner_ref, all_ref, tile_ref, forcing_ref,
                  scale_ref, trace_ref, lift_ref, volume_ref, inverse_ref, low_ref, high_ref, *rest):
    pieces, (out_ref, factor_ref, traces) = rest[:shards], rest[shards:]
    step = pl.program_id(0)
    steps = pl.num_programs(0)
    count, dof, total = all_ref.shape
    width = trace_ref.shape[0] // 6
    tile = tile_ref.shape[2]
    section, inst, space = place_ref[0], place_ref[1], place_ref[2]

    @pl.when(step == 0)
    def _():
        for n in range(count):
            for c in range(total // tile):
                cols = slice(c * tile, (c + 1) * tile)
                made = dot(trace_ref[...], all_ref[n, :, cols]).astype(jnp.bfloat16)
                for f in range(6):
                    traces[f, n * width : (n + 1) * width, cols] = made[f * width : (f + 1) * width]

    column = lax.broadcasted_iota(jnp.int32, (1, tile), 1)
    at_edge = jnp.logical_or(step == 0, step == steps - 1)

    def gathered(edge):
        found = []
        for f in range(6):
            adj = adj_ref[f : f + 1, :]
            values = dot(traces[OPPOSITE[f]], one_hot(adj - LAYER, total))
            if edge and f >= 4:
                part = slice((5 - f) * width, (6 - f) * width)
                below = jnp.concatenate([low_ref[n, part, :] for n in range(count)], axis=0)
                above = jnp.concatenate([high_ref[n, part, :] for n in range(count)], axis=0)
                values += dot(below, one_hot(adj, LAYER))
                values += dot(above, one_hot(adj - (LAYER + total), LAYER))
            values = values.astype(jnp.bfloat16)
            if edge and f < 2:
                rows = partner_ref.shape[1]
                use = jnp.logical_and(step == 0, section == 1 - f)
                crossed = []
                for n in range(count):
                    wanted = partner_ref[n : n + 1, :]
                    arrived = jnp.zeros((width, rows), jnp.float32)
                    for d in range(shards):
                        source = lax.rem(space - d + shards, shards)
                        arrived += dot(pieces[d][n], one_hot(wanted - source * rows, rows))
                    crossed.append(arrived)
                crossed = jnp.concatenate(crossed, axis=0).astype(jnp.bfloat16)
                crossed = jnp.concatenate(
                    [crossed, jnp.zeros((count * width, tile - rows), jnp.bfloat16)], axis=1)
                take = jnp.logical_and(column < rows, use)
                values = jnp.where(take, crossed, values)
            found.append(values)
        return found

    def finish(edge):
        found = gathered(edge)
        frequency = freq_ref[0]
        scale = scale_ref[...]
        inverse_scale = 1.0 / scale
        for n in range(count):
            for d in range(1, peers):
                owner = lax.rem(inst - d + peers, peers)
                for m in range(count):
                    weight = table_ref[inst * count + n, owner * count + m] * frequency
                    at = (n * (peers - 1) + d - 1) * count + m
                    factor_ref[at : at + 1, :] = weight * inverse_scale
        for n in range(count):
            beside = jnp.concatenate([v[n * width : (n + 1) * width] for v in found], axis=0)
            inner = dot(lift_ref[...], beside) + dot(volume_ref[...], tile_ref[n])
            value = forcing_ref[n].astype(jnp.float32) - scale * inner
            for m in range(count):
                weight = table_ref[inst * count + n, inst * count + m] * frequency
                value -= weight * tile_ref[m].astype(jnp.float32)
            update = dot(inverse_ref[...], value.astype(jnp.bfloat16))
            out_ref[n] = tile_ref[n].astype(jnp.float32) + update * inverse_scale

    @pl.when(at_edge)
    def _():
        finish(True)

    @pl.when(jnp.logical_not(at_edge))
    def _():
        finish(False)


def update_kernel(tile, blocks, ready_ref, factor_ref, inverse_ref, *rest):
    others, (out_ref, made, sems) = rest[:-3], rest[-3:]
    count, dof, total = ready_ref.shape
    copies = []
    for b in range(blocks):
        rows = slice(b * dof // blocks, (b + 1) * dof // blocks)
        for t in range(total // tile):
            cols = slice(t * tile, (t + 1) * tile)
            moved = [dot(inverse_ref[rows, :], other[m, :, cols]) for other in others for m in range(count)]
            for n in range(count):
                value = ready_ref[n, rows, cols]
                for k, part in enumerate(moved):
                    at = n * len(moved) + k
                    value -= factor_ref[at : at + 1, cols] * part
                made[n, rows, cols] = value.astype(jnp.bfloat16)
        for n in range(count):
            copy = pltpu.make_async_copy(made.at[n, rows, :], out_ref.at[n, rows, :], sems.at[b, n])
            copy.start()
            copies.append(copy)
    for copy in copies:
        copy.wait()


def whole(array):
    return pl.BlockSpec(array.shape, lambda j: (0,) * array.ndim)


def body(solution, forcing, metric_scale, frequency, adjacency, partner, volume_matrix, trace_matrix, lift_matrix,
         block_inverse):
    current = solution[0]
    forcing_local = forcing[0]
    neighbours = adjacency[0]
    partner_rows = partner[0]
    count, dof, total = current.shape
    width = trace_matrix.shape[0] // 6
    iface_rows = partner_rows.shape[1]
    shards = lax.axis_size("space")
    peers = lax.axis_size("inst")
    section = lax.axis_index("row")
    place = jnp.stack([section, lax.axis_index("inst"), lax.axis_index("space")]).astype(jnp.int32)
    table = jnp.asarray(spectral_table(count * peers))
    smem = pl.BlockSpec(memory_space=pltpu.SMEM)
    bf16 = jnp.bfloat16

    with jax.named_scope("instances"):
        others = [lax.ppermute(current, "inst", [(i, (i + d) % peers) for i in range(peers)])
                  for d in range(1, peers)]

    with jax.named_scope("ends"):
        up, down, cross = pl.pallas_call(
            ends_kernel,
            grid=(1,),
            out_shape=(jax.ShapeDtypeStruct((count, 2 * width, LAYER), bf16),
                       jax.ShapeDtypeStruct((count, 2 * width, LAYER), bf16),
                       jax.ShapeDtypeStruct((count, width, iface_rows), bf16)),
            in_specs=[smem,
                      pl.BlockSpec((count, dof, LANES), lambda j: (0, 0, 0)),
                      pl.BlockSpec((count, dof, LANES), lambda j: (0, 0, total // LANES - 1)),
                      whole(trace_matrix)],
            out_specs=(pl.BlockSpec((count, 2 * width, LAYER), lambda j: (0, 0, 0)),
                       pl.BlockSpec((count, 2 * width, LAYER), lambda j: (0, 0, 0)),
                       pl.BlockSpec((count, width, iface_rows), lambda j: (0, 0, 0))),
            compiler_params=pltpu.CompilerParams(vmem_limit_bytes=VMEM_LIMIT),
            cost_estimate=pl.CostEstimate(flops=8 * width * dof * LANES * 2 * count,
                                          bytes_accessed=1_000_000, transcendentals=0),
            name="ends",
        )(place, current, current, trace_matrix)

    with jax.named_scope("halo"):
        low = lax.ppermute(up, "space", [(i, (i + 1) % shards) for i in range(shards)])
        high = lax.ppermute(down, "space", [(i, (i - 1) % shards) for i in range(shards)])
    with jax.named_scope("interface"):
        pieces = [lax.ppermute(cross, ("space", "row"),
                               [(i * 2 + r, (i + d) % shards * 2 + 1 - r) for i in range(shards) for r in range(2)])
                  for d in range(shards)]

    tile = 256
    steps = total // tile
    by_tile = lambda *lead: pl.BlockSpec(lead + (tile,), lambda j: (0,) * len(lead) + (j,))
    with jax.named_scope("couple"):
        ready, factors = pl.pallas_call(
            functools.partial(couple_kernel, shards, peers),
            grid=(steps,),
            out_shape=(jax.ShapeDtypeStruct((count, dof, total), jnp.float32),
                       jax.ShapeDtypeStruct((count * count * (peers - 1), total), jnp.float32)),
            in_specs=[smem, smem, smem, by_tile(6), whole(partner_rows), whole(current), by_tile(count, dof),
                      by_tile(count, dof), by_tile(1), whole(trace_matrix), whole(lift_matrix),
                      whole(volume_matrix), whole(block_inverse), whole(low), whole(high)] + [whole(p) for p in pieces],
            out_specs=(by_tile(count, dof), by_tile(count * count * (peers - 1))),
            scratch_shapes=[pltpu.VMEM((6, count * width, total), bf16)],
            compiler_params=pltpu.CompilerParams(vmem_limit_bytes=VMEM_LIMIT),
            cost_estimate=pl.CostEstimate(
                flops=2 * count * total * (6 * width * dof * 2 + dof * dof + 6 * width * total),
                bytes_accessed=count * dof * total * 10, transcendentals=0),
            name="couple",
        )(place, frequency, table, neighbours, partner_rows, current, current, forcing_local, metric_scale,
          trace_matrix, lift_matrix, volume_matrix, block_inverse, low, high, *pieces)

    vmem = pl.BlockSpec(memory_space=pltpu.VMEM)
    blocks = 2
    with jax.named_scope("update"):
        result = pl.pallas_call(
            functools.partial(update_kernel, tile, blocks),
            out_shape=jax.ShapeDtypeStruct((count, dof, total), bf16),
            in_specs=[vmem] * (2 + peers),
            out_specs=pl.BlockSpec(memory_space=pl.ANY),
            scratch_shapes=[pltpu.VMEM((count, dof, total), bf16), pltpu.SemaphoreType.DMA((blocks, count))],
            compiler_params=pltpu.CompilerParams(vmem_limit_bytes=VMEM_LIMIT),
            cost_estimate=pl.CostEstimate(flops=2 * count * total * dof * dof * (peers - 1),
                                          bytes_accessed=count * dof * total * 8, transcendentals=0),
            name="update",
        )(ready, factors, block_inverse, *others)
    return result[None]


def solution(mesh):
    in_specs = (
        P("row", "inst", None, ("groups", "space")),
        P("row", "inst", None, ("groups", "space")),
        P("row", ("groups", "space")),
        P(),
        P("row", None, ("groups", "space")),
        P("row", "inst", ("groups", "space")),
        P(),
        P(),
        P(),
        P(),
    )
    out_specs = P("row", "inst", None, ("groups", "space"))
    return jax.shard_map(body, mesh=mesh, in_specs=in_specs, out_specs=out_specs, check_vma=False)
```

```python
import functools

import jax
import jax.numpy as jnp
import numpy as np
from jax import lax
from jax.experimental import pallas as pl
from jax.experimental.pallas import tpu as pltpu
from jax.sharding import PartitionSpec as P

LAYER = 64
OPPOSITE = (1, 0, 3, 2, 5, 4)
LANES = 128
VMEM_LIMIT = 40 * 1024 * 1024


def spectral_table(instances):
    positions = np.arange(instances)
    distance = positions[:, None] - positions[None, :]
    parity = np.where(distance % 2 == 0, 1.0, -1.0)
    angles = np.pi * distance / instances
    sines = np.where(distance == 0, 1.0, np.sin(angles))
    cotangent = np.where(distance == 0, 0.0, np.cos(angles) / sines)
    return (0.5 * parity * cotangent).astype(np.float32)


def one_hot(picked, rows):
    numbers = lax.broadcasted_iota(jnp.int32, (rows, picked.shape[1]), 0)
    return jnp.where(numbers == picked, 1.0, 0.0).astype(jnp.bfloat16)


def dot(left, right):
    return jnp.dot(left, right, preferred_element_type=jnp.float32)


def ends_kernel(place_ref, first_ref, last_ref, trace_ref, up_ref, down_ref, cross_ref):
    width = trace_ref.shape[0] // 6
    section = place_ref[0]
    for n in range(first_ref.shape[0]):
        first = dot(trace_ref[...], first_ref[n]).astype(jnp.bfloat16)
        last = dot(trace_ref[4 * width :, :], last_ref[n]).astype(jnp.bfloat16)
        down_ref[n] = first[4 * width :, :LAYER]
        up_ref[n] = last[:, last.shape[1] - LAYER :]
        rows = cross_ref.shape[2]
        cross_ref[n] = jnp.where(section == 0, first[width : 2 * width, :rows], first[:width, :rows])


def couple_kernel(shards, peers, place_ref, freq_ref, table_ref, adj_ref, partner_ref, all_ref, tile_ref, forcing_ref,
                  scale_ref, trace_ref, lift_ref, volume_ref, inverse_ref, low_ref, high_ref, *rest):
    pieces, (out_ref, factor_ref, traces) = rest[:shards], rest[shards:]
    step = pl.program_id(0)
    steps = pl.num_programs(0)
    count, dof, total = all_ref.shape
    width = trace_ref.shape[0] // 6
    tile = tile_ref.shape[2]
    section, inst, space = place_ref[0], place_ref[1], place_ref[2]

    @pl.when(step == 0)
    def _():
        for n in range(count):
            for c in range(total // tile):
                cols = slice(c * tile, (c + 1) * tile)
                made = dot(trace_ref[...], all_ref[n, :, cols]).astype(jnp.bfloat16)
                for f in range(6):
                    traces[f, n * width : (n + 1) * width, cols] = made[f * width : (f + 1) * width]

    column = lax.broadcasted_iota(jnp.int32, (1, tile), 1)
    at_edge = jnp.logical_or(step == 0, step == steps - 1)

    def gathered(edge):
        found = []
        for f in range(6):
            adj = adj_ref[f : f + 1, :]
            values = dot(traces[OPPOSITE[f]], one_hot(adj - LAYER, total))
            if edge and f >= 4:
                part = slice((5 - f) * width, (6 - f) * width)
                below = jnp.concatenate([low_ref[n, part, :] for n in range(count)], axis=0)
                above = jnp.concatenate([high_ref[n, part, :] for n in range(count)], axis=0)
                values += dot(below, one_hot(adj, LAYER))
                values += dot(above, one_hot(adj - (LAYER + total), LAYER))
            values = values.astype(jnp.bfloat16)
            if edge and f < 2:
                rows = partner_ref.shape[1]
                use = jnp.logical_and(step == 0, section == 1 - f)
                crossed = []
                for n in range(count):
                    wanted = partner_ref[n : n + 1, :]
                    arrived = jnp.zeros((width, rows), jnp.float32)
                    for d in range(shards):
                        source = lax.rem(space - d + shards, shards)
                        arrived += dot(pieces[d][n], one_hot(wanted - source * rows, rows))
                    crossed.append(arrived)
                crossed = jnp.concatenate(crossed, axis=0).astype(jnp.bfloat16)
                crossed = jnp.concatenate(
                    [crossed, jnp.zeros((count * width, tile - rows), jnp.bfloat16)], axis=1)
                take = jnp.logical_and(column < rows, use)
                values = jnp.where(take, crossed, values)
            found.append(values)
        return found

    def finish(edge):
        found = gathered(edge)
        frequency = freq_ref[0]
        scale = scale_ref[...]
        inverse_scale = 1.0 / scale
        for n in range(count):
            for d in range(1, peers):
                owner = lax.rem(inst - d + peers, peers)
                for m in range(count):
                    weight = table_ref[inst * count + n, owner * count + m] * frequency
                    at = (n * (peers - 1) + d - 1) * count + m
                    factor_ref[at : at + 1, :] = weight * inverse_scale
        for n in range(count):
            beside = jnp.concatenate([v[n * width : (n + 1) * width] for v in found], axis=0)
            inner = dot(lift_ref[...], beside) + dot(volume_ref[...], tile_ref[n])
            value = forcing_ref[n].astype(jnp.float32) - scale * inner
            for m in range(count):
                weight = table_ref[inst * count + n, inst * count + m] * frequency
                value -= weight * tile_ref[m].astype(jnp.float32)
            update = dot(inverse_ref[...], value.astype(jnp.bfloat16))
            out_ref[n] = tile_ref[n].astype(jnp.float32) + update * inverse_scale

    @pl.when(at_edge)
    def _():
        finish(True)

    @pl.when(jnp.logical_not(at_edge))
    def _():
        finish(False)


def update_kernel(tile, wide, ready_ref, factor_ref, inverse_ref, *rest):
    others, (out_ref, made, sems) = rest[:-3], rest[-3:]
    count, dof, total = ready_ref.shape
    copies = []
    for start in range(0, total, wide):
        moved = [dot(inverse_ref[...], other[m, :, start : start + wide]) for other in others for m in range(count)]
        for t in range(start // tile, min(start + wide, total) // tile):
            cols = slice(t * tile, (t + 1) * tile)
            for n in range(count):
                value = ready_ref[n, :, cols]
                for k, part in enumerate(moved):
                    at = n * len(moved) + k
                    value -= factor_ref[at : at + 1, cols] * part[:, t * tile - start : (t + 1) * tile - start]
                made[t, n] = value.astype(jnp.bfloat16)
            copy = pltpu.make_async_copy(made.at[t], out_ref.at[:, :, cols], sems.at[t])
            copy.start()
            copies.append(copy)
    for copy in copies:
        copy.wait()


def whole(array):
    return pl.BlockSpec(array.shape, lambda j: (0,) * array.ndim)


def body(solution, forcing, metric_scale, frequency, adjacency, partner, volume_matrix, trace_matrix, lift_matrix,
         block_inverse):
    current = solution[0]
    forcing_local = forcing[0]
    neighbours = adjacency[0]
    partner_rows = partner[0]
    count, dof, total = current.shape
    width = trace_matrix.shape[0] // 6
    iface_rows = partner_rows.shape[1]
    shards = lax.axis_size("space")
    peers = lax.axis_size("inst")
    section = lax.axis_index("row")
    place = jnp.stack([section, lax.axis_index("inst"), lax.axis_index("space")]).astype(jnp.int32)
    table = jnp.asarray(spectral_table(count * peers))
    smem = pl.BlockSpec(memory_space=pltpu.SMEM)
    bf16 = jnp.bfloat16

    with jax.named_scope("instances"):
        others = [lax.ppermute(current, "inst", [(i, (i + d) % peers) for i in range(peers)])
                  for d in range(1, peers)]

    with jax.named_scope("ends"):
        up, down, cross = pl.pallas_call(
            ends_kernel,
            grid=(1,),
            out_shape=(jax.ShapeDtypeStruct((count, 2 * width, LAYER), bf16),
                       jax.ShapeDtypeStruct((count, 2 * width, LAYER), bf16),
                       jax.ShapeDtypeStruct((count, width, iface_rows), bf16)),
            in_specs=[smem,
                      pl.BlockSpec((count, dof, LANES), lambda j: (0, 0, 0)),
                      pl.BlockSpec((count, dof, LANES), lambda j: (0, 0, total // LANES - 1)),
                      whole(trace_matrix)],
            out_specs=(pl.BlockSpec((count, 2 * width, LAYER), lambda j: (0, 0, 0)),
                       pl.BlockSpec((count, 2 * width, LAYER), lambda j: (0, 0, 0)),
                       pl.BlockSpec((count, width, iface_rows), lambda j: (0, 0, 0))),
            compiler_params=pltpu.CompilerParams(vmem_limit_bytes=VMEM_LIMIT),
            cost_estimate=pl.CostEstimate(flops=8 * width * dof * LANES * 2 * count,
                                          bytes_accessed=1_000_000, transcendentals=0),
            name="ends",
        )(place, current, current, trace_matrix)

    with jax.named_scope("halo"):
        low = lax.ppermute(up, "space", [(i, (i + 1) % shards) for i in range(shards)])
        high = lax.ppermute(down, "space", [(i, (i - 1) % shards) for i in range(shards)])
    with jax.named_scope("interface"):
        pieces = [lax.ppermute(cross, ("space", "row"),
                               [(i * 2 + r, (i + d) % shards * 2 + 1 - r) for i in range(shards) for r in range(2)])
                  for d in range(shards)]

    tile = 256
    steps = total // tile
    by_tile = lambda *lead: pl.BlockSpec(lead + (tile,), lambda j: (0,) * len(lead) + (j,))
    with jax.named_scope("couple"):
        ready, factors = pl.pallas_call(
            functools.partial(couple_kernel, shards, peers),
            grid=(steps,),
            out_shape=(jax.ShapeDtypeStruct((count, dof, total), jnp.float32),
                       jax.ShapeDtypeStruct((count * count * (peers - 1), total), jnp.float32)),
            in_specs=[smem, smem, smem, by_tile(6), whole(partner_rows), whole(current), by_tile(count, dof),
                      by_tile(count, dof), by_tile(1), whole(trace_matrix), whole(lift_matrix),
                      whole(volume_matrix), whole(block_inverse), whole(low), whole(high)] + [whole(p) for p in pieces],
            out_specs=(by_tile(count, dof), by_tile(count * count * (peers - 1))),
            scratch_shapes=[pltpu.VMEM((6, count * width, total), bf16)],
            compiler_params=pltpu.CompilerParams(vmem_limit_bytes=VMEM_LIMIT),
            cost_estimate=pl.CostEstimate(
                flops=2 * count * total * (6 * width * dof * 2 + dof * dof + 6 * width * total),
                bytes_accessed=count * dof * total * 10, transcendentals=0),
            name="couple",
        )(place, frequency, table, neighbours, partner_rows, current, current, forcing_local, metric_scale,
          trace_matrix, lift_matrix, volume_matrix, block_inverse, low, high, *pieces)

    vmem = pl.BlockSpec(memory_space=pltpu.VMEM)
    with jax.named_scope("update"):
        result = pl.pallas_call(
            functools.partial(update_kernel, tile, 2 * tile),
            out_shape=jax.ShapeDtypeStruct((count, dof, total), bf16),
            in_specs=[vmem] * (2 + peers),
            out_specs=pl.BlockSpec(memory_space=pl.ANY),
            scratch_shapes=[pltpu.VMEM((steps, count, dof, tile), bf16), pltpu.SemaphoreType.DMA((steps,))],
            compiler_params=pltpu.CompilerParams(vmem_limit_bytes=VMEM_LIMIT),
            cost_estimate=pl.CostEstimate(flops=2 * count * total * dof * dof * (peers - 1),
                                          bytes_accessed=count * dof * total * 8, transcendentals=0),
            name="update",
        )(ready, factors, block_inverse, *others)
    return result[None]


def solution(mesh):
    in_specs = (
        P("row", "inst", None, ("groups", "space")),
        P("row", "inst", None, ("groups", "space")),
        P("row", ("groups", "space")),
        P(),
        P("row", None, ("groups", "space")),
        P("row", "inst", ("groups", "space")),
        P(),
        P(),
        P(),
        P(),
    )
    out_specs = P("row", "inst", None, ("groups", "space"))
    return jax.shard_map(body, mesh=mesh, in_specs=in_specs, out_specs=out_specs, check_vma=False)
```

```python
import functools

import jax
import jax.numpy as jnp
import numpy as np
from jax import lax
from jax.experimental import pallas as pl
from jax.experimental.pallas import tpu as pltpu
from jax.sharding import PartitionSpec as P

LAYER = 64
OPPOSITE = (1, 0, 3, 2, 5, 4)
LANES = 128
VMEM_LIMIT = 40 * 1024 * 1024
CUT_LIMIT = 56 * 1024 * 1024
COUPLE_FLOPS = 7_500_000_000


def spectral_table(instances):
    positions = np.arange(instances)
    distance = positions[:, None] - positions[None, :]
    parity = np.where(distance % 2 == 0, 1.0, -1.0)
    angles = np.pi * distance / instances
    sines = np.where(distance == 0, 1.0, np.sin(angles))
    cotangent = np.where(distance == 0, 0.0, np.cos(angles) / sines)
    return (0.5 * parity * cotangent).astype(np.float32)


def one_hot(picked, rows):
    numbers = lax.broadcasted_iota(jnp.int32, (rows, picked.shape[1]), 0)
    return jnp.where(numbers == picked, 1.0, 0.0).astype(jnp.bfloat16)


def dot(left, right):
    return jnp.dot(left, right, preferred_element_type=jnp.float32)


def cut_kernel(bounds, head_ref, all_ref, *rest):
    out_refs, sems = rest[:-1], rest[-1]
    copies = []
    for k, (first, last) in enumerate(bounds):
        copies.append(pltpu.make_async_copy(all_ref.at[:, :, first:last], out_refs[k], sems.at[k]))
        copies[k].start()
    for copy in copies:
        copy.wait()


def ends_kernel(place_ref, first_ref, last_ref, trace_ref, up_ref, down_ref, cross_ref):
    width = trace_ref.shape[0] // 6
    section = place_ref[0]
    for n in range(first_ref.shape[0]):
        first = dot(trace_ref[...], first_ref[n]).astype(jnp.bfloat16)
        last = dot(trace_ref[4 * width :, :], last_ref[n]).astype(jnp.bfloat16)
        down_ref[n] = first[4 * width :, :LAYER]
        up_ref[n] = last[:, last.shape[1] - LAYER :]
        rows = cross_ref.shape[2]
        cross_ref[n] = jnp.where(section == 0, first[width : 2 * width, :rows], first[:width, :rows])


def couple_kernel(shards, peers, place_ref, freq_ref, table_ref, adj_ref, partner_ref, all_ref, tile_ref, forcing_ref,
                  scale_ref, trace_ref, lift_ref, volume_ref, inverse_ref, low_ref, high_ref, *rest):
    pieces, heads, (out_ref, factor_ref, traces) = rest[:shards], rest[shards:-3], rest[-3:]
    step = pl.program_id(0)
    steps = pl.num_programs(0)
    count, dof, total = all_ref.shape
    width = trace_ref.shape[0] // 6
    tile = tile_ref.shape[2]
    section, inst, space = place_ref[0], place_ref[1], place_ref[2]

    @pl.when(step == 0)
    def _():
        for n in range(count):
            for c in range(total // tile):
                cols = slice(c * tile, (c + 1) * tile)
                made = dot(trace_ref[...], all_ref[n, :, cols]).astype(jnp.bfloat16)
                for f in range(6):
                    traces[f, n * width : (n + 1) * width, cols] = made[f * width : (f + 1) * width]

    column = lax.broadcasted_iota(jnp.int32, (1, tile), 1)
    at_edge = jnp.logical_or(step == 0, step == steps - 1)

    def gathered(edge):
        found = []
        for f in range(6):
            adj = adj_ref[f : f + 1, :]
            values = dot(traces[OPPOSITE[f]], one_hot(adj - LAYER, total))
            if edge and f >= 4:
                part = slice((5 - f) * width, (6 - f) * width)
                below = jnp.concatenate([low_ref[n, part, :] for n in range(count)], axis=0)
                above = jnp.concatenate([high_ref[n, part, :] for n in range(count)], axis=0)
                values += dot(below, one_hot(adj, LAYER))
                values += dot(above, one_hot(adj - (LAYER + total), LAYER))
            values = values.astype(jnp.bfloat16)
            if edge and f < 2:
                rows = partner_ref.shape[1]
                use = jnp.logical_and(step == 0, section == 1 - f)
                crossed = []
                for n in range(count):
                    wanted = partner_ref[n : n + 1, :]
                    arrived = jnp.zeros((width, rows), jnp.float32)
                    for d in range(shards):
                        source = lax.rem(space - d + shards, shards)
                        arrived += dot(pieces[d][n], one_hot(wanted - source * rows, rows))
                    crossed.append(arrived)
                crossed = jnp.concatenate(crossed, axis=0).astype(jnp.bfloat16)
                crossed = jnp.concatenate(
                    [crossed, jnp.zeros((count * width, tile - rows), jnp.bfloat16)], axis=1)
                take = jnp.logical_and(column < rows, use)
                values = jnp.where(take, crossed, values)
            found.append(values)
        return found

    def finish(edge):
        found = gathered(edge)
        frequency = freq_ref[0]
        scale = scale_ref[...]
        inverse_scale = 1.0 / scale
        for n in range(count):
            for d in range(1, peers):
                owner = lax.rem(inst - d + peers, peers)
                for m in range(count):
                    weight = table_ref[inst * count + n, owner * count + m] * frequency
                    at = (n * (peers - 1) + d - 1) * count + m
                    factor_ref[at : at + 1, :] = weight * inverse_scale
        for n in range(count):
            beside = jnp.concatenate([v[n * width : (n + 1) * width] for v in found], axis=0)
            inner = dot(lift_ref[...], beside) + dot(volume_ref[...], tile_ref[n])
            value = forcing_ref[n].astype(jnp.float32) - scale * inner
            for m in range(count):
                weight = table_ref[inst * count + n, inst * count + m] * frequency
                value -= weight * tile_ref[m].astype(jnp.float32)
            update = dot(inverse_ref[...], value.astype(jnp.bfloat16))
            out_ref[n] = tile_ref[n].astype(jnp.float32) + update * inverse_scale

        @pl.when(step == 0)
        def _():
            moved = [dot(inverse_ref[...], head[m]) for head in heads for m in range(count)]
            for n in range(count):
                for k, part in enumerate(moved):
                    row = n * len(moved) + k
                    out_ref[n, :, :LANES] -= factor_ref[row : row + 1, :LANES] * part

    @pl.when(at_edge)
    def _():
        finish(True)

    @pl.when(jnp.logical_not(at_edge))
    def _():
        finish(False)


def update_kernel(base, bounds, peers, tile, ready_ref, factor_ref, inverse_ref, *rest):
    pieces = len(bounds) * (peers - 1)
    arrived, (out_ref, made, sems) = rest[:pieces], rest[-3:]
    count, dof, total = ready_ref.shape
    copies = []

    def send(first, last):
        copy = pltpu.make_async_copy(
            made.at[:, :, first - base : last - base], out_ref.at[:, :, first:last], sems.at[len(copies)])
        copy.start()
        copies.append(copy)

    if base < bounds[0][0]:
        for n in range(count):
            made[n, :, : bounds[0][0] - base] = ready_ref[n, :, base : bounds[0][0]].astype(jnp.bfloat16)
        send(base, bounds[0][0])
    for b, (first, last) in enumerate(bounds):
        others = arrived[b * (peers - 1) : (b + 1) * (peers - 1)]
        for start in range(first, last, tile):
            stop = min(start + tile, last)
            moved = [dot(inverse_ref[...], other[m, :, start - first : stop - first])
                     for other in others for m in range(count)]
            for n in range(count):
                value = ready_ref[n, :, start:stop]
                for k, part in enumerate(moved):
                    row = n * len(moved) + k
                    value -= factor_ref[row : row + 1, start:stop] * part
                made[n, :, start - base : stop - base] = value.astype(jnp.bfloat16)
            send(start, stop)
    for copy in copies:
        copy.wait()


def whole(array):
    return pl.BlockSpec(array.shape, lambda j: (0,) * array.ndim)


def body(solution, forcing, metric_scale, frequency, adjacency, partner, volume_matrix, trace_matrix, lift_matrix,
         block_inverse):
    current = solution[0]
    forcing_local = forcing[0]
    neighbours = adjacency[0]
    partner_rows = partner[0]
    count, dof, total = current.shape
    width = trace_matrix.shape[0] // 6
    iface_rows = partner_rows.shape[1]
    shards = lax.axis_size("space")
    peers = lax.axis_size("inst")
    section = lax.axis_index("row")
    place = jnp.stack([section, lax.axis_index("inst"), lax.axis_index("space")]).astype(jnp.int32)
    table = jnp.asarray(spectral_table(count * peers))
    smem = pl.BlockSpec(memory_space=pltpu.SMEM)
    bf16 = jnp.bfloat16

    with jax.named_scope("instances"):
        tile = 256
        bounds = [(0, LANES), (LANES, total - tile), (total - tile, total)]
        head = current[:, :, :LANES]
        chunks = [head] + list(pl.pallas_call(
            functools.partial(cut_kernel, bounds[1:]),
            out_shape=tuple(jax.ShapeDtypeStruct((count, dof, last - first), bf16) for first, last in bounds[1:]),
            in_specs=[pl.BlockSpec(memory_space=pl.ANY)] * 2,
            out_specs=tuple([pl.BlockSpec(memory_space=pl.ANY)] * (len(bounds) - 1)),
            scratch_shapes=[pltpu.SemaphoreType.DMA((len(bounds) - 1,))],
            compiler_params=pltpu.CompilerParams(vmem_limit_bytes=CUT_LIMIT),
            cost_estimate=pl.CostEstimate(flops=0, bytes_accessed=0, transcendentals=0),
            name="cut",
        )(head, current))
        arriving = [[lax.ppermute(chunk, "inst", [(i, (i + d) % peers) for i in range(peers)])
                     for d in range(1, peers)] for chunk in chunks]

    with jax.named_scope("ends"):
        up, down, cross = pl.pallas_call(
            ends_kernel,
            grid=(1,),
            out_shape=(jax.ShapeDtypeStruct((count, 2 * width, LAYER), bf16),
                       jax.ShapeDtypeStruct((count, 2 * width, LAYER), bf16),
                       jax.ShapeDtypeStruct((count, width, iface_rows), bf16)),
            in_specs=[smem,
                      whole(head),
                      pl.BlockSpec((count, dof, LANES), lambda j: (0, 0, total // LANES - 1)),
                      whole(trace_matrix)],
            out_specs=(pl.BlockSpec((count, 2 * width, LAYER), lambda j: (0, 0, 0)),
                       pl.BlockSpec((count, 2 * width, LAYER), lambda j: (0, 0, 0)),
                       pl.BlockSpec((count, width, iface_rows), lambda j: (0, 0, 0))),
            compiler_params=pltpu.CompilerParams(vmem_limit_bytes=VMEM_LIMIT),
            cost_estimate=pl.CostEstimate(flops=8 * width * dof * LANES * 2 * count,
                                          bytes_accessed=1_000_000, transcendentals=0),
            name="ends",
        )(place, head, current, trace_matrix)

    with jax.named_scope("halo"):
        low = lax.ppermute(up, "space", [(i, (i + 1) % shards) for i in range(shards)])
        high = lax.ppermute(down, "space", [(i, (i - 1) % shards) for i in range(shards)])
    with jax.named_scope("interface"):
        pieces = [lax.ppermute(cross, ("space", "row"),
                               [(i * 2 + r, (i + d) % shards * 2 + 1 - r) for i in range(shards) for r in range(2)])
                  for d in range(shards)]

    steps = total // tile
    by_tile = lambda *lead: pl.BlockSpec(lead + (tile,), lambda j: (0,) * len(lead) + (j,))
    with jax.named_scope("couple"):
        ready, factors = pl.pallas_call(
            functools.partial(couple_kernel, shards, peers),
            grid=(steps,),
            out_shape=(jax.ShapeDtypeStruct((count, dof, total), jnp.float32),
                       jax.ShapeDtypeStruct((count * count * (peers - 1), total), jnp.float32)),
            in_specs=[smem, smem, smem, by_tile(6), whole(partner_rows), whole(current), by_tile(count, dof),
                      by_tile(count, dof), by_tile(1), whole(trace_matrix), whole(lift_matrix),
                      whole(volume_matrix), whole(block_inverse), whole(low), whole(high)] + [whole(p) for p in pieces + arriving[0]],
            out_specs=(by_tile(count, dof), by_tile(count * count * (peers - 1))),
            scratch_shapes=[pltpu.VMEM((6, count * width, total), bf16)],
            compiler_params=pltpu.CompilerParams(vmem_limit_bytes=VMEM_LIMIT),
            cost_estimate=pl.CostEstimate(
                flops=COUPLE_FLOPS,
                bytes_accessed=count * dof * total * 10, transcendentals=0),
            name="couple",
        )(place, frequency, table, neighbours, partner_rows, current, current, forcing_local, metric_scale,
          trace_matrix, lift_matrix, volume_matrix, block_inverse, low, high, *pieces, *arriving[0])

    vmem = pl.BlockSpec(memory_space=pltpu.VMEM)
    with jax.named_scope("update"):
        result = None
        for base, mine, others in ((0, bounds[1:2], arriving[1]), (bounds[2][0], bounds[2:], arriving[2])):
            more = [] if result is None else [result]
            span = mine[-1][1] - base
            result = pl.pallas_call(
                functools.partial(update_kernel, base, mine, peers, tile),
                out_shape=jax.ShapeDtypeStruct((count, dof, total), bf16),
                in_specs=[vmem] * (3 + len(others)) + [pl.BlockSpec(memory_space=pl.ANY)] * len(more),
                out_specs=pl.BlockSpec(memory_space=pl.ANY),
                scratch_shapes=[pltpu.VMEM((count, dof, span), bf16), pltpu.SemaphoreType.DMA((steps,))],
                input_output_aliases={3 + len(others): 0} if more else {},
                compiler_params=pltpu.CompilerParams(vmem_limit_bytes=VMEM_LIMIT),
                cost_estimate=pl.CostEstimate(flops=2 * count * span * dof * dof * (peers - 1),
                                              bytes_accessed=count * dof * span * 8, transcendentals=0),
                name="update",
            )(ready, factors, block_inverse, *others, *more)
    return result[None]


def solution(mesh):
    in_specs = (
        P("row", "inst", None, ("groups", "space")),
        P("row", "inst", None, ("groups", "space")),
        P("row", ("groups", "space")),
        P(),
        P("row", None, ("groups", "space")),
        P("row", "inst", ("groups", "space")),
        P(),
        P(),
        P(),
        P(),
    )
    out_specs = P("row", "inst", None, ("groups", "space"))
    return jax.shard_map(body, mesh=mesh, in_specs=in_specs, out_specs=out_specs, check_vma=False)
```

```python
import functools

import jax
import jax.numpy as jnp
import numpy as np
from jax import lax
from jax.experimental import pallas as pl
from jax.experimental.pallas import tpu as pltpu
from jax.sharding import PartitionSpec as P

LAYER = 64
OPPOSITE = (1, 0, 3, 2, 5, 4)
LANES = 128
VMEM_LIMIT = 40 * 1024 * 1024
ENDS_LIMIT = 63 * 1024 * 1024
UPDATE_LIMIT = 40 * 1024 * 1024


def spectral_table(instances):
    positions = np.arange(instances)
    distance = positions[:, None] - positions[None, :]
    parity = np.where(distance % 2 == 0, 1.0, -1.0)
    angles = np.pi * distance / instances
    sines = np.where(distance == 0, 1.0, np.sin(angles))
    cotangent = np.where(distance == 0, 0.0, np.cos(angles) / sines)
    return (0.5 * parity * cotangent).astype(np.float32)


def one_hot(picked, rows):
    numbers = lax.broadcasted_iota(jnp.int32, (rows, picked.shape[1]), 0)
    return jnp.where(numbers == picked, 1.0, 0.0).astype(jnp.bfloat16)


def dot(left, right):
    return jnp.dot(left, right, preferred_element_type=jnp.float32)


def ends_kernel(place_ref, first_ref, last_ref, trace_ref, up_ref, down_ref, cross_ref):
    width = trace_ref.shape[0] // 6
    section = place_ref[0]
    for n in range(first_ref.shape[0]):
        first = dot(trace_ref[...], first_ref[n]).astype(jnp.bfloat16)
        last = dot(trace_ref[4 * width :, :], last_ref[n]).astype(jnp.bfloat16)
        down_ref[n] = first[4 * width :, :LAYER]
        up_ref[n] = last[:, last.shape[1] - LAYER :]
        rows = cross_ref.shape[2]
        cross_ref[n] = jnp.where(section == 0, first[width : 2 * width, :rows], first[:width, :rows])


def couple_kernel(shards, peers, place_ref, freq_ref, table_ref, adj_ref, partner_ref, all_ref, tile_ref, forcing_ref,
                  scale_ref, trace_ref, lift_ref, volume_ref, inverse_ref, low_ref, high_ref, *rest):
    pieces, (out_ref, factor_ref, traces) = rest[:shards], rest[shards:]
    step = pl.program_id(0)
    steps = pl.num_programs(0)
    count, dof, total = all_ref.shape
    width = trace_ref.shape[0] // 6
    tile = tile_ref.shape[2]
    section, inst, space = place_ref[0], place_ref[1], place_ref[2]

    @pl.when(step == 0)
    def _():
        for n in range(count):
            for c in range(total // tile):
                cols = slice(c * tile, (c + 1) * tile)
                made = dot(trace_ref[...], all_ref[n, :, cols]).astype(jnp.bfloat16)
                for f in range(6):
                    traces[f, n * width : (n + 1) * width, cols] = made[f * width : (f + 1) * width]

    column = lax.broadcasted_iota(jnp.int32, (1, tile), 1)
    at_edge = jnp.logical_or(step == 0, step == steps - 1)

    def gathered(edge):
        found = []
        for f in range(6):
            adj = adj_ref[f : f + 1, :]
            values = dot(traces[OPPOSITE[f]], one_hot(adj - LAYER, total))
            if edge and f >= 4:
                part = slice((5 - f) * width, (6 - f) * width)
                below = jnp.concatenate([low_ref[n, part, :] for n in range(count)], axis=0)
                above = jnp.concatenate([high_ref[n, part, :] for n in range(count)], axis=0)
                values += dot(below, one_hot(adj, LAYER))
                values += dot(above, one_hot(adj - (LAYER + total), LAYER))
            values = values.astype(jnp.bfloat16)
            if edge and f < 2:
                rows = partner_ref.shape[1]
                use = jnp.logical_and(step == 0, section == 1 - f)
                crossed = []
                for n in range(count):
                    wanted = partner_ref[n : n + 1, :]
                    arrived = jnp.zeros((width, rows), jnp.float32)
                    for d in range(shards):
                        source = lax.rem(space - d + shards, shards)
                        arrived += dot(pieces[d][n], one_hot(wanted - source * rows, rows))
                    crossed.append(arrived)
                crossed = jnp.concatenate(crossed, axis=0).astype(jnp.bfloat16)
                crossed = jnp.concatenate(
                    [crossed, jnp.zeros((count * width, tile - rows), jnp.bfloat16)], axis=1)
                take = jnp.logical_and(column < rows, use)
                values = jnp.where(take, crossed, values)
            found.append(values)
        return found

    def finish(edge):
        found = gathered(edge)
        frequency = freq_ref[0]
        scale = scale_ref[...]
        inverse_scale = 1.0 / scale
        for n in range(count):
            for d in range(1, peers):
                owner = lax.rem(inst - d + peers, peers)
                for m in range(count):
                    weight = table_ref[inst * count + n, owner * count + m] * frequency
                    at = (n * (peers - 1) + d - 1) * count + m
                    factor_ref[at : at + 1, :] = weight * inverse_scale
        for n in range(count):
            beside = jnp.concatenate([v[n * width : (n + 1) * width] for v in found], axis=0)
            inner = dot(lift_ref[...], beside) + dot(volume_ref[...], tile_ref[n])
            value = forcing_ref[n].astype(jnp.float32) - scale * inner
            for m in range(count):
                weight = table_ref[inst * count + n, inst * count + m] * frequency
                value -= weight * tile_ref[m].astype(jnp.float32)
            update = dot(inverse_ref[...], value.astype(jnp.bfloat16))
            out_ref[n] = tile_ref[n].astype(jnp.float32) + update * inverse_scale

    @pl.when(at_edge)
    def _():
        finish(True)

    @pl.when(jnp.logical_not(at_edge))
    def _():
        finish(False)


def update_kernel(tile, ready_ref, factor_ref, inverse_ref, *rest):
    others, (out_ref, taken, made, in_sems, sems) = rest[:-5], rest[-5:]
    count, dof, total = ready_ref.shape
    steps = total // tile
    loads = []
    for t in range(steps):
        for d, other in enumerate(others):
            load = pltpu.make_async_copy(
                other.at[:, :, t * tile : (t + 1) * tile], taken.at[t, d], in_sems.at[t, d])
            load.start()
            loads.append(load)
    copies = []
    for t in range(steps):
        cols = slice(t * tile, (t + 1) * tile)
        for load in loads[t * len(others) : (t + 1) * len(others)]:
            load.wait()
        moved = [dot(inverse_ref[...], taken[t, d, m]) for d in range(len(others)) for m in range(count)]
        for n in range(count):
            value = ready_ref[n, :, cols]
            for k, part in enumerate(moved):
                at = n * len(moved) + k
                value -= factor_ref[at : at + 1, cols] * part
            made[t, n] = value.astype(jnp.bfloat16)
        copy = pltpu.make_async_copy(made.at[t], out_ref.at[:, :, cols], sems.at[t])
        copy.start()
        copies.append(copy)
    for copy in copies:
        copy.wait()


def whole(array):
    return pl.BlockSpec(array.shape, lambda j: (0,) * array.ndim)


def body(solution, forcing, metric_scale, frequency, adjacency, partner, volume_matrix, trace_matrix, lift_matrix,
         block_inverse):
    current = solution[0]
    forcing_local = forcing[0]
    neighbours = adjacency[0]
    partner_rows = partner[0]
    count, dof, total = current.shape
    width = trace_matrix.shape[0] // 6
    iface_rows = partner_rows.shape[1]
    shards = lax.axis_size("space")
    peers = lax.axis_size("inst")
    section = lax.axis_index("row")
    place = jnp.stack([section, lax.axis_index("inst"), lax.axis_index("space")]).astype(jnp.int32)
    table = jnp.asarray(spectral_table(count * peers))
    smem = pl.BlockSpec(memory_space=pltpu.SMEM)
    bf16 = jnp.bfloat16

    with jax.named_scope("instances"):
        others = [lax.ppermute(current, "inst", [(i, (i + d) % peers) for i in range(peers)])
                  for d in range(1, peers)]

    with jax.named_scope("ends"):
        up, down, cross = pl.pallas_call(
            ends_kernel,
            grid=(1,),
            out_shape=(jax.ShapeDtypeStruct((count, 2 * width, LAYER), bf16),
                       jax.ShapeDtypeStruct((count, 2 * width, LAYER), bf16),
                       jax.ShapeDtypeStruct((count, width, iface_rows), bf16)),
            in_specs=[smem,
                      pl.BlockSpec((count, dof, LANES), lambda j: (0, 0, 0)),
                      pl.BlockSpec((count, dof, LANES), lambda j: (0, 0, total // LANES - 1)),
                      whole(trace_matrix)],
            out_specs=(pl.BlockSpec((count, 2 * width, LAYER), lambda j: (0, 0, 0)),
                       pl.BlockSpec((count, 2 * width, LAYER), lambda j: (0, 0, 0)),
                       pl.BlockSpec((count, width, iface_rows), lambda j: (0, 0, 0))),
            compiler_params=pltpu.CompilerParams(vmem_limit_bytes=ENDS_LIMIT),
            cost_estimate=pl.CostEstimate(flops=8 * width * dof * LANES * 2 * count,
                                          bytes_accessed=1_000_000, transcendentals=0),
            name="ends",
        )(place, current, current, trace_matrix)

    with jax.named_scope("halo"):
        low = lax.ppermute(up, "space", [(i, (i + 1) % shards) for i in range(shards)])
        high = lax.ppermute(down, "space", [(i, (i - 1) % shards) for i in range(shards)])
    with jax.named_scope("interface"):
        pieces = [lax.ppermute(cross, ("space", "row"),
                               [(i * 2 + r, (i + d) % shards * 2 + 1 - r) for i in range(shards) for r in range(2)])
                  for d in range(shards)]

    tile = 256
    steps = total // tile
    by_tile = lambda *lead: pl.BlockSpec(lead + (tile,), lambda j: (0,) * len(lead) + (j,))
    with jax.named_scope("couple"):
        ready, factors = pl.pallas_call(
            functools.partial(couple_kernel, shards, peers),
            grid=(steps,),
            out_shape=(jax.ShapeDtypeStruct((count, dof, total), jnp.float32),
                       jax.ShapeDtypeStruct((count * count * (peers - 1), total), jnp.float32)),
            in_specs=[smem, smem, smem, by_tile(6), whole(partner_rows), whole(current), by_tile(count, dof),
                      by_tile(count, dof), by_tile(1), whole(trace_matrix), whole(lift_matrix),
                      whole(volume_matrix), whole(block_inverse), whole(low), whole(high)] + [whole(p) for p in pieces],
            out_specs=(by_tile(count, dof), by_tile(count * count * (peers - 1))),
            scratch_shapes=[pltpu.VMEM((6, count * width, total), bf16)],
            compiler_params=pltpu.CompilerParams(vmem_limit_bytes=VMEM_LIMIT),
            cost_estimate=pl.CostEstimate(
                flops=2 * count * total * (6 * width * dof * 2 + dof * dof + 6 * width * total),
                bytes_accessed=count * dof * total * 10, transcendentals=0),
            name="couple",
        )(place, frequency, table, neighbours, partner_rows, current, current, forcing_local, metric_scale,
          trace_matrix, lift_matrix, volume_matrix, block_inverse, low, high, *pieces)

    vmem = pl.BlockSpec(memory_space=pltpu.VMEM)
    with jax.named_scope("update"):
        result = pl.pallas_call(
            functools.partial(update_kernel, tile),
            out_shape=jax.ShapeDtypeStruct((count, dof, total), bf16),
            in_specs=[vmem] * 3 + [pl.BlockSpec(memory_space=pl.ANY)] * (peers - 1),
            out_specs=pl.BlockSpec(memory_space=pl.ANY),
            scratch_shapes=[pltpu.VMEM((steps, peers - 1, count, dof, tile), bf16),
                            pltpu.VMEM((steps, count, dof, tile), bf16),
                            pltpu.SemaphoreType.DMA((steps, peers - 1)), pltpu.SemaphoreType.DMA((steps,))],
            compiler_params=pltpu.CompilerParams(vmem_limit_bytes=UPDATE_LIMIT),
            cost_estimate=pl.CostEstimate(flops=2 * count * total * dof * dof * (peers - 1),
                                          bytes_accessed=count * dof * total * 8, transcendentals=0),
            name="update",
        )(ready, factors, block_inverse, *others)
    return result[None]


def solution(mesh):
    in_specs = (
        P("row", "inst", None, ("groups", "space")),
        P("row", "inst", None, ("groups", "space")),
        P("row", ("groups", "space")),
        P(),
        P("row", None, ("groups", "space")),
        P("row", "inst", ("groups", "space")),
        P(),
        P(),
        P(),
        P(),
    )
    out_specs = P("row", "inst", None, ("groups", "space"))
    return jax.shard_map(body, mesh=mesh, in_specs=in_specs, out_specs=out_specs, check_vma=False)
```

```python
import functools

import jax
import jax.numpy as jnp
import numpy as np
from jax import lax
from jax.experimental import pallas as pl
from jax.experimental.pallas import tpu as pltpu
from jax.sharding import PartitionSpec as P

LAYER = 64
OPPOSITE = (1, 0, 3, 2, 5, 4)
LANES = 128
VMEM_LIMIT = 40 * 1024 * 1024


def spectral_table(instances):
    positions = np.arange(instances)
    distance = positions[:, None] - positions[None, :]
    parity = np.where(distance % 2 == 0, 1.0, -1.0)
    angles = np.pi * distance / instances
    sines = np.where(distance == 0, 1.0, np.sin(angles))
    cotangent = np.where(distance == 0, 0.0, np.cos(angles) / sines)
    return (0.5 * parity * cotangent).astype(np.float32)


def one_hot(picked, rows):
    numbers = lax.broadcasted_iota(jnp.int32, (rows, picked.shape[1]), 0)
    return jnp.where(numbers == picked, 1.0, 0.0).astype(jnp.bfloat16)


def dot(left, right):
    return jnp.dot(left, right, preferred_element_type=jnp.float32)


def ends_kernel(place_ref, first_ref, last_ref, trace_ref, up_ref, down_ref, cross_ref):
    width = trace_ref.shape[0] // 6
    section = place_ref[0]
    for n in range(first_ref.shape[0]):
        first = dot(trace_ref[...], first_ref[n]).astype(jnp.bfloat16)
        last = dot(trace_ref[4 * width :, :], last_ref[n]).astype(jnp.bfloat16)
        down_ref[n] = first[4 * width :, :LAYER]
        up_ref[n] = last[:, last.shape[1] - LAYER :]
        rows = cross_ref.shape[2]
        cross_ref[n] = jnp.where(section == 0, first[width : 2 * width, :rows], first[:width, :rows])


def couple_kernel(shards, peers, place_ref, freq_ref, table_ref, adj_ref, partner_ref, all_ref, tile_ref, forcing_ref,
                  scale_ref, trace_ref, lift_ref, volume_ref, inverse_ref, low_ref, high_ref, *rest):
    pieces, (out_ref, factor_ref, traces) = rest[:shards], rest[shards:]
    step = pl.program_id(0)
    steps = pl.num_programs(0)
    count, dof, total = all_ref.shape
    width = trace_ref.shape[0] // 6
    tile = tile_ref.shape[2]
    section, inst, space = place_ref[0], place_ref[1], place_ref[2]

    @pl.when(step == 0)
    def _():
        for n in range(count):
            for c in range(total // tile):
                cols = slice(c * tile, (c + 1) * tile)
                made = dot(trace_ref[...], all_ref[n, :, cols]).astype(jnp.bfloat16)
                for f in range(6):
                    traces[f, n * width : (n + 1) * width, cols] = made[f * width : (f + 1) * width]

    column = lax.broadcasted_iota(jnp.int32, (1, tile), 1)
    at_edge = jnp.logical_or(step == 0, step == steps - 1)

    def gathered(edge):
        found = []
        for f in range(6):
            adj = adj_ref[f : f + 1, :]
            values = dot(traces[OPPOSITE[f]], one_hot(adj - LAYER, total))
            if edge and f >= 4:
                part = slice((5 - f) * width, (6 - f) * width)
                below = jnp.concatenate([low_ref[n, part, :] for n in range(count)], axis=0)
                above = jnp.concatenate([high_ref[n, part, :] for n in range(count)], axis=0)
                values += dot(below, one_hot(adj, LAYER))
                values += dot(above, one_hot(adj - (LAYER + total), LAYER))
            values = values.astype(jnp.bfloat16)
            if edge and f < 2:
                rows = partner_ref.shape[1]
                use = jnp.logical_and(step == 0, section == 1 - f)
                crossed = []
                for n in range(count):
                    wanted = partner_ref[n : n + 1, :]
                    arrived = jnp.zeros((width, rows), jnp.float32)
                    for d in range(shards):
                        source = lax.rem(space - d + shards, shards)
                        arrived += dot(pieces[d][n], one_hot(wanted - source * rows, rows))
                    crossed.append(arrived)
                crossed = jnp.concatenate(crossed, axis=0).astype(jnp.bfloat16)
                crossed = jnp.concatenate(
                    [crossed, jnp.zeros((count * width, tile - rows), jnp.bfloat16)], axis=1)
                take = jnp.logical_and(column < rows, use)
                values = jnp.where(take, crossed, values)
            found.append(values)
        return found

    def finish(edge):
        found = gathered(edge)
        frequency = freq_ref[0]
        scale = scale_ref[...]
        inverse_scale = 1.0 / scale
        for n in range(count):
            for d in range(1, peers):
                owner = lax.rem(inst - d + peers, peers)
                for m in range(count):
                    weight = table_ref[inst * count + n, owner * count + m] * frequency
                    at = (n * (peers - 1) + d - 1) * count + m
                    factor_ref[at : at + 1, :] = weight * inverse_scale
        for n in range(count):
            beside = jnp.concatenate([v[n * width : (n + 1) * width] for v in found], axis=0)
            inner = dot(lift_ref[...], beside) + dot(volume_ref[...], tile_ref[n])
            value = forcing_ref[n].astype(jnp.float32) - scale * inner
            for m in range(count):
                weight = table_ref[inst * count + n, inst * count + m] * frequency
                value -= weight * tile_ref[m].astype(jnp.float32)
            update = dot(inverse_ref[...], value.astype(jnp.bfloat16))
            out_ref[n] = tile_ref[n].astype(jnp.float32) + update * inverse_scale

    @pl.when(at_edge)
    def _():
        finish(True)

    @pl.when(jnp.logical_not(at_edge))
    def _():
        finish(False)


def update_kernel(tile, ready_ref, factor_ref, inverse_ref, *rest):
    others, (out_ref, made, sems) = rest[:-3], rest[-3:]
    count, dof, total = ready_ref.shape
    copies = []
    for t in range(total // tile):
        cols = slice(t * tile, (t + 1) * tile)
        moved = [dot(inverse_ref[...], other[m, :, cols]) for other in others for m in range(count)]
        for n in range(count):
            value = ready_ref[n, :, cols]
            for k, part in enumerate(moved):
                at = n * len(moved) + k
                value -= factor_ref[at : at + 1, cols] * part
            made[t, n] = value.astype(jnp.bfloat16)
        copy = pltpu.make_async_copy(made.at[t], out_ref.at[:, :, cols], sems.at[t])
        copy.start(priority=t % 2)
        copies.append(copy)
    for copy in copies:
        copy.wait()


def whole(array):
    return pl.BlockSpec(array.shape, lambda j: (0,) * array.ndim)


def body(solution, forcing, metric_scale, frequency, adjacency, partner, volume_matrix, trace_matrix, lift_matrix,
         block_inverse):
    current = solution[0]
    forcing_local = forcing[0]
    neighbours = adjacency[0]
    partner_rows = partner[0]
    count, dof, total = current.shape
    width = trace_matrix.shape[0] // 6
    iface_rows = partner_rows.shape[1]
    shards = lax.axis_size("space")
    peers = lax.axis_size("inst")
    section = lax.axis_index("row")
    place = jnp.stack([section, lax.axis_index("inst"), lax.axis_index("space")]).astype(jnp.int32)
    table = jnp.asarray(spectral_table(count * peers))
    smem = pl.BlockSpec(memory_space=pltpu.SMEM)
    bf16 = jnp.bfloat16

    with jax.named_scope("instances"):
        others = [lax.ppermute(current, "inst", [(i, (i + d) % peers) for i in range(peers)])
                  for d in range(1, peers)]

    with jax.named_scope("ends"):
        up, down, cross = pl.pallas_call(
            ends_kernel,
            grid=(1,),
            out_shape=(jax.ShapeDtypeStruct((count, 2 * width, LAYER), bf16),
                       jax.ShapeDtypeStruct((count, 2 * width, LAYER), bf16),
                       jax.ShapeDtypeStruct((count, width, iface_rows), bf16)),
            in_specs=[smem,
                      pl.BlockSpec((count, dof, LANES), lambda j: (0, 0, 0)),
                      pl.BlockSpec((count, dof, LANES), lambda j: (0, 0, total // LANES - 1)),
                      whole(trace_matrix)],
            out_specs=(pl.BlockSpec((count, 2 * width, LAYER), lambda j: (0, 0, 0)),
                       pl.BlockSpec((count, 2 * width, LAYER), lambda j: (0, 0, 0)),
                       pl.BlockSpec((count, width, iface_rows), lambda j: (0, 0, 0))),
            compiler_params=pltpu.CompilerParams(vmem_limit_bytes=VMEM_LIMIT),
            cost_estimate=pl.CostEstimate(flops=8 * width * dof * LANES * 2 * count,
                                          bytes_accessed=1_000_000, transcendentals=0),
            name="ends",
        )(place, current, current, trace_matrix)

    with jax.named_scope("halo"):
        low = lax.ppermute(up, "space", [(i, (i + 1) % shards) for i in range(shards)])
        high = lax.ppermute(down, "space", [(i, (i - 1) % shards) for i in range(shards)])
    with jax.named_scope("interface"):
        pieces = [lax.ppermute(cross, ("space", "row"),
                               [(i * 2 + r, (i + d) % shards * 2 + 1 - r) for i in range(shards) for r in range(2)])
                  for d in range(shards)]

    tile = 256
    steps = total // tile
    by_tile = lambda *lead: pl.BlockSpec(lead + (tile,), lambda j: (0,) * len(lead) + (j,))
    with jax.named_scope("couple"):
        ready, factors = pl.pallas_call(
            functools.partial(couple_kernel, shards, peers),
            grid=(steps,),
            out_shape=(jax.ShapeDtypeStruct((count, dof, total), jnp.float32),
                       jax.ShapeDtypeStruct((count * count * (peers - 1), total), jnp.float32)),
            in_specs=[smem, smem, smem, by_tile(6), whole(partner_rows), whole(current), by_tile(count, dof),
                      by_tile(count, dof), by_tile(1), whole(trace_matrix), whole(lift_matrix),
                      whole(volume_matrix), whole(block_inverse), whole(low), whole(high)] + [whole(p) for p in pieces],
            out_specs=(by_tile(count, dof), by_tile(count * count * (peers - 1))),
            scratch_shapes=[pltpu.VMEM((6, count * width, total), bf16)],
            compiler_params=pltpu.CompilerParams(vmem_limit_bytes=VMEM_LIMIT),
            cost_estimate=pl.CostEstimate(
                flops=2 * count * total * (6 * width * dof * 2 + dof * dof + 6 * width * total),
                bytes_accessed=count * dof * total * 10, transcendentals=0),
            name="couple",
        )(place, frequency, table, neighbours, partner_rows, current, current, forcing_local, metric_scale,
          trace_matrix, lift_matrix, volume_matrix, block_inverse, low, high, *pieces)

    vmem = pl.BlockSpec(memory_space=pltpu.VMEM)
    with jax.named_scope("update"):
        result = pl.pallas_call(
            functools.partial(update_kernel, tile),
            out_shape=jax.ShapeDtypeStruct((count, dof, total), bf16),
            in_specs=[vmem] * (2 + peers),
            out_specs=pl.BlockSpec(memory_space=pl.ANY),
            scratch_shapes=[pltpu.VMEM((steps, count, dof, tile), bf16), pltpu.SemaphoreType.DMA((steps,))],
            compiler_params=pltpu.CompilerParams(vmem_limit_bytes=VMEM_LIMIT),
            cost_estimate=pl.CostEstimate(flops=2 * count * total * dof * dof * (peers - 1),
                                          bytes_accessed=count * dof * total * 8, transcendentals=0),
            name="update",
        )(ready, factors, block_inverse, *others)
    return result[None]


def solution(mesh):
    in_specs = (
        P("row", "inst", None, ("groups", "space")),
        P("row", "inst", None, ("groups", "space")),
        P("row", ("groups", "space")),
        P(),
        P("row", None, ("groups", "space")),
        P("row", "inst", ("groups", "space")),
        P(),
        P(),
        P(),
        P(),
    )
    out_specs = P("row", "inst", None, ("groups", "space"))
    return jax.shard_map(body, mesh=mesh, in_specs=in_specs, out_specs=out_specs, check_vma=False)
```

```python
import functools

import jax
import jax.numpy as jnp
import numpy as np
from jax import lax
from jax.experimental import pallas as pl
from jax.experimental.pallas import tpu as pltpu
from jax.sharding import PartitionSpec as P

LAYER = 64
OPPOSITE = (1, 0, 3, 2, 5, 4)
LANES = 128
VMEM_LIMIT = 40 * 1024 * 1024


def spectral_table(instances):
    positions = np.arange(instances)
    distance = positions[:, None] - positions[None, :]
    parity = np.where(distance % 2 == 0, 1.0, -1.0)
    angles = np.pi * distance / instances
    sines = np.where(distance == 0, 1.0, np.sin(angles))
    cotangent = np.where(distance == 0, 0.0, np.cos(angles) / sines)
    return (0.5 * parity * cotangent).astype(np.float32)


def one_hot(picked, rows):
    numbers = lax.broadcasted_iota(jnp.int32, (rows, picked.shape[1]), 0)
    return jnp.where(numbers == picked, 1.0, 0.0).astype(jnp.bfloat16)


def dot(left, right):
    return jnp.dot(left, right, preferred_element_type=jnp.float32)


def ends_kernel(place_ref, first_ref, last_ref, trace_ref, up_ref, down_ref, cross_ref):
    width = trace_ref.shape[0] // 6
    section = place_ref[0]
    for n in range(first_ref.shape[0]):
        first = dot(trace_ref[...], first_ref[n]).astype(jnp.bfloat16)
        last = dot(trace_ref[4 * width :, :], last_ref[n]).astype(jnp.bfloat16)
        down_ref[n] = first[4 * width :, :LAYER]
        up_ref[n] = last[:, last.shape[1] - LAYER :]
        rows = cross_ref.shape[2]
        cross_ref[n] = jnp.where(section == 0, first[width : 2 * width, :rows], first[:width, :rows])


def couple_kernel(shards, peers, place_ref, freq_ref, table_ref, adj_ref, partner_ref, all_ref, tile_ref, forcing_ref,
                  scale_ref, trace_ref, lift_ref, volume_ref, inverse_ref, low_ref, high_ref, *rest):
    pieces, (out_ref, factor_ref, traces) = rest[:shards], rest[shards:]
    step = pl.program_id(0)
    steps = pl.num_programs(0)
    count, dof, total = all_ref.shape
    width = trace_ref.shape[0] // 6
    tile = tile_ref.shape[2]
    section, inst, space = place_ref[0], place_ref[1], place_ref[2]

    @pl.when(step == 0)
    def _():
        for n in range(count):
            for c in range(total // tile):
                cols = slice(c * tile, (c + 1) * tile)
                made = dot(trace_ref[...], all_ref[n, :, cols]).astype(jnp.bfloat16)
                for f in range(6):
                    traces[f, n * width : (n + 1) * width, cols] = made[f * width : (f + 1) * width]

    column = lax.broadcasted_iota(jnp.int32, (1, tile), 1)
    at_edge = jnp.logical_or(step == 0, step == steps - 1)

    def gathered(edge):
        found = []
        for f in range(6):
            adj = adj_ref[f : f + 1, :]
            values = dot(traces[OPPOSITE[f]], one_hot(adj - LAYER, total))
            if edge and f >= 4:
                part = slice((5 - f) * width, (6 - f) * width)
                below = jnp.concatenate([low_ref[n, part, :] for n in range(count)], axis=0)
                above = jnp.concatenate([high_ref[n, part, :] for n in range(count)], axis=0)
                values += dot(below, one_hot(adj, LAYER))
                values += dot(above, one_hot(adj - (LAYER + total), LAYER))
            values = values.astype(jnp.bfloat16)
            if edge and f < 2:
                rows = partner_ref.shape[1]
                use = jnp.logical_and(step == 0, section == 1 - f)
                crossed = []
                for n in range(count):
                    wanted = partner_ref[n : n + 1, :]
                    arrived = jnp.zeros((width, rows), jnp.float32)
                    for d in range(shards):
                        source = lax.rem(space - d + shards, shards)
                        arrived += dot(pieces[d][n], one_hot(wanted - source * rows, rows))
                    crossed.append(arrived)
                crossed = jnp.concatenate(crossed, axis=0).astype(jnp.bfloat16)
                crossed = jnp.concatenate(
                    [crossed, jnp.zeros((count * width, tile - rows), jnp.bfloat16)], axis=1)
                take = jnp.logical_and(column < rows, use)
                values = jnp.where(take, crossed, values)
            found.append(values)
        return found

    def finish(edge):
        found = gathered(edge)
        frequency = freq_ref[0]
        scale = scale_ref[...]
        inverse_scale = 1.0 / scale
        for n in range(count):
            for d in range(1, peers):
                owner = lax.rem(inst - d + peers, peers)
                for m in range(count):
                    weight = table_ref[inst * count + n, owner * count + m] * frequency
                    at = (n * (peers - 1) + d - 1) * count + m
                    factor_ref[at : at + 1, :] = weight * inverse_scale
        for n in range(count):
            beside = jnp.concatenate([v[n * width : (n + 1) * width] for v in found], axis=0)
            inner = dot(lift_ref[...], beside) + dot(volume_ref[...], tile_ref[n])
            value = forcing_ref[n].astype(jnp.float32) - scale * inner
            for m in range(count):
                weight = table_ref[inst * count + n, inst * count + m] * frequency
                value -= weight * tile_ref[m].astype(jnp.float32)
            update = dot(inverse_ref[...], value.astype(jnp.bfloat16))
            out_ref[n] = tile_ref[n].astype(jnp.float32) + update * inverse_scale

    @pl.when(at_edge)
    def _():
        finish(True)

    @pl.when(jnp.logical_not(at_edge))
    def _():
        finish(False)


def update_kernel(tile, ready_ref, factor_ref, inverse_ref, *rest):
    others, (out_ref, made, sems) = rest[:-3], rest[-3:]
    count, dof, total = ready_ref.shape

    def copy(t):
        cols = pl.ds(pl.multiple_of(t * tile, tile), tile)
        return pltpu.make_async_copy(made.at[t], out_ref.at[:, :, cols], sems.at[t])

    @pl.loop(0, total // tile)
    def _(t):
        cols = pl.ds(pl.multiple_of(t * tile, tile), tile)
        moved = [dot(inverse_ref[...], other[m, :, cols]) for other in others for m in range(count)]
        for n in range(count):
            value = ready_ref[n, :, cols]
            for k, part in enumerate(moved):
                at = n * len(moved) + k
                value -= factor_ref[at : at + 1, cols] * part
            made[t, n] = value.astype(jnp.bfloat16)
        copy(t).start()

    @pl.loop(0, total // tile)
    def _(t):
        copy(t).wait()


def whole(array):
    return pl.BlockSpec(array.shape, lambda j: (0,) * array.ndim)


def body(solution, forcing, metric_scale, frequency, adjacency, partner, volume_matrix, trace_matrix, lift_matrix,
         block_inverse):
    current = solution[0]
    forcing_local = forcing[0]
    neighbours = adjacency[0]
    partner_rows = partner[0]
    count, dof, total = current.shape
    width = trace_matrix.shape[0] // 6
    iface_rows = partner_rows.shape[1]
    shards = lax.axis_size("space")
    peers = lax.axis_size("inst")
    section = lax.axis_index("row")
    place = jnp.stack([section, lax.axis_index("inst"), lax.axis_index("space")]).astype(jnp.int32)
    table = jnp.asarray(spectral_table(count * peers))
    smem = pl.BlockSpec(memory_space=pltpu.SMEM)
    bf16 = jnp.bfloat16

    with jax.named_scope("instances"):
        others = [lax.ppermute(current, "inst", [(i, (i + d) % peers) for i in range(peers)])
                  for d in range(1, peers)]

    with jax.named_scope("ends"):
        up, down, cross = pl.pallas_call(
            ends_kernel,
            grid=(1,),
            out_shape=(jax.ShapeDtypeStruct((count, 2 * width, LAYER), bf16),
                       jax.ShapeDtypeStruct((count, 2 * width, LAYER), bf16),
                       jax.ShapeDtypeStruct((count, width, iface_rows), bf16)),
            in_specs=[smem,
                      pl.BlockSpec((count, dof, LANES), lambda j: (0, 0, 0)),
                      pl.BlockSpec((count, dof, LANES), lambda j: (0, 0, total // LANES - 1)),
                      whole(trace_matrix)],
            out_specs=(pl.BlockSpec((count, 2 * width, LAYER), lambda j: (0, 0, 0)),
                       pl.BlockSpec((count, 2 * width, LAYER), lambda j: (0, 0, 0)),
                       pl.BlockSpec((count, width, iface_rows), lambda j: (0, 0, 0))),
            compiler_params=pltpu.CompilerParams(vmem_limit_bytes=VMEM_LIMIT),
            cost_estimate=pl.CostEstimate(flops=8 * width * dof * LANES * 2 * count,
                                          bytes_accessed=1_000_000, transcendentals=0),
            name="ends",
        )(place, current, current, trace_matrix)

    with jax.named_scope("halo"):
        low = lax.ppermute(up, "space", [(i, (i + 1) % shards) for i in range(shards)])
        high = lax.ppermute(down, "space", [(i, (i - 1) % shards) for i in range(shards)])
    with jax.named_scope("interface"):
        pieces = [lax.ppermute(cross, ("space", "row"),
                               [(i * 2 + r, (i + d) % shards * 2 + 1 - r) for i in range(shards) for r in range(2)])
                  for d in range(shards)]

    tile = 256
    steps = total // tile
    by_tile = lambda *lead: pl.BlockSpec(lead + (tile,), lambda j: (0,) * len(lead) + (j,))
    with jax.named_scope("couple"):
        ready, factors = pl.pallas_call(
            functools.partial(couple_kernel, shards, peers),
            grid=(steps,),
            out_shape=(jax.ShapeDtypeStruct((count, dof, total), jnp.float32),
                       jax.ShapeDtypeStruct((count * count * (peers - 1), total), jnp.float32)),
            in_specs=[smem, smem, smem, by_tile(6), whole(partner_rows), whole(current), by_tile(count, dof),
                      by_tile(count, dof), by_tile(1), whole(trace_matrix), whole(lift_matrix),
                      whole(volume_matrix), whole(block_inverse), whole(low), whole(high)] + [whole(p) for p in pieces],
            out_specs=(by_tile(count, dof), by_tile(count * count * (peers - 1))),
            scratch_shapes=[pltpu.VMEM((6, count * width, total), bf16)],
            compiler_params=pltpu.CompilerParams(vmem_limit_bytes=VMEM_LIMIT),
            cost_estimate=pl.CostEstimate(
                flops=2 * count * total * (6 * width * dof * 2 + dof * dof + 6 * width * total),
                bytes_accessed=count * dof * total * 10, transcendentals=0),
            name="couple",
        )(place, frequency, table, neighbours, partner_rows, current, current, forcing_local, metric_scale,
          trace_matrix, lift_matrix, volume_matrix, block_inverse, low, high, *pieces)

    vmem = pl.BlockSpec(memory_space=pltpu.VMEM)
    with jax.named_scope("update"):
        result = pl.pallas_call(
            functools.partial(update_kernel, tile),
            out_shape=jax.ShapeDtypeStruct((count, dof, total), bf16),
            in_specs=[vmem] * (2 + peers),
            out_specs=pl.BlockSpec(memory_space=pl.ANY),
            scratch_shapes=[pltpu.VMEM((steps, count, dof, tile), bf16), pltpu.SemaphoreType.DMA((steps,))],
            compiler_params=pltpu.CompilerParams(vmem_limit_bytes=VMEM_LIMIT),
            cost_estimate=pl.CostEstimate(flops=2 * count * total * dof * dof * (peers - 1),
                                          bytes_accessed=count * dof * total * 8, transcendentals=0),
            name="update",
        )(ready, factors, block_inverse, *others)
    return result[None]


def solution(mesh):
    in_specs = (
        P("row", "inst", None, ("groups", "space")),
        P("row", "inst", None, ("groups", "space")),
        P("row", ("groups", "space")),
        P(),
        P("row", None, ("groups", "space")),
        P("row", "inst", ("groups", "space")),
        P(),
        P(),
        P(),
        P(),
    )
    out_specs = P("row", "inst", None, ("groups", "space"))
    return jax.shard_map(body, mesh=mesh, in_specs=in_specs, out_specs=out_specs, check_vma=False)
```

```python
import functools

import jax
import jax.numpy as jnp
import numpy as np
from jax import lax
from jax.experimental import pallas as pl
from jax.experimental.pallas import tpu as pltpu
from jax.sharding import PartitionSpec as P

LAYER = 64
OPPOSITE = (1, 0, 3, 2, 5, 4)
LANES = 128
STRIP = 32
VMEM_LIMIT = 40 * 1024 * 1024


def spectral_table(instances):
    positions = np.arange(instances)
    distance = positions[:, None] - positions[None, :]
    parity = np.where(distance % 2 == 0, 1.0, -1.0)
    angles = np.pi * distance / instances
    sines = np.where(distance == 0, 1.0, np.sin(angles))
    cotangent = np.where(distance == 0, 0.0, np.cos(angles) / sines)
    return (0.5 * parity * cotangent).astype(np.float32)


def one_hot(picked, rows):
    numbers = lax.broadcasted_iota(jnp.int32, (rows, picked.shape[1]), 0)
    return jnp.where(numbers == picked, 1.0, 0.0).astype(jnp.bfloat16)


def dot(left, right):
    return jnp.dot(left, right, preferred_element_type=jnp.float32)


def ends_kernel(place_ref, first_ref, last_ref, trace_ref, up_ref, down_ref, cross_ref):
    width = trace_ref.shape[0] // 6
    section = place_ref[0]
    for n in range(first_ref.shape[0]):
        first = dot(trace_ref[...], first_ref[n]).astype(jnp.bfloat16)
        last = dot(trace_ref[4 * width :, :], last_ref[n]).astype(jnp.bfloat16)
        down_ref[n] = first[4 * width :, :LAYER]
        up_ref[n] = last[:, last.shape[1] - LAYER :]
        rows = cross_ref.shape[2]
        cross_ref[n] = jnp.where(section == 0, first[width : 2 * width, :rows], first[:width, :rows])


def couple_kernel(shards, peers, place_ref, freq_ref, table_ref, adj_ref, partner_ref, all_ref, tile_ref, forcing_ref,
                  scale_ref, trace_ref, lift_ref, volume_ref, inverse_ref, low_ref, high_ref, *rest):
    pieces, (out_ref, factor_ref, traces) = rest[:shards], rest[shards:]
    step = pl.program_id(0)
    steps = pl.num_programs(0)
    count, dof, total = all_ref.shape
    width = trace_ref.shape[0] // 6
    tile = tile_ref.shape[2]
    section, inst, space = place_ref[0], place_ref[1], place_ref[2]

    @pl.when(step == 0)
    def _():
        for n in range(count):
            for c in range(total // tile):
                cols = slice(c * tile, (c + 1) * tile)
                made = dot(trace_ref[...], all_ref[n, :, cols]).astype(jnp.bfloat16)
                for f in range(6):
                    traces[f, n * width : (n + 1) * width, cols] = made[f * width : (f + 1) * width]

    column = lax.broadcasted_iota(jnp.int32, (1, tile), 1)
    at_edge = jnp.logical_or(step == 0, step == steps - 1)

    def gathered(edge):
        found = []
        for f in range(6):
            adj = adj_ref[f : f + 1, :]
            values = dot(traces[OPPOSITE[f]], one_hot(adj - LAYER, total))
            if edge and f >= 4:
                part = slice((5 - f) * width, (6 - f) * width)
                below = jnp.concatenate([low_ref[n, part, :] for n in range(count)], axis=0)
                above = jnp.concatenate([high_ref[n, part, :] for n in range(count)], axis=0)
                values += dot(below, one_hot(adj, LAYER))
                values += dot(above, one_hot(adj - (LAYER + total), LAYER))
            values = values.astype(jnp.bfloat16)
            if edge and f < 2:
                rows = partner_ref.shape[1]
                use = jnp.logical_and(step == 0, section == 1 - f)
                crossed = []
                for n in range(count):
                    wanted = partner_ref[n : n + 1, :]
                    arrived = jnp.zeros((width, rows), jnp.float32)
                    for d in range(shards):
                        source = lax.rem(space - d + shards, shards)
                        arrived += dot(pieces[d][n], one_hot(wanted - source * rows, rows))
                    crossed.append(arrived)
                crossed = jnp.concatenate(crossed, axis=0).astype(jnp.bfloat16)
                crossed = jnp.concatenate(
                    [crossed, jnp.zeros((count * width, tile - rows), jnp.bfloat16)], axis=1)
                take = jnp.logical_and(column < rows, use)
                values = jnp.where(take, crossed, values)
            found.append(values)
        return found

    def finish(edge):
        found = gathered(edge)
        frequency = freq_ref[0]
        scale = scale_ref[...]
        inverse_scale = 1.0 / scale
        for n in range(count):
            for d in range(1, peers):
                owner = lax.rem(inst - d + peers, peers)
                for m in range(count):
                    weight = table_ref[inst * count + n, owner * count + m] * frequency
                    at = (n * (peers - 1) + d - 1) * count + m
                    factor_ref[at : at + 1, :] = weight * inverse_scale
        for n in range(count):
            beside = jnp.concatenate([v[n * width : (n + 1) * width] for v in found], axis=0)
            inner = dot(lift_ref[...], beside) + dot(volume_ref[...], tile_ref[n])
            value = forcing_ref[n].astype(jnp.float32) - scale * inner
            for m in range(count):
                weight = table_ref[inst * count + n, inst * count + m] * frequency
                value -= weight * tile_ref[m].astype(jnp.float32)
            update = dot(inverse_ref[...], value.astype(jnp.bfloat16))
            out_ref[n] = tile_ref[n].astype(jnp.float32) + update * inverse_scale

    @pl.when(at_edge)
    def _():
        finish(True)

    @pl.when(jnp.logical_not(at_edge))
    def _():
        finish(False)


def update_kernel(tile, ready_ref, factor_ref, inverse_ref, *rest):
    others, (out_ref, made, moved, sems) = rest[:-4], rest[-4:]
    count, dof, total = ready_ref.shape
    products = len(others) * count
    steps = total // tile
    copies = []

    def multiply(t):
        for k in range(products):
            moved[t % 2, k] = dot(inverse_ref[...], others[k // count][k % count, :, t * tile : (t + 1) * tile])

    multiply(0)
    for t in range(steps):
        cols = slice(t * tile, (t + 1) * tile)
        if t + 1 < steps:
            multiply(t + 1)
        factors = [[factor_ref[n * products + k : n * products + k + 1, cols] for k in range(products)]
                   for n in range(count)]
        for strip in range(0, dof, STRIP):
            rows = slice(strip, strip + STRIP)
            parts = [moved[t % 2, k, rows, :] for k in range(products)]
            for n in range(count):
                value = ready_ref[n, rows, cols]
                for factor, part in zip(factors[n], parts):
                    value -= factor * part
                made[t, n, rows, :] = value.astype(jnp.bfloat16)
        copy = pltpu.make_async_copy(made.at[t], out_ref.at[:, :, cols], sems.at[t])
        copy.start()
        copies.append(copy)
    for copy in copies:
        copy.wait()


def whole(array):
    return pl.BlockSpec(array.shape, lambda j: (0,) * array.ndim)


def body(solution, forcing, metric_scale, frequency, adjacency, partner, volume_matrix, trace_matrix, lift_matrix,
         block_inverse):
    current = solution[0]
    forcing_local = forcing[0]
    neighbours = adjacency[0]
    partner_rows = partner[0]
    count, dof, total = current.shape
    width = trace_matrix.shape[0] // 6
    iface_rows = partner_rows.shape[1]
    shards = lax.axis_size("space")
    peers = lax.axis_size("inst")
    section = lax.axis_index("row")
    place = jnp.stack([section, lax.axis_index("inst"), lax.axis_index("space")]).astype(jnp.int32)
    table = jnp.asarray(spectral_table(count * peers))
    smem = pl.BlockSpec(memory_space=pltpu.SMEM)
    bf16 = jnp.bfloat16

    with jax.named_scope("instances"):
        others = [lax.ppermute(current, "inst", [(i, (i + d) % peers) for i in range(peers)])
                  for d in range(1, peers)]

    with jax.named_scope("ends"):
        up, down, cross = pl.pallas_call(
            ends_kernel,
            grid=(1,),
            out_shape=(jax.ShapeDtypeStruct((count, 2 * width, LAYER), bf16),
                       jax.ShapeDtypeStruct((count, 2 * width, LAYER), bf16),
                       jax.ShapeDtypeStruct((count, width, iface_rows), bf16)),
            in_specs=[smem,
                      pl.BlockSpec((count, dof, LANES), lambda j: (0, 0, 0)),
                      pl.BlockSpec((count, dof, LANES), lambda j: (0, 0, total // LANES - 1)),
                      whole(trace_matrix)],
            out_specs=(pl.BlockSpec((count, 2 * width, LAYER), lambda j: (0, 0, 0)),
                       pl.BlockSpec((count, 2 * width, LAYER), lambda j: (0, 0, 0)),
                       pl.BlockSpec((count, width, iface_rows), lambda j: (0, 0, 0))),
            compiler_params=pltpu.CompilerParams(vmem_limit_bytes=VMEM_LIMIT),
            cost_estimate=pl.CostEstimate(flops=8 * width * dof * LANES * 2 * count,
                                          bytes_accessed=1_000_000, transcendentals=0),
            name="ends",
        )(place, current, current, trace_matrix)

    with jax.named_scope("halo"):
        low = lax.ppermute(up, "space", [(i, (i + 1) % shards) for i in range(shards)])
        high = lax.ppermute(down, "space", [(i, (i - 1) % shards) for i in range(shards)])
    with jax.named_scope("interface"):
        pieces = [lax.ppermute(cross, ("space", "row"),
                               [(i * 2 + r, (i + d) % shards * 2 + 1 - r) for i in range(shards) for r in range(2)])
                  for d in range(shards)]

    tile = 256
    steps = total // tile
    by_tile = lambda *lead: pl.BlockSpec(lead + (tile,), lambda j: (0,) * len(lead) + (j,))
    with jax.named_scope("couple"):
        ready, factors = pl.pallas_call(
            functools.partial(couple_kernel, shards, peers),
            grid=(steps,),
            out_shape=(jax.ShapeDtypeStruct((count, dof, total), jnp.float32),
                       jax.ShapeDtypeStruct((count * count * (peers - 1), total), jnp.float32)),
            in_specs=[smem, smem, smem, by_tile(6), whole(partner_rows), whole(current), by_tile(count, dof),
                      by_tile(count, dof), by_tile(1), whole(trace_matrix), whole(lift_matrix),
                      whole(volume_matrix), whole(block_inverse), whole(low), whole(high)] + [whole(p) for p in pieces],
            out_specs=(by_tile(count, dof), by_tile(count * count * (peers - 1))),
            scratch_shapes=[pltpu.VMEM((6, count * width, total), bf16)],
            compiler_params=pltpu.CompilerParams(vmem_limit_bytes=VMEM_LIMIT),
            cost_estimate=pl.CostEstimate(
                flops=2 * count * total * (6 * width * dof * 2 + dof * dof + 6 * width * total),
                bytes_accessed=count * dof * total * 10, transcendentals=0),
            name="couple",
        )(place, frequency, table, neighbours, partner_rows, current, current, forcing_local, metric_scale,
          trace_matrix, lift_matrix, volume_matrix, block_inverse, low, high, *pieces)

    vmem = pl.BlockSpec(memory_space=pltpu.VMEM)
    with jax.named_scope("update"):
        result = pl.pallas_call(
            functools.partial(update_kernel, tile),
            out_shape=jax.ShapeDtypeStruct((count, dof, total), bf16),
            in_specs=[vmem] * (2 + peers),
            out_specs=pl.BlockSpec(memory_space=pl.ANY),
            scratch_shapes=[pltpu.VMEM((steps, count, dof, tile), bf16),
                            pltpu.VMEM((2, (peers - 1) * count, dof, tile), jnp.float32),
                            pltpu.SemaphoreType.DMA((steps,))],
            compiler_params=pltpu.CompilerParams(vmem_limit_bytes=VMEM_LIMIT),
            cost_estimate=pl.CostEstimate(flops=2 * count * total * dof * dof * (peers - 1),
                                          bytes_accessed=count * dof * total * 8, transcendentals=0),
            name="update",
        )(ready, factors, block_inverse, *others)
    return result[None]


def solution(mesh):
    in_specs = (
        P("row", "inst", None, ("groups", "space")),
        P("row", "inst", None, ("groups", "space")),
        P("row", ("groups", "space")),
        P(),
        P("row", None, ("groups", "space")),
        P("row", "inst", ("groups", "space")),
        P(),
        P(),
        P(),
        P(),
    )
    out_specs = P("row", "inst", None, ("groups", "space"))
    return jax.shard_map(body, mesh=mesh, in_specs=in_specs, out_specs=out_specs, check_vma=False)
```

```python
import functools

import jax
import jax.numpy as jnp
import numpy as np
from jax import lax
from jax.experimental import pallas as pl
from jax.experimental.pallas import tpu as pltpu
from jax.sharding import PartitionSpec as P

LAYER = 64
OPPOSITE = (1, 0, 3, 2, 5, 4)
LANES = 128
VMEM_LIMIT = 40 * 1024 * 1024


def spectral_table(instances):
    positions = np.arange(instances)
    distance = positions[:, None] - positions[None, :]
    parity = np.where(distance % 2 == 0, 1.0, -1.0)
    angles = np.pi * distance / instances
    sines = np.where(distance == 0, 1.0, np.sin(angles))
    cotangent = np.where(distance == 0, 0.0, np.cos(angles) / sines)
    return (0.5 * parity * cotangent).astype(np.float32)


def one_hot(picked, rows):
    numbers = lax.broadcasted_iota(jnp.int32, (rows, picked.shape[1]), 0)
    return jnp.where(numbers == picked, 1.0, 0.0).astype(jnp.bfloat16)


def dot(left, right):
    return jnp.dot(left, right, preferred_element_type=jnp.float32)


def ends_kernel(place_ref, first_ref, last_ref, trace_ref, up_ref, down_ref, cross_ref):
    width = trace_ref.shape[0] // 6
    section = place_ref[0]
    for n in range(first_ref.shape[0]):
        first = dot(trace_ref[...], first_ref[n]).astype(jnp.bfloat16)
        last = dot(trace_ref[4 * width :, :], last_ref[n]).astype(jnp.bfloat16)
        down_ref[n] = first[4 * width :, :LAYER]
        up_ref[n] = last[:, last.shape[1] - LAYER :]
        rows = cross_ref.shape[2]
        cross_ref[n] = jnp.where(section == 0, first[width : 2 * width, :rows], first[:width, :rows])


def couple_kernel(shards, peers, place_ref, freq_ref, table_ref, adj_ref, partner_ref, all_ref, tile_ref, forcing_ref,
                  scale_ref, trace_ref, lift_ref, volume_ref, inverse_ref, low_ref, high_ref, *rest):
    pieces, (out_ref, factor_ref, traces) = rest[:shards], rest[shards:]
    step = pl.program_id(0)
    steps = pl.num_programs(0)
    count, dof, total = all_ref.shape
    width = trace_ref.shape[0] // 6
    tile = tile_ref.shape[2]
    section, inst, space = place_ref[0], place_ref[1], place_ref[2]

    @pl.when(step == 0)
    def _():
        for n in range(count):
            for c in range(total // tile):
                cols = slice(c * tile, (c + 1) * tile)
                made = dot(trace_ref[...], all_ref[n, :, cols]).astype(jnp.bfloat16)
                for f in range(6):
                    traces[f, n * width : (n + 1) * width, cols] = made[f * width : (f + 1) * width]

    column = lax.broadcasted_iota(jnp.int32, (1, tile), 1)
    at_edge = jnp.logical_or(step == 0, step == steps - 1)

    def gathered(edge):
        found = []
        for f in range(6):
            adj = adj_ref[f : f + 1, :]
            values = dot(traces[OPPOSITE[f]], one_hot(adj - LAYER, total))
            if edge and f >= 4:
                part = slice((5 - f) * width, (6 - f) * width)
                below = jnp.concatenate([low_ref[n, part, :] for n in range(count)], axis=0)
                above = jnp.concatenate([high_ref[n, part, :] for n in range(count)], axis=0)
                values += dot(below, one_hot(adj, LAYER))
                values += dot(above, one_hot(adj - (LAYER + total), LAYER))
            values = values.astype(jnp.bfloat16)
            if edge and f < 2:
                rows = partner_ref.shape[1]
                use = jnp.logical_and(step == 0, section == 1 - f)
                crossed = []
                for n in range(count):
                    wanted = partner_ref[n : n + 1, :]
                    arrived = jnp.zeros((width, rows), jnp.float32)
                    for d in range(shards):
                        source = lax.rem(space - d + shards, shards)
                        arrived += dot(pieces[d][n], one_hot(wanted - source * rows, rows))
                    crossed.append(arrived)
                crossed = jnp.concatenate(crossed, axis=0).astype(jnp.bfloat16)
                crossed = jnp.concatenate(
                    [crossed, jnp.zeros((count * width, tile - rows), jnp.bfloat16)], axis=1)
                take = jnp.logical_and(column < rows, use)
                values = jnp.where(take, crossed, values)
            found.append(values)
        return found

    def finish(edge):
        found = gathered(edge)
        frequency = freq_ref[0]
        scale = scale_ref[...]
        inverse_scale = 1.0 / scale
        for n in range(count):
            for d in range(1, peers):
                owner = lax.rem(inst - d + peers, peers)
                for m in range(count):
                    weight = table_ref[inst * count + n, owner * count + m] * frequency
                    at = (n * (peers - 1) + d - 1) * count + m
                    factor_ref[at : at + 1, :] = weight * inverse_scale
        for n in range(count):
            beside = jnp.concatenate([v[n * width : (n + 1) * width] for v in found], axis=0)
            inner = dot(lift_ref[...], beside) + dot(volume_ref[...], tile_ref[n])
            value = forcing_ref[n].astype(jnp.float32) - scale * inner
            for m in range(count):
                weight = table_ref[inst * count + n, inst * count + m] * frequency
                value -= weight * tile_ref[m].astype(jnp.float32)
            update = dot(inverse_ref[...], value.astype(jnp.bfloat16))
            out_ref[n] = tile_ref[n].astype(jnp.float32) + update * inverse_scale

    @pl.when(at_edge)
    def _():
        finish(True)

    @pl.when(jnp.logical_not(at_edge))
    def _():
        finish(False)


def update_kernel(tile, ready_ref, factor_ref, inverse_ref, *rest):
    others, (out_ref, made, sems) = rest[:-3], rest[-3:]
    count, dof, total = ready_ref.shape
    copies = []
    for t in range(total // tile):
        cols = slice(t * tile, (t + 1) * tile)
        moved = [dot(inverse_ref[...], other[m, :, cols]) for other in others for m in range(count)]
        for n in range(count):
            value = ready_ref[n, :, cols]
            for k, part in enumerate(moved):
                at = n * len(moved) + k
                value -= factor_ref[at : at + 1, cols] * part
            made[t, n] = value.astype(jnp.bfloat16)
        for n in range(count):
            for half in range(2):
                rows = slice(half * dof // 2, (half + 1) * dof // 2)
                copy = pltpu.make_async_copy(
                    made.at[t, n, rows, :], out_ref.at[n, rows, cols], sems.at[t, n, half])
                copy.start(priority=half)
                copies.append(copy)
    for copy in copies:
        copy.wait()


def whole(array):
    return pl.BlockSpec(array.shape, lambda j: (0,) * array.ndim)


def body(solution, forcing, metric_scale, frequency, adjacency, partner, volume_matrix, trace_matrix, lift_matrix,
         block_inverse):
    current = solution[0]
    forcing_local = forcing[0]
    neighbours = adjacency[0]
    partner_rows = partner[0]
    count, dof, total = current.shape
    width = trace_matrix.shape[0] // 6
    iface_rows = partner_rows.shape[1]
    shards = lax.axis_size("space")
    peers = lax.axis_size("inst")
    section = lax.axis_index("row")
    place = jnp.stack([section, lax.axis_index("inst"), lax.axis_index("space")]).astype(jnp.int32)
    table = jnp.asarray(spectral_table(count * peers))
    smem = pl.BlockSpec(memory_space=pltpu.SMEM)
    bf16 = jnp.bfloat16

    with jax.named_scope("instances"):
        others = [lax.ppermute(current, "inst", [(i, (i + d) % peers) for i in range(peers)])
                  for d in range(1, peers)]

    with jax.named_scope("ends"):
        up, down, cross = pl.pallas_call(
            ends_kernel,
            grid=(1,),
            out_shape=(jax.ShapeDtypeStruct((count, 2 * width, LAYER), bf16),
                       jax.ShapeDtypeStruct((count, 2 * width, LAYER), bf16),
                       jax.ShapeDtypeStruct((count, width, iface_rows), bf16)),
            in_specs=[smem,
                      pl.BlockSpec((count, dof, LANES), lambda j: (0, 0, 0)),
                      pl.BlockSpec((count, dof, LANES), lambda j: (0, 0, total // LANES - 1)),
                      whole(trace_matrix)],
            out_specs=(pl.BlockSpec((count, 2 * width, LAYER), lambda j: (0, 0, 0)),
                       pl.BlockSpec((count, 2 * width, LAYER), lambda j: (0, 0, 0)),
                       pl.BlockSpec((count, width, iface_rows), lambda j: (0, 0, 0))),
            compiler_params=pltpu.CompilerParams(vmem_limit_bytes=VMEM_LIMIT),
            cost_estimate=pl.CostEstimate(flops=8 * width * dof * LANES * 2 * count,
                                          bytes_accessed=1_000_000, transcendentals=0),
            name="ends",
        )(place, current, current, trace_matrix)

    with jax.named_scope("halo"):
        low = lax.ppermute(up, "space", [(i, (i + 1) % shards) for i in range(shards)])
        high = lax.ppermute(down, "space", [(i, (i - 1) % shards) for i in range(shards)])
    with jax.named_scope("interface"):
        pieces = [lax.ppermute(cross, ("space", "row"),
                               [(i * 2 + r, (i + d) % shards * 2 + 1 - r) for i in range(shards) for r in range(2)])
                  for d in range(shards)]

    tile = 256
    steps = total // tile
    by_tile = lambda *lead: pl.BlockSpec(lead + (tile,), lambda j: (0,) * len(lead) + (j,))
    with jax.named_scope("couple"):
        ready, factors = pl.pallas_call(
            functools.partial(couple_kernel, shards, peers),
            grid=(steps,),
            out_shape=(jax.ShapeDtypeStruct((count, dof, total), jnp.float32),
                       jax.ShapeDtypeStruct((count * count * (peers - 1), total), jnp.float32)),
            in_specs=[smem, smem, smem, by_tile(6), whole(partner_rows), whole(current), by_tile(count, dof),
                      by_tile(count, dof), by_tile(1), whole(trace_matrix), whole(lift_matrix),
                      whole(volume_matrix), whole(block_inverse), whole(low), whole(high)] + [whole(p) for p in pieces],
            out_specs=(by_tile(count, dof), by_tile(count * count * (peers - 1))),
            scratch_shapes=[pltpu.VMEM((6, count * width, total), bf16)],
            compiler_params=pltpu.CompilerParams(vmem_limit_bytes=VMEM_LIMIT),
            cost_estimate=pl.CostEstimate(
                flops=2 * count * total * (6 * width * dof * 2 + dof * dof + 6 * width * total),
                bytes_accessed=count * dof * total * 10, transcendentals=0),
            name="couple",
        )(place, frequency, table, neighbours, partner_rows, current, current, forcing_local, metric_scale,
          trace_matrix, lift_matrix, volume_matrix, block_inverse, low, high, *pieces)

    vmem = pl.BlockSpec(memory_space=pltpu.VMEM)
    with jax.named_scope("update"):
        result = pl.pallas_call(
            functools.partial(update_kernel, tile),
            out_shape=jax.ShapeDtypeStruct((count, dof, total), bf16),
            in_specs=[vmem] * (2 + peers),
            out_specs=pl.BlockSpec(memory_space=pl.ANY),
            scratch_shapes=[pltpu.VMEM((steps, count, dof, tile), bf16), pltpu.SemaphoreType.DMA((steps, count, 2))],
            compiler_params=pltpu.CompilerParams(vmem_limit_bytes=VMEM_LIMIT),
            cost_estimate=pl.CostEstimate(flops=2 * count * total * dof * dof * (peers - 1),
                                          bytes_accessed=count * dof * total * 8, transcendentals=0),
            name="update",
        )(ready, factors, block_inverse, *others)
    return result[None]


def solution(mesh):
    in_specs = (
        P("row", "inst", None, ("groups", "space")),
        P("row", "inst", None, ("groups", "space")),
        P("row", ("groups", "space")),
        P(),
        P("row", None, ("groups", "space")),
        P("row", "inst", ("groups", "space")),
        P(),
        P(),
        P(),
        P(),
    )
    out_specs = P("row", "inst", None, ("groups", "space"))
    return jax.shard_map(body, mesh=mesh, in_specs=in_specs, out_specs=out_specs, check_vma=False)
```

```python
import functools

import jax
import jax.numpy as jnp
import numpy as np
from jax import lax
from jax.experimental import pallas as pl
from jax.experimental.pallas import tpu as pltpu
from jax.sharding import PartitionSpec as P

LAYER = 64
OPPOSITE = (1, 0, 3, 2, 5, 4)
LANES = 128
VMEM_LIMIT = 40 * 1024 * 1024


def spectral_table(instances):
    positions = np.arange(instances)
    distance = positions[:, None] - positions[None, :]
    parity = np.where(distance % 2 == 0, 1.0, -1.0)
    angles = np.pi * distance / instances
    sines = np.where(distance == 0, 1.0, np.sin(angles))
    cotangent = np.where(distance == 0, 0.0, np.cos(angles) / sines)
    return (0.5 * parity * cotangent).astype(np.float32)


def one_hot(picked, rows):
    numbers = lax.broadcasted_iota(jnp.int32, (rows, picked.shape[1]), 0)
    return jnp.where(numbers == picked, 1.0, 0.0).astype(jnp.bfloat16)


def dot(left, right):
    return jnp.dot(left, right, preferred_element_type=jnp.float32)


def ends_kernel(place_ref, first_ref, last_ref, trace_ref, up_ref, down_ref, cross_ref):
    width = trace_ref.shape[0] // 6
    section = place_ref[0]
    for n in range(first_ref.shape[0]):
        first = dot(trace_ref[...], first_ref[n]).astype(jnp.bfloat16)
        last = dot(trace_ref[4 * width :, :], last_ref[n]).astype(jnp.bfloat16)
        down_ref[n] = first[4 * width :, :LAYER]
        up_ref[n] = last[:, last.shape[1] - LAYER :]
        rows = cross_ref.shape[2]
        cross_ref[n] = jnp.where(section == 0, first[width : 2 * width, :rows], first[:width, :rows])


def couple_kernel(shards, peers, place_ref, freq_ref, table_ref, adj_ref, partner_ref, all_ref, tile_ref, forcing_ref,
                  scale_ref, trace_ref, lift_ref, volume_ref, inverse_ref, low_ref, high_ref, *rest):
    pieces, (out_ref, factor_ref, traces) = rest[:shards], rest[shards:]
    step = pl.program_id(0)
    steps = pl.num_programs(0)
    count, dof, total = all_ref.shape
    width = trace_ref.shape[0] // 6
    tile = tile_ref.shape[2]
    section, inst, space = place_ref[0], place_ref[1], place_ref[2]

    @pl.when(step == 0)
    def _():
        for n in range(count):
            for c in range(total // tile):
                cols = slice(c * tile, (c + 1) * tile)
                made = dot(trace_ref[...], all_ref[n, :, cols]).astype(jnp.bfloat16)
                for f in range(6):
                    traces[f, n * width : (n + 1) * width, cols] = made[f * width : (f + 1) * width]

    column = lax.broadcasted_iota(jnp.int32, (1, tile), 1)
    at_edge = jnp.logical_or(step == 0, step == steps - 1)

    def gathered(edge):
        found = []
        for f in range(6):
            adj = adj_ref[f : f + 1, :]
            values = dot(traces[OPPOSITE[f]], one_hot(adj - LAYER, total))
            if edge and f >= 4:
                part = slice((5 - f) * width, (6 - f) * width)
                below = jnp.concatenate([low_ref[n, part, :] for n in range(count)], axis=0)
                above = jnp.concatenate([high_ref[n, part, :] for n in range(count)], axis=0)
                values += dot(below, one_hot(adj, LAYER))
                values += dot(above, one_hot(adj - (LAYER + total), LAYER))
            values = values.astype(jnp.bfloat16)
            if edge and f < 2:
                rows = partner_ref.shape[1]
                use = jnp.logical_and(step == 0, section == 1 - f)
                crossed = []
                for n in range(count):
                    wanted = partner_ref[n : n + 1, :]
                    arrived = jnp.zeros((width, rows), jnp.float32)
                    for d in range(shards):
                        source = lax.rem(space - d + shards, shards)
                        arrived += dot(pieces[d][n], one_hot(wanted - source * rows, rows))
                    crossed.append(arrived)
                crossed = jnp.concatenate(crossed, axis=0).astype(jnp.bfloat16)
                crossed = jnp.concatenate(
                    [crossed, jnp.zeros((count * width, tile - rows), jnp.bfloat16)], axis=1)
                take = jnp.logical_and(column < rows, use)
                values = jnp.where(take, crossed, values)
            found.append(values)
        return found

    def finish(edge):
        found = gathered(edge)
        frequency = freq_ref[0]
        scale = scale_ref[...]
        inverse_scale = 1.0 / scale
        for n in range(count):
            for d in range(1, peers):
                owner = lax.rem(inst - d + peers, peers)
                for m in range(count):
                    weight = table_ref[inst * count + n, owner * count + m] * frequency
                    at = (n * (peers - 1) + d - 1) * count + m
                    factor_ref[at : at + 1, :] = weight * inverse_scale
        for n in range(count):
            beside = jnp.concatenate([v[n * width : (n + 1) * width] for v in found], axis=0)
            inner = dot(lift_ref[...], beside) + dot(volume_ref[...], tile_ref[n])
            value = forcing_ref[n].astype(jnp.float32) - scale * inner
            for m in range(count):
                weight = table_ref[inst * count + n, inst * count + m] * frequency
                value -= weight * tile_ref[m].astype(jnp.float32)
            update = dot(inverse_ref[...], value.astype(jnp.bfloat16))
            out_ref[n] = tile_ref[n].astype(jnp.float32) + update * inverse_scale

    @pl.when(at_edge)
    def _():
        finish(True)

    @pl.when(jnp.logical_not(at_edge))
    def _():
        finish(False)


def update_kernel(tile, ready_ref, factor_ref, inverse_ref, *rest):
    others, (out_ref, made, sems) = rest[:-3], rest[-3:]
    count, dof, total = ready_ref.shape
    depths = [(low, min(low + tile, dof)) for low in range(0, dof, tile)]
    copies = []
    for t in range(total // tile):
        cols = slice(t * tile, (t + 1) * tile)
        moved = [[dot(inverse_ref[:, low:high], other[m, low:high, cols]) for low, high in depths]
                 for other in others for m in range(count)]
        moved = [functools.reduce(jnp.add, parts) for parts in moved]
        for n in range(count):
            value = ready_ref[n, :, cols]
            for k, part in enumerate(moved):
                at = n * len(moved) + k
                value -= factor_ref[at : at + 1, cols] * part
            made[t, n] = value.astype(jnp.bfloat16)
        copy = pltpu.make_async_copy(made.at[t], out_ref.at[:, :, cols], sems.at[t])
        copy.start()
        copies.append(copy)
    for copy in copies:
        copy.wait()


def whole(array):
    return pl.BlockSpec(array.shape, lambda j: (0,) * array.ndim)


def body(solution, forcing, metric_scale, frequency, adjacency, partner, volume_matrix, trace_matrix, lift_matrix,
         block_inverse):
    current = solution[0]
    forcing_local = forcing[0]
    neighbours = adjacency[0]
    partner_rows = partner[0]
    count, dof, total = current.shape
    width = trace_matrix.shape[0] // 6
    iface_rows = partner_rows.shape[1]
    shards = lax.axis_size("space")
    peers = lax.axis_size("inst")
    section = lax.axis_index("row")
    place = jnp.stack([section, lax.axis_index("inst"), lax.axis_index("space")]).astype(jnp.int32)
    table = jnp.asarray(spectral_table(count * peers))
    smem = pl.BlockSpec(memory_space=pltpu.SMEM)
    bf16 = jnp.bfloat16

    with jax.named_scope("instances"):
        others = [lax.ppermute(current, "inst", [(i, (i + d) % peers) for i in range(peers)])
                  for d in range(1, peers)]

    with jax.named_scope("ends"):
        up, down, cross = pl.pallas_call(
            ends_kernel,
            grid=(1,),
            out_shape=(jax.ShapeDtypeStruct((count, 2 * width, LAYER), bf16),
                       jax.ShapeDtypeStruct((count, 2 * width, LAYER), bf16),
                       jax.ShapeDtypeStruct((count, width, iface_rows), bf16)),
            in_specs=[smem,
                      pl.BlockSpec((count, dof, LANES), lambda j: (0, 0, 0)),
                      pl.BlockSpec((count, dof, LANES), lambda j: (0, 0, total // LANES - 1)),
                      whole(trace_matrix)],
            out_specs=(pl.BlockSpec((count, 2 * width, LAYER), lambda j: (0, 0, 0)),
                       pl.BlockSpec((count, 2 * width, LAYER), lambda j: (0, 0, 0)),
                       pl.BlockSpec((count, width, iface_rows), lambda j: (0, 0, 0))),
            compiler_params=pltpu.CompilerParams(vmem_limit_bytes=VMEM_LIMIT),
            cost_estimate=pl.CostEstimate(flops=8 * width * dof * LANES * 2 * count,
                                          bytes_accessed=1_000_000, transcendentals=0),
            name="ends",
        )(place, current, current, trace_matrix)

    with jax.named_scope("halo"):
        low = lax.ppermute(up, "space", [(i, (i + 1) % shards) for i in range(shards)])
        high = lax.ppermute(down, "space", [(i, (i - 1) % shards) for i in range(shards)])
    with jax.named_scope("interface"):
        pieces = [lax.ppermute(cross, ("space", "row"),
                               [(i * 2 + r, (i + d) % shards * 2 + 1 - r) for i in range(shards) for r in range(2)])
                  for d in range(shards)]

    tile = 256
    steps = total // tile
    by_tile = lambda *lead: pl.BlockSpec(lead + (tile,), lambda j: (0,) * len(lead) + (j,))
    with jax.named_scope("couple"):
        ready, factors = pl.pallas_call(
            functools.partial(couple_kernel, shards, peers),
            grid=(steps,),
            out_shape=(jax.ShapeDtypeStruct((count, dof, total), jnp.float32),
                       jax.ShapeDtypeStruct((count * count * (peers - 1), total), jnp.float32)),
            in_specs=[smem, smem, smem, by_tile(6), whole(partner_rows), whole(current), by_tile(count, dof),
                      by_tile(count, dof), by_tile(1), whole(trace_matrix), whole(lift_matrix),
                      whole(volume_matrix), whole(block_inverse), whole(low), whole(high)] + [whole(p) for p in pieces],
            out_specs=(by_tile(count, dof), by_tile(count * count * (peers - 1))),
            scratch_shapes=[pltpu.VMEM((6, count * width, total), bf16)],
            compiler_params=pltpu.CompilerParams(vmem_limit_bytes=VMEM_LIMIT),
            cost_estimate=pl.CostEstimate(
                flops=2 * count * total * (6 * width * dof * 2 + dof * dof + 6 * width * total),
                bytes_accessed=count * dof * total * 10, transcendentals=0),
            name="couple",
        )(place, frequency, table, neighbours, partner_rows, current, current, forcing_local, metric_scale,
          trace_matrix, lift_matrix, volume_matrix, block_inverse, low, high, *pieces)

    vmem = pl.BlockSpec(memory_space=pltpu.VMEM)
    with jax.named_scope("update"):
        result = pl.pallas_call(
            functools.partial(update_kernel, tile),
            out_shape=jax.ShapeDtypeStruct((count, dof, total), bf16),
            in_specs=[vmem] * (2 + peers),
            out_specs=pl.BlockSpec(memory_space=pl.ANY),
            scratch_shapes=[pltpu.VMEM((steps, count, dof, tile), bf16), pltpu.SemaphoreType.DMA((steps,))],
            compiler_params=pltpu.CompilerParams(vmem_limit_bytes=VMEM_LIMIT),
            cost_estimate=pl.CostEstimate(flops=2 * count * total * dof * dof * (peers - 1),
                                          bytes_accessed=count * dof * total * 8, transcendentals=0),
            name="update",
        )(ready, factors, block_inverse, *others)
    return result[None]


def solution(mesh):
    in_specs = (
        P("row", "inst", None, ("groups", "space")),
        P("row", "inst", None, ("groups", "space")),
        P("row", ("groups", "space")),
        P(),
        P("row", None, ("groups", "space")),
        P("row", "inst", ("groups", "space")),
        P(),
        P(),
        P(),
        P(),
    )
    out_specs = P("row", "inst", None, ("groups", "space"))
    return jax.shard_map(body, mesh=mesh, in_specs=in_specs, out_specs=out_specs, check_vma=False)
```

```python
import functools

import jax
import jax.numpy as jnp
import numpy as np
from jax import lax
from jax.experimental import pallas as pl
from jax.experimental.pallas import tpu as pltpu
from jax.sharding import PartitionSpec as P

LAYER = 64
OPPOSITE = (1, 0, 3, 2, 5, 4)
LANES = 128
VMEM_LIMIT = 40 * 1024 * 1024
CUT_LIMIT = 8 * 1024 * 1024
COUPLE_FLOPS = 7_500_000_000


def spectral_table(instances):
    positions = np.arange(instances)
    distance = positions[:, None] - positions[None, :]
    parity = np.where(distance % 2 == 0, 1.0, -1.0)
    angles = np.pi * distance / instances
    sines = np.where(distance == 0, 1.0, np.sin(angles))
    cotangent = np.where(distance == 0, 0.0, np.cos(angles) / sines)
    return (0.5 * parity * cotangent).astype(np.float32)


def one_hot(picked, rows):
    numbers = lax.broadcasted_iota(jnp.int32, (rows, picked.shape[1]), 0)
    return jnp.where(numbers == picked, 1.0, 0.0).astype(jnp.bfloat16)


def dot(left, right):
    return jnp.dot(left, right, preferred_element_type=jnp.float32)


def cut_kernel(bounds, before_ref, all_ref, *rest):
    out_refs, sems = rest[:-1], rest[-1]
    copies = []
    for k, (first, last) in enumerate(bounds):
        copies.append(pltpu.make_async_copy(all_ref.at[:, :, first:last], out_refs[k], sems.at[k]))
        copies[k].start()
    for copy in copies:
        copy.wait()


def ends_kernel(place_ref, first_ref, last_ref, trace_ref, up_ref, down_ref, cross_ref):
    width = trace_ref.shape[0] // 6
    section = place_ref[0]
    for n in range(first_ref.shape[0]):
        first = dot(trace_ref[...], first_ref[n]).astype(jnp.bfloat16)
        last = dot(trace_ref[4 * width :, :], last_ref[n]).astype(jnp.bfloat16)
        down_ref[n] = first[4 * width :, :LAYER]
        up_ref[n] = last[:, last.shape[1] - LAYER :]
        rows = cross_ref.shape[2]
        cross_ref[n] = jnp.where(section == 0, first[width : 2 * width, :rows], first[:width, :rows])


def couple_kernel(shards, peers, place_ref, freq_ref, table_ref, adj_ref, partner_ref, all_ref, tile_ref, forcing_ref,
                  scale_ref, trace_ref, lift_ref, volume_ref, inverse_ref, low_ref, high_ref, *rest):
    pieces, heads, (out_ref, factor_ref, traces) = rest[:shards], rest[shards:-3], rest[-3:]
    step = pl.program_id(0)
    steps = pl.num_programs(0)
    count, dof, total = all_ref.shape
    width = trace_ref.shape[0] // 6
    tile = tile_ref.shape[2]
    section, inst, space = place_ref[0], place_ref[1], place_ref[2]

    @pl.when(step == 0)
    def _():
        for n in range(count):
            for c in range(total // tile):
                cols = slice(c * tile, (c + 1) * tile)
                made = dot(trace_ref[...], all_ref[n, :, cols]).astype(jnp.bfloat16)
                for f in range(6):
                    traces[f, n * width : (n + 1) * width, cols] = made[f * width : (f + 1) * width]

    column = lax.broadcasted_iota(jnp.int32, (1, tile), 1)
    at_edge = jnp.logical_or(step == 0, step == steps - 1)

    def gathered(edge):
        found = []
        for f in range(6):
            adj = adj_ref[f : f + 1, :]
            values = dot(traces[OPPOSITE[f]], one_hot(adj - LAYER, total))
            if edge and f >= 4:
                part = slice((5 - f) * width, (6 - f) * width)
                below = jnp.concatenate([low_ref[n, part, :] for n in range(count)], axis=0)
                above = jnp.concatenate([high_ref[n, part, :] for n in range(count)], axis=0)
                values += dot(below, one_hot(adj, LAYER))
                values += dot(above, one_hot(adj - (LAYER + total), LAYER))
            values = values.astype(jnp.bfloat16)
            if edge and f < 2:
                rows = partner_ref.shape[1]
                use = jnp.logical_and(step == 0, section == 1 - f)
                crossed = []
                for n in range(count):
                    wanted = partner_ref[n : n + 1, :]
                    arrived = jnp.zeros((width, rows), jnp.float32)
                    for d in range(shards):
                        source = lax.rem(space - d + shards, shards)
                        arrived += dot(pieces[d][n], one_hot(wanted - source * rows, rows))
                    crossed.append(arrived)
                crossed = jnp.concatenate(crossed, axis=0).astype(jnp.bfloat16)
                crossed = jnp.concatenate(
                    [crossed, jnp.zeros((count * width, tile - rows), jnp.bfloat16)], axis=1)
                take = jnp.logical_and(column < rows, use)
                values = jnp.where(take, crossed, values)
            found.append(values)
        return found

    def finish(edge):
        found = gathered(edge)
        frequency = freq_ref[0]
        scale = scale_ref[...]
        inverse_scale = 1.0 / scale
        for n in range(count):
            for d in range(1, peers):
                owner = lax.rem(inst - d + peers, peers)
                for m in range(count):
                    weight = table_ref[inst * count + n, owner * count + m] * frequency
                    at = (n * (peers - 1) + d - 1) * count + m
                    factor_ref[at : at + 1, :] = weight * inverse_scale
        for n in range(count):
            beside = jnp.concatenate([v[n * width : (n + 1) * width] for v in found], axis=0)
            inner = dot(lift_ref[...], beside) + dot(volume_ref[...], tile_ref[n])
            value = forcing_ref[n].astype(jnp.float32) - scale * inner
            for m in range(count):
                weight = table_ref[inst * count + n, inst * count + m] * frequency
                value -= weight * tile_ref[m].astype(jnp.float32)
            update = dot(inverse_ref[...], value.astype(jnp.bfloat16))
            out_ref[n] = tile_ref[n].astype(jnp.float32) + update * inverse_scale

        @pl.when(step == 0)
        def _():
            moved = [dot(inverse_ref[...], head[m]) for head in heads for m in range(count)]
            for n in range(count):
                for k, part in enumerate(moved):
                    row = n * len(moved) + k
                    out_ref[n, :, :LANES] -= factor_ref[row : row + 1, :LANES] * part

    @pl.when(at_edge)
    def _():
        finish(True)

    @pl.when(jnp.logical_not(at_edge))
    def _():
        finish(False)


def update_kernel(base, bounds, peers, tile, ready_ref, factor_ref, inverse_ref, *rest):
    pieces = len(bounds) * (peers - 1)
    arrived, (out_ref, made, sems) = rest[:pieces], rest[-3:]
    count, dof, total = ready_ref.shape
    copies = []

    def send(first, last):
        copy = pltpu.make_async_copy(
            made.at[:, :, first - base : last - base], out_ref.at[:, :, first:last], sems.at[len(copies)])
        copy.start()
        copies.append(copy)

    if base < bounds[0][0]:
        for n in range(count):
            made[n, :, : bounds[0][0] - base] = ready_ref[n, :, base : bounds[0][0]].astype(jnp.bfloat16)
        send(base, bounds[0][0])
    for b, (first, last) in enumerate(bounds):
        others = arrived[b * (peers - 1) : (b + 1) * (peers - 1)]
        for start in range(first, last, tile):
            stop = min(start + tile, last)
            moved = [dot(inverse_ref[...], other[m, :, start - first : stop - first])
                     for other in others for m in range(count)]
            for n in range(count):
                value = ready_ref[n, :, start:stop]
                for k, part in enumerate(moved):
                    row = n * len(moved) + k
                    value -= factor_ref[row : row + 1, start:stop] * part
                made[n, :, start - base : stop - base] = value.astype(jnp.bfloat16)
            send(start, stop)
    for copy in copies:
        copy.wait()


def whole(array):
    return pl.BlockSpec(array.shape, lambda j: (0,) * array.ndim)


def body(solution, forcing, metric_scale, frequency, adjacency, partner, volume_matrix, trace_matrix, lift_matrix,
         block_inverse):
    current = solution[0]
    forcing_local = forcing[0]
    neighbours = adjacency[0]
    partner_rows = partner[0]
    count, dof, total = current.shape
    width = trace_matrix.shape[0] // 6
    iface_rows = partner_rows.shape[1]
    shards = lax.axis_size("space")
    peers = lax.axis_size("inst")
    section = lax.axis_index("row")
    place = jnp.stack([section, lax.axis_index("inst"), lax.axis_index("space")]).astype(jnp.int32)
    table = jnp.asarray(spectral_table(count * peers))
    smem = pl.BlockSpec(memory_space=pltpu.SMEM)
    bf16 = jnp.bfloat16

    with jax.named_scope("instances"):
        tile = 256
        bounds = [(0, LANES), (LANES, total - tile), (total - tile, total)]
        vmem = pl.BlockSpec(memory_space=pltpu.VMEM)
        (head,) = pl.pallas_call(
            functools.partial(cut_kernel, bounds[:1], None),
            out_shape=(jax.ShapeDtypeStruct((count, dof, LANES), bf16),),
            in_specs=[pl.BlockSpec(memory_space=pltpu.HBM)],
            out_specs=(vmem,),
            scratch_shapes=[pltpu.SemaphoreType.DMA((1,))],
            compiler_params=pltpu.CompilerParams(vmem_limit_bytes=CUT_LIMIT),
            cost_estimate=pl.CostEstimate(flops=0, bytes_accessed=0, transcendentals=0),
            name="head",
        )(pltpu.with_memory_space_constraint(current, pltpu.HBM))
        chunks = [head] + list(pl.pallas_call(
            functools.partial(cut_kernel, bounds[1:]),
            out_shape=tuple(jax.ShapeDtypeStruct((count, dof, last - first), bf16) for first, last in bounds[1:]),
            in_specs=[pl.BlockSpec(memory_space=pl.ANY), pl.BlockSpec(memory_space=pltpu.HBM)],
            out_specs=tuple([vmem] * (len(bounds) - 1)),
            scratch_shapes=[pltpu.SemaphoreType.DMA((len(bounds) - 1,))],
            compiler_params=pltpu.CompilerParams(vmem_limit_bytes=CUT_LIMIT),
            cost_estimate=pl.CostEstimate(flops=0, bytes_accessed=0, transcendentals=0),
            name="cut",
        )(head, pltpu.with_memory_space_constraint(current, pltpu.HBM)))
        arriving = [[lax.ppermute(chunk, "inst", [(i, (i + d) % peers) for i in range(peers)])
                     for d in range(1, peers)] for chunk in chunks]

    with jax.named_scope("ends"):
        up, down, cross = pl.pallas_call(
            ends_kernel,
            grid=(1,),
            out_shape=(jax.ShapeDtypeStruct((count, 2 * width, LAYER), bf16),
                       jax.ShapeDtypeStruct((count, 2 * width, LAYER), bf16),
                       jax.ShapeDtypeStruct((count, width, iface_rows), bf16)),
            in_specs=[smem,
                      whole(head),
                      pl.BlockSpec((count, dof, LANES), lambda j: (0, 0, total // LANES - 1)),
                      whole(trace_matrix)],
            out_specs=(pl.BlockSpec((count, 2 * width, LAYER), lambda j: (0, 0, 0)),
                       pl.BlockSpec((count, 2 * width, LAYER), lambda j: (0, 0, 0)),
                       pl.BlockSpec((count, width, iface_rows), lambda j: (0, 0, 0))),
            compiler_params=pltpu.CompilerParams(vmem_limit_bytes=VMEM_LIMIT),
            cost_estimate=pl.CostEstimate(flops=8 * width * dof * LANES * 2 * count,
                                          bytes_accessed=1_000_000, transcendentals=0),
            name="ends",
        )(place, head, current, trace_matrix)

    with jax.named_scope("halo"):
        low = lax.ppermute(up, "space", [(i, (i + 1) % shards) for i in range(shards)])
        high = lax.ppermute(down, "space", [(i, (i - 1) % shards) for i in range(shards)])
    with jax.named_scope("interface"):
        pieces = [lax.ppermute(cross, ("space", "row"),
                               [(i * 2 + r, (i + d) % shards * 2 + 1 - r) for i in range(shards) for r in range(2)])
                  for d in range(shards)]

    steps = total // tile
    by_tile = lambda *lead: pl.BlockSpec(lead + (tile,), lambda j: (0,) * len(lead) + (j,))
    with jax.named_scope("couple"):
        ready, factors = pl.pallas_call(
            functools.partial(couple_kernel, shards, peers),
            grid=(steps,),
            out_shape=(jax.ShapeDtypeStruct((count, dof, total), jnp.float32),
                       jax.ShapeDtypeStruct((count * count * (peers - 1), total), jnp.float32)),
            in_specs=[smem, smem, smem, by_tile(6), whole(partner_rows), whole(current), by_tile(count, dof),
                      by_tile(count, dof), by_tile(1), whole(trace_matrix), whole(lift_matrix),
                      whole(volume_matrix), whole(block_inverse), whole(low), whole(high)] + [whole(p) for p in pieces + arriving[0]],
            out_specs=(by_tile(count, dof), by_tile(count * count * (peers - 1))),
            scratch_shapes=[pltpu.VMEM((6, count * width, total), bf16)],
            compiler_params=pltpu.CompilerParams(vmem_limit_bytes=VMEM_LIMIT),
            cost_estimate=pl.CostEstimate(
                flops=COUPLE_FLOPS,
                bytes_accessed=count * dof * total * 10, transcendentals=0),
            name="couple",
        )(place, frequency, table, neighbours, partner_rows, current, current, forcing_local, metric_scale,
          trace_matrix, lift_matrix, volume_matrix, block_inverse, low, high, *pieces, *arriving[0])

    with jax.named_scope("update"):
        result = None
        for base, mine, others in ((0, bounds[1:2], arriving[1]), (bounds[2][0], bounds[2:], arriving[2])):
            more = [] if result is None else [result]
            span = mine[-1][1] - base
            result = pl.pallas_call(
                functools.partial(update_kernel, base, mine, peers, tile),
                out_shape=jax.ShapeDtypeStruct((count, dof, total), bf16),
                in_specs=[vmem] * (3 + len(others)) + [pl.BlockSpec(memory_space=pl.ANY)] * len(more),
                out_specs=pl.BlockSpec(memory_space=pl.ANY),
                scratch_shapes=[pltpu.VMEM((count, dof, span), bf16), pltpu.SemaphoreType.DMA((steps,))],
                input_output_aliases={3 + len(others): 0} if more else {},
                compiler_params=pltpu.CompilerParams(vmem_limit_bytes=VMEM_LIMIT),
                cost_estimate=pl.CostEstimate(flops=2 * count * span * dof * dof * (peers - 1),
                                              bytes_accessed=count * dof * span * 8, transcendentals=0),
                name="update",
            )(ready, factors, block_inverse, *others, *more)
    return result[None]


def solution(mesh):
    in_specs = (
        P("row", "inst", None, ("groups", "space")),
        P("row", "inst", None, ("groups", "space")),
        P("row", ("groups", "space")),
        P(),
        P("row", None, ("groups", "space")),
        P("row", "inst", ("groups", "space")),
        P(),
        P(),
        P(),
        P(),
    )
    out_specs = P("row", "inst", None, ("groups", "space"))
    return jax.shard_map(body, mesh=mesh, in_specs=in_specs, out_specs=out_specs, check_vma=False)
```

```python
import functools

import jax
import jax.numpy as jnp
import numpy as np
from jax import lax
from jax.experimental import pallas as pl
from jax.experimental.pallas import tpu as pltpu
from jax.sharding import PartitionSpec as P

LAYER = 64
OPPOSITE = (1, 0, 3, 2, 5, 4)
LANES = 128
VMEM_LIMIT = 40 * 1024 * 1024


def spectral_table(instances):
    positions = np.arange(instances)
    distance = positions[:, None] - positions[None, :]
    parity = np.where(distance % 2 == 0, 1.0, -1.0)
    angles = np.pi * distance / instances
    sines = np.where(distance == 0, 1.0, np.sin(angles))
    cotangent = np.where(distance == 0, 0.0, np.cos(angles) / sines)
    return (0.5 * parity * cotangent).astype(np.float32)


def one_hot(picked, rows):
    numbers = lax.broadcasted_iota(jnp.int32, (rows, picked.shape[1]), 0)
    return jnp.where(numbers == picked, 1.0, 0.0).astype(jnp.bfloat16)


def dot(left, right):
    return jnp.dot(left, right, preferred_element_type=jnp.float32)


def ends_kernel(place_ref, first_ref, last_ref, trace_ref, up_ref, down_ref, cross_ref):
    width = trace_ref.shape[0] // 6
    section = place_ref[0]
    for n in range(first_ref.shape[0]):
        first = dot(trace_ref[...], first_ref[n]).astype(jnp.bfloat16)
        last = dot(trace_ref[4 * width :, :], last_ref[n]).astype(jnp.bfloat16)
        down_ref[n] = first[4 * width :, :LAYER]
        up_ref[n] = last[:, last.shape[1] - LAYER :]
        rows = cross_ref.shape[2]
        cross_ref[n] = jnp.where(section == 0, first[width : 2 * width, :rows], first[:width, :rows])


def couple_kernel(shards, peers, place_ref, freq_ref, table_ref, adj_ref, partner_ref, all_ref, tile_ref, forcing_ref,
                  scale_ref, trace_ref, lift_ref, volume_ref, inverse_ref, low_ref, high_ref, *rest):
    pieces, (out_ref, factor_ref, traces) = rest[:shards], rest[shards:]
    step = pl.program_id(0)
    steps = pl.num_programs(0)
    count, dof, total = all_ref.shape
    width = trace_ref.shape[0] // 6
    tile = tile_ref.shape[2]
    section, inst, space = place_ref[0], place_ref[1], place_ref[2]

    @pl.when(step == 0)
    def _():
        for n in range(count):
            for c in range(total // tile):
                cols = slice(c * tile, (c + 1) * tile)
                made = dot(trace_ref[...], all_ref[n, :, cols]).astype(jnp.bfloat16)
                for f in range(6):
                    traces[f, n * width : (n + 1) * width, cols] = made[f * width : (f + 1) * width]

    column = lax.broadcasted_iota(jnp.int32, (1, tile), 1)
    at_edge = jnp.logical_or(step == 0, step == steps - 1)

    def gathered(edge):
        found = []
        for f in range(6):
            adj = adj_ref[f : f + 1, :]
            values = dot(traces[OPPOSITE[f]], one_hot(adj - LAYER, total))
            if edge and f >= 4:
                part = slice((5 - f) * width, (6 - f) * width)
                below = jnp.concatenate([low_ref[n, part, :] for n in range(count)], axis=0)
                above = jnp.concatenate([high_ref[n, part, :] for n in range(count)], axis=0)
                values += dot(below, one_hot(adj, LAYER))
                values += dot(above, one_hot(adj - (LAYER + total), LAYER))
            values = values.astype(jnp.bfloat16)
            if edge and f < 2:
                rows = partner_ref.shape[1]
                use = jnp.logical_and(step == 0, section == 1 - f)
                crossed = []
                for n in range(count):
                    wanted = partner_ref[n : n + 1, :]
                    arrived = jnp.zeros((width, rows), jnp.float32)
                    for d in range(shards):
                        source = lax.rem(space - d + shards, shards)
                        arrived += dot(pieces[d][n], one_hot(wanted - source * rows, rows))
                    crossed.append(arrived)
                crossed = jnp.concatenate(crossed, axis=0).astype(jnp.bfloat16)
                crossed = jnp.concatenate(
                    [crossed, jnp.zeros((count * width, tile - rows), jnp.bfloat16)], axis=1)
                take = jnp.logical_and(column < rows, use)
                values = jnp.where(take, crossed, values)
            found.append(values)
        return found

    def finish(edge):
        found = gathered(edge)
        frequency = freq_ref[0]
        scale = scale_ref[...]
        inverse_scale = 1.0 / scale
        for n in range(count):
            for d in range(1, peers):
                owner = lax.rem(inst - d + peers, peers)
                for m in range(count):
                    weight = table_ref[inst * count + n, owner * count + m] * frequency
                    at = (n * (peers - 1) + d - 1) * count + m
                    factor_ref[at : at + 1, :] = weight * inverse_scale
        for n in range(count):
            beside = jnp.concatenate([v[n * width : (n + 1) * width] for v in found], axis=0)
            inner = dot(lift_ref[...], beside) + dot(volume_ref[...], tile_ref[n])
            value = forcing_ref[n].astype(jnp.float32) - scale * inner
            for m in range(count):
                weight = table_ref[inst * count + n, inst * count + m] * frequency
                value -= weight * tile_ref[m].astype(jnp.float32)
            update = dot(inverse_ref[...], value.astype(jnp.bfloat16))
            out_ref[n] = tile_ref[n].astype(jnp.float32) + update * inverse_scale

    @pl.when(at_edge)
    def _():
        finish(True)

    @pl.when(jnp.logical_not(at_edge))
    def _():
        finish(False)


def update_kernel(tile, ready_ref, factor_ref, inverse_ref, *rest):
    others, (out_ref, made, sems) = rest[:-3], rest[-3:]
    count, dof, total = ready_ref.shape
    pieces = [(t, slice(0, dof)) for t in range(total // tile - 1)]
    pieces += [(total // tile - 1, slice(0, dof // 2)), (total // tile - 1, slice(dof // 2, dof))]
    copies = []
    for p, (t, rows) in enumerate(pieces):
        cols = slice(t * tile, (t + 1) * tile)
        moved = [dot(inverse_ref[rows, :], other[m, :, cols]) for other in others for m in range(count)]
        for n in range(count):
            value = ready_ref[n, rows, cols]
            for k, part in enumerate(moved):
                at = n * len(moved) + k
                value -= factor_ref[at : at + 1, cols] * part
            made[t, n, rows, :] = value.astype(jnp.bfloat16)
        copy = pltpu.make_async_copy(made.at[t, :, rows, :], out_ref.at[:, rows, cols], sems.at[p])
        copy.start()
        copies.append(copy)
    for copy in copies:
        copy.wait()


def whole(array):
    return pl.BlockSpec(array.shape, lambda j: (0,) * array.ndim)


def body(solution, forcing, metric_scale, frequency, adjacency, partner, volume_matrix, trace_matrix, lift_matrix,
         block_inverse):
    current = solution[0]
    forcing_local = forcing[0]
    neighbours = adjacency[0]
    partner_rows = partner[0]
    count, dof, total = current.shape
    width = trace_matrix.shape[0] // 6
    iface_rows = partner_rows.shape[1]
    shards = lax.axis_size("space")
    peers = lax.axis_size("inst")
    section = lax.axis_index("row")
    place = jnp.stack([section, lax.axis_index("inst"), lax.axis_index("space")]).astype(jnp.int32)
    table = jnp.asarray(spectral_table(count * peers))
    smem = pl.BlockSpec(memory_space=pltpu.SMEM)
    bf16 = jnp.bfloat16

    with jax.named_scope("instances"):
        others = [lax.ppermute(current, "inst", [(i, (i + d) % peers) for i in range(peers)])
                  for d in range(1, peers)]

    with jax.named_scope("ends"):
        up, down, cross = pl.pallas_call(
            ends_kernel,
            grid=(1,),
            out_shape=(jax.ShapeDtypeStruct((count, 2 * width, LAYER), bf16),
                       jax.ShapeDtypeStruct((count, 2 * width, LAYER), bf16),
                       jax.ShapeDtypeStruct((count, width, iface_rows), bf16)),
            in_specs=[smem,
                      pl.BlockSpec((count, dof, LANES), lambda j: (0, 0, 0)),
                      pl.BlockSpec((count, dof, LANES), lambda j: (0, 0, total // LANES - 1)),
                      whole(trace_matrix)],
            out_specs=(pl.BlockSpec((count, 2 * width, LAYER), lambda j: (0, 0, 0)),
                       pl.BlockSpec((count, 2 * width, LAYER), lambda j: (0, 0, 0)),
                       pl.BlockSpec((count, width, iface_rows), lambda j: (0, 0, 0))),
            compiler_params=pltpu.CompilerParams(vmem_limit_bytes=VMEM_LIMIT),
            cost_estimate=pl.CostEstimate(flops=8 * width * dof * LANES * 2 * count,
                                          bytes_accessed=1_000_000, transcendentals=0),
            name="ends",
        )(place, current, current, trace_matrix)

    with jax.named_scope("halo"):
        low = lax.ppermute(up, "space", [(i, (i + 1) % shards) for i in range(shards)])
        high = lax.ppermute(down, "space", [(i, (i - 1) % shards) for i in range(shards)])
    with jax.named_scope("interface"):
        pieces = [lax.ppermute(cross, ("space", "row"),
                               [(i * 2 + r, (i + d) % shards * 2 + 1 - r) for i in range(shards) for r in range(2)])
                  for d in range(shards)]

    tile = 256
    steps = total // tile
    by_tile = lambda *lead: pl.BlockSpec(lead + (tile,), lambda j: (0,) * len(lead) + (j,))
    with jax.named_scope("couple"):
        ready, factors = pl.pallas_call(
            functools.partial(couple_kernel, shards, peers),
            grid=(steps,),
            out_shape=(jax.ShapeDtypeStruct((count, dof, total), jnp.float32),
                       jax.ShapeDtypeStruct((count * count * (peers - 1), total), jnp.float32)),
            in_specs=[smem, smem, smem, by_tile(6), whole(partner_rows), whole(current), by_tile(count, dof),
                      by_tile(count, dof), by_tile(1), whole(trace_matrix), whole(lift_matrix),
                      whole(volume_matrix), whole(block_inverse), whole(low), whole(high)] + [whole(p) for p in pieces],
            out_specs=(by_tile(count, dof), by_tile(count * count * (peers - 1))),
            scratch_shapes=[pltpu.VMEM((6, count * width, total), bf16)],
            compiler_params=pltpu.CompilerParams(vmem_limit_bytes=VMEM_LIMIT),
            cost_estimate=pl.CostEstimate(
                flops=2 * count * total * (6 * width * dof * 2 + dof * dof + 6 * width * total),
                bytes_accessed=count * dof * total * 10, transcendentals=0),
            name="couple",
        )(place, frequency, table, neighbours, partner_rows, current, current, forcing_local, metric_scale,
          trace_matrix, lift_matrix, volume_matrix, block_inverse, low, high, *pieces)

    vmem = pl.BlockSpec(memory_space=pltpu.VMEM)
    with jax.named_scope("update"):
        result = pl.pallas_call(
            functools.partial(update_kernel, tile),
            out_shape=jax.ShapeDtypeStruct((count, dof, total), bf16),
            in_specs=[vmem] * (2 + peers),
            out_specs=pl.BlockSpec(memory_space=pl.ANY),
            scratch_shapes=[pltpu.VMEM((steps, count, dof, tile), bf16), pltpu.SemaphoreType.DMA((steps + 1,))],
            compiler_params=pltpu.CompilerParams(vmem_limit_bytes=VMEM_LIMIT),
            cost_estimate=pl.CostEstimate(flops=2 * count * total * dof * dof * (peers - 1),
                                          bytes_accessed=count * dof * total * 8, transcendentals=0),
            name="update",
        )(ready, factors, block_inverse, *others)
    return result[None]


def solution(mesh):
    in_specs = (
        P("row", "inst", None, ("groups", "space")),
        P("row", "inst", None, ("groups", "space")),
        P("row", ("groups", "space")),
        P(),
        P("row", None, ("groups", "space")),
        P("row", "inst", ("groups", "space")),
        P(),
        P(),
        P(),
        P(),
    )
    out_specs = P("row", "inst", None, ("groups", "space"))
    return jax.shard_map(body, mesh=mesh, in_specs=in_specs, out_specs=out_specs, check_vma=False)
```

```python
import functools

import jax
import jax.numpy as jnp
import numpy as np
from jax import lax
from jax.experimental import pallas as pl
from jax.experimental.pallas import tpu as pltpu
from jax.sharding import PartitionSpec as P

LAYER = 64
OPPOSITE = (1, 0, 3, 2, 5, 4)
LANES = 128
VMEM_LIMIT = 40 * 1024 * 1024


def spectral_table(instances):
    positions = np.arange(instances)
    distance = positions[:, None] - positions[None, :]
    parity = np.where(distance % 2 == 0, 1.0, -1.0)
    angles = np.pi * distance / instances
    sines = np.where(distance == 0, 1.0, np.sin(angles))
    cotangent = np.where(distance == 0, 0.0, np.cos(angles) / sines)
    return (0.5 * parity * cotangent).astype(np.float32)


def one_hot(picked, rows):
    numbers = lax.broadcasted_iota(jnp.int32, (rows, picked.shape[1]), 0)
    return jnp.where(numbers == picked, 1.0, 0.0).astype(jnp.bfloat16)


def dot(left, right):
    return jnp.dot(left, right, preferred_element_type=jnp.float32)


def ends_kernel(place_ref, first_ref, last_ref, trace_ref, up_ref, down_ref, cross_ref):
    width = trace_ref.shape[0] // 6
    section = place_ref[0]
    for n in range(first_ref.shape[0]):
        first = dot(trace_ref[...], first_ref[n]).astype(jnp.bfloat16)
        last = dot(trace_ref[4 * width :, :], last_ref[n]).astype(jnp.bfloat16)
        down_ref[n] = first[4 * width :, :LAYER]
        up_ref[n] = last[:, last.shape[1] - LAYER :]
        rows = cross_ref.shape[2]
        cross_ref[n] = jnp.where(section == 0, first[width : 2 * width, :rows], first[:width, :rows])


def couple_kernel(shards, peers, deep, place_ref, freq_ref, table_ref, adj_ref, partner_ref, all_ref, tile_ref, forcing_ref,
                  scale_ref, trace_ref, lift_ref, volume_ref, inverse_ref, low_ref, high_ref, *rest):
    pieces, (out_ref, factor_ref, spread_ref, traces) = rest[:shards], rest[shards:]
    step = pl.program_id(0)
    steps = pl.num_programs(0)
    count, dof, total = all_ref.shape
    width = trace_ref.shape[0] // 6
    tile = tile_ref.shape[2]
    section, inst, space = place_ref[0], place_ref[1], place_ref[2]

    @pl.when(step == 0)
    def _():
        for n in range(count):
            for c in range(total // tile):
                cols = slice(c * tile, (c + 1) * tile)
                made = dot(trace_ref[...], all_ref[n, :, cols]).astype(jnp.bfloat16)
                for f in range(6):
                    traces[f, n * width : (n + 1) * width, cols] = made[f * width : (f + 1) * width]

        left = dof - deep
        spread_ref[...] = jnp.zeros_like(spread_ref)
        for m in range(count):
            spread_ref[m, :, m * left : (m + 1) * left] = inverse_ref[:, deep:]

    column = lax.broadcasted_iota(jnp.int32, (1, tile), 1)
    at_edge = jnp.logical_or(step == 0, step == steps - 1)

    def gathered(edge):
        found = []
        for f in range(6):
            adj = adj_ref[f : f + 1, :]
            values = dot(traces[OPPOSITE[f]], one_hot(adj - LAYER, total))
            if edge and f >= 4:
                part = slice((5 - f) * width, (6 - f) * width)
                below = jnp.concatenate([low_ref[n, part, :] for n in range(count)], axis=0)
                above = jnp.concatenate([high_ref[n, part, :] for n in range(count)], axis=0)
                values += dot(below, one_hot(adj, LAYER))
                values += dot(above, one_hot(adj - (LAYER + total), LAYER))
            values = values.astype(jnp.bfloat16)
            if edge and f < 2:
                rows = partner_ref.shape[1]
                use = jnp.logical_and(step == 0, section == 1 - f)
                crossed = []
                for n in range(count):
                    wanted = partner_ref[n : n + 1, :]
                    arrived = jnp.zeros((width, rows), jnp.float32)
                    for d in range(shards):
                        source = lax.rem(space - d + shards, shards)
                        arrived += dot(pieces[d][n], one_hot(wanted - source * rows, rows))
                    crossed.append(arrived)
                crossed = jnp.concatenate(crossed, axis=0).astype(jnp.bfloat16)
                crossed = jnp.concatenate(
                    [crossed, jnp.zeros((count * width, tile - rows), jnp.bfloat16)], axis=1)
                take = jnp.logical_and(column < rows, use)
                values = jnp.where(take, crossed, values)
            found.append(values)
        return found

    def finish(edge):
        found = gathered(edge)
        frequency = freq_ref[0]
        scale = scale_ref[...]
        inverse_scale = 1.0 / scale
        for n in range(count):
            for d in range(1, peers):
                owner = lax.rem(inst - d + peers, peers)
                for m in range(count):
                    weight = table_ref[inst * count + n, owner * count + m] * frequency
                    at = (n * (peers - 1) + d - 1) * count + m
                    factor_ref[at : at + 1, :] = weight * inverse_scale
        for n in range(count):
            beside = jnp.concatenate([v[n * width : (n + 1) * width] for v in found], axis=0)
            inner = dot(lift_ref[...], beside) + dot(volume_ref[...], tile_ref[n])
            value = forcing_ref[n].astype(jnp.float32) - scale * inner
            for m in range(count):
                weight = table_ref[inst * count + n, inst * count + m] * frequency
                value -= weight * tile_ref[m].astype(jnp.float32)
            update = dot(inverse_ref[...], value.astype(jnp.bfloat16))
            out_ref[n] = tile_ref[n].astype(jnp.float32) + update * inverse_scale

    @pl.when(at_edge)
    def _():
        finish(True)

    @pl.when(jnp.logical_not(at_edge))
    def _():
        finish(False)


def update_kernel(tile, deep, ready_ref, factor_ref, inverse_ref, spread_ref, *rest):
    others, (out_ref, made, sems) = rest[:-3], rest[-3:]
    count, dof, total = ready_ref.shape
    copies = []
    for t in range(total // tile):
        cols = slice(t * tile, (t + 1) * tile)
        moved = []
        for other in others:
            stack = jnp.concatenate([other[m, deep:, cols] for m in range(count)], axis=0)
            for m in range(count):
                moved.append(dot(inverse_ref[:, :deep], other[m, :deep, cols]) + dot(spread_ref[m], stack))
        for n in range(count):
            value = ready_ref[n, :, cols]
            for k, part in enumerate(moved):
                at = n * len(moved) + k
                value -= factor_ref[at : at + 1, cols] * part
            made[t, n] = value.astype(jnp.bfloat16)
        copy = pltpu.make_async_copy(made.at[t], out_ref.at[:, :, cols], sems.at[t])
        copy.start()
        copies.append(copy)
    for copy in copies:
        copy.wait()


def whole(array):
    return pl.BlockSpec(array.shape, lambda j: (0,) * array.ndim)


def body(solution, forcing, metric_scale, frequency, adjacency, partner, volume_matrix, trace_matrix, lift_matrix,
         block_inverse):
    current = solution[0]
    forcing_local = forcing[0]
    neighbours = adjacency[0]
    partner_rows = partner[0]
    count, dof, total = current.shape
    width = trace_matrix.shape[0] // 6
    iface_rows = partner_rows.shape[1]
    shards = lax.axis_size("space")
    peers = lax.axis_size("inst")
    section = lax.axis_index("row")
    place = jnp.stack([section, lax.axis_index("inst"), lax.axis_index("space")]).astype(jnp.int32)
    table = jnp.asarray(spectral_table(count * peers))
    smem = pl.BlockSpec(memory_space=pltpu.SMEM)
    bf16 = jnp.bfloat16

    with jax.named_scope("instances"):
        others = [lax.ppermute(current, "inst", [(i, (i + d) % peers) for i in range(peers)])
                  for d in range(1, peers)]

    with jax.named_scope("ends"):
        up, down, cross = pl.pallas_call(
            ends_kernel,
            grid=(1,),
            out_shape=(jax.ShapeDtypeStruct((count, 2 * width, LAYER), bf16),
                       jax.ShapeDtypeStruct((count, 2 * width, LAYER), bf16),
                       jax.ShapeDtypeStruct((count, width, iface_rows), bf16)),
            in_specs=[smem,
                      pl.BlockSpec((count, dof, LANES), lambda j: (0, 0, 0)),
                      pl.BlockSpec((count, dof, LANES), lambda j: (0, 0, total // LANES - 1)),
                      whole(trace_matrix)],
            out_specs=(pl.BlockSpec((count, 2 * width, LAYER), lambda j: (0, 0, 0)),
                       pl.BlockSpec((count, 2 * width, LAYER), lambda j: (0, 0, 0)),
                       pl.BlockSpec((count, width, iface_rows), lambda j: (0, 0, 0))),
            compiler_params=pltpu.CompilerParams(vmem_limit_bytes=VMEM_LIMIT),
            cost_estimate=pl.CostEstimate(flops=8 * width * dof * LANES * 2 * count,
                                          bytes_accessed=1_000_000, transcendentals=0),
            name="ends",
        )(place, current, current, trace_matrix)

    with jax.named_scope("halo"):
        low = lax.ppermute(up, "space", [(i, (i + 1) % shards) for i in range(shards)])
        high = lax.ppermute(down, "space", [(i, (i - 1) % shards) for i in range(shards)])
    with jax.named_scope("interface"):
        pieces = [lax.ppermute(cross, ("space", "row"),
                               [(i * 2 + r, (i + d) % shards * 2 + 1 - r) for i in range(shards) for r in range(2)])
                  for d in range(shards)]

    tile = 256
    steps = total // tile
    deep = dof // tile * tile
    by_tile = lambda *lead: pl.BlockSpec(lead + (tile,), lambda j: (0,) * len(lead) + (j,))
    with jax.named_scope("couple"):
        ready, factors, spread = pl.pallas_call(
            functools.partial(couple_kernel, shards, peers, deep),
            grid=(steps,),
            out_shape=(jax.ShapeDtypeStruct((count, dof, total), jnp.float32),
                       jax.ShapeDtypeStruct((count * count * (peers - 1), total), jnp.float32),
                       jax.ShapeDtypeStruct((count, dof, count * (dof - deep)), bf16)),
            in_specs=[smem, smem, smem, by_tile(6), whole(partner_rows), whole(current), by_tile(count, dof),
                      by_tile(count, dof), by_tile(1), whole(trace_matrix), whole(lift_matrix),
                      whole(volume_matrix), whole(block_inverse), whole(low), whole(high)] + [whole(p) for p in pieces],
            out_specs=(by_tile(count, dof), by_tile(count * count * (peers - 1)),
                       pl.BlockSpec((count, dof, count * (dof - deep)), lambda j: (0, 0, 0))),
            scratch_shapes=[pltpu.VMEM((6, count * width, total), bf16)],
            compiler_params=pltpu.CompilerParams(vmem_limit_bytes=VMEM_LIMIT),
            cost_estimate=pl.CostEstimate(
                flops=2 * count * total * (6 * width * dof * 2 + dof * dof + 6 * width * total),
                bytes_accessed=count * dof * total * 10, transcendentals=0),
            name="couple",
        )(place, frequency, table, neighbours, partner_rows, current, current, forcing_local, metric_scale,
          trace_matrix, lift_matrix, volume_matrix, block_inverse, low, high, *pieces)

    vmem = pl.BlockSpec(memory_space=pltpu.VMEM)
    with jax.named_scope("update"):
        result = pl.pallas_call(
            functools.partial(update_kernel, tile, deep),
            out_shape=jax.ShapeDtypeStruct((count, dof, total), bf16),
            in_specs=[vmem] * (3 + peers),
            out_specs=pl.BlockSpec(memory_space=pl.ANY),
            scratch_shapes=[pltpu.VMEM((steps, count, dof, tile), bf16), pltpu.SemaphoreType.DMA((steps,))],
            compiler_params=pltpu.CompilerParams(vmem_limit_bytes=VMEM_LIMIT),
            cost_estimate=pl.CostEstimate(flops=2 * count * total * dof * dof * (peers - 1),
                                          bytes_accessed=count * dof * total * 8, transcendentals=0),
            name="update",
        )(ready, factors, block_inverse, spread, *others)
    return result[None]


def solution(mesh):
    in_specs = (
        P("row", "inst", None, ("groups", "space")),
        P("row", "inst", None, ("groups", "space")),
        P("row", ("groups", "space")),
        P(),
        P("row", None, ("groups", "space")),
        P("row", "inst", ("groups", "space")),
        P(),
        P(),
        P(),
        P(),
    )
    out_specs = P("row", "inst", None, ("groups", "space"))
    return jax.shard_map(body, mesh=mesh, in_specs=in_specs, out_specs=out_specs, check_vma=False)
```

```python
import functools

import jax
import jax.numpy as jnp
import numpy as np
from jax import lax
from jax.experimental import pallas as pl
from jax.experimental.pallas import tpu as pltpu
from jax.sharding import PartitionSpec as P

LAYER = 64
OPPOSITE = (1, 0, 3, 2, 5, 4)
LANES = 128
VMEM_LIMIT = 40 * 1024 * 1024


def spectral_table(instances):
    positions = np.arange(instances)
    distance = positions[:, None] - positions[None, :]
    parity = np.where(distance % 2 == 0, 1.0, -1.0)
    angles = np.pi * distance / instances
    sines = np.where(distance == 0, 1.0, np.sin(angles))
    cotangent = np.where(distance == 0, 0.0, np.cos(angles) / sines)
    return (0.5 * parity * cotangent).astype(np.float32)


def one_hot(picked, rows):
    numbers = lax.broadcasted_iota(jnp.int32, (rows, picked.shape[1]), 0)
    return jnp.where(numbers == picked, 1.0, 0.0).astype(jnp.bfloat16)


def dot(left, right):
    return jnp.dot(left, right, preferred_element_type=jnp.float32)


def ends_kernel(place_ref, first_ref, last_ref, trace_ref, up_ref, down_ref, cross_ref):
    width = trace_ref.shape[0] // 6
    section = place_ref[0]
    for n in range(first_ref.shape[0]):
        first = dot(trace_ref[...], first_ref[n]).astype(jnp.bfloat16)
        last = dot(trace_ref[4 * width :, :], last_ref[n]).astype(jnp.bfloat16)
        down_ref[n] = first[4 * width :, :LAYER]
        up_ref[n] = last[:, last.shape[1] - LAYER :]
        rows = cross_ref.shape[2]
        cross_ref[n] = jnp.where(section == 0, first[width : 2 * width, :rows], first[:width, :rows])


def couple_kernel(shards, peers, deep, place_ref, freq_ref, table_ref, adj_ref, partner_ref, all_ref, tile_ref, forcing_ref,
                  scale_ref, trace_ref, lift_ref, volume_ref, inverse_ref, low_ref, high_ref, *rest):
    pieces, (out_ref, factor_ref, spread_ref, traces) = rest[:shards], rest[shards:]
    step = pl.program_id(0)
    steps = pl.num_programs(0)
    count, dof, total = all_ref.shape
    width = trace_ref.shape[0] // 6
    tile = tile_ref.shape[2]
    section, inst, space = place_ref[0], place_ref[1], place_ref[2]

    @pl.when(step == 0)
    def _():
        for n in range(count):
            for c in range(total // tile):
                cols = slice(c * tile, (c + 1) * tile)
                made = dot(trace_ref[...], all_ref[n, :, cols]).astype(jnp.bfloat16)
                for f in range(6):
                    traces[f, n * width : (n + 1) * width, cols] = made[f * width : (f + 1) * width]

        left = dof - deep
        spread_ref[...] = jnp.zeros_like(spread_ref)
        for m in range(count):
            spread_ref[m, :, m * left : (m + 1) * left] = inverse_ref[:, deep:]

    column = lax.broadcasted_iota(jnp.int32, (1, tile), 1)
    at_edge = jnp.logical_or(step == 0, step == steps - 1)

    def gathered(edge):
        found = []
        for f in range(6):
            adj = adj_ref[f : f + 1, :]
            values = dot(traces[OPPOSITE[f]], one_hot(adj - LAYER, total))
            if edge and f >= 4:
                part = slice((5 - f) * width, (6 - f) * width)
                below = jnp.concatenate([low_ref[n, part, :] for n in range(count)], axis=0)
                above = jnp.concatenate([high_ref[n, part, :] for n in range(count)], axis=0)
                values += dot(below, one_hot(adj, LAYER))
                values += dot(above, one_hot(adj - (LAYER + total), LAYER))
            values = values.astype(jnp.bfloat16)
            if edge and f < 2:
                rows = partner_ref.shape[1]
                use = jnp.logical_and(step == 0, section == 1 - f)
                crossed = []
                for n in range(count):
                    wanted = partner_ref[n : n + 1, :]
                    arrived = jnp.zeros((width, rows), jnp.float32)
                    for d in range(shards):
                        source = lax.rem(space - d + shards, shards)
                        arrived += dot(pieces[d][n], one_hot(wanted - source * rows, rows))
                    crossed.append(arrived)
                crossed = jnp.concatenate(crossed, axis=0).astype(jnp.bfloat16)
                crossed = jnp.concatenate(
                    [crossed, jnp.zeros((count * width, tile - rows), jnp.bfloat16)], axis=1)
                take = jnp.logical_and(column < rows, use)
                values = jnp.where(take, crossed, values)
            found.append(values)
        return found

    def finish(edge):
        found = gathered(edge)
        frequency = freq_ref[0]
        scale = scale_ref[...]
        inverse_scale = 1.0 / scale
        for n in range(count):
            for d in range(1, peers):
                owner = lax.rem(inst - d + peers, peers)
                for m in range(count):
                    weight = table_ref[inst * count + n, owner * count + m] * frequency
                    at = (n * (peers - 1) + d - 1) * count + m
                    factor_ref[at : at + 1, :] = weight * inverse_scale
        for n in range(count):
            beside = jnp.concatenate([v[n * width : (n + 1) * width] for v in found], axis=0)
            inner = dot(lift_ref[...], beside) + dot(volume_ref[...], tile_ref[n])
            value = forcing_ref[n].astype(jnp.float32) - scale * inner
            for m in range(count):
                weight = table_ref[inst * count + n, inst * count + m] * frequency
                value -= weight * tile_ref[m].astype(jnp.float32)
            update = dot(inverse_ref[...], value.astype(jnp.bfloat16))
            out_ref[n] = tile_ref[n].astype(jnp.float32) + update * inverse_scale

    @pl.when(at_edge)
    def _():
        finish(True)

    @pl.when(jnp.logical_not(at_edge))
    def _():
        finish(False)


def update_kernel(tile, deep, ready_ref, factor_ref, inverse_ref, spread_ref, *rest):
    others, (out_ref, made, sems) = rest[:-3], rest[-3:]
    count, dof, total = ready_ref.shape
    pieces = [(0, slice(0, dof // 2)), (0, slice(dof // 2, dof))]
    pieces += [(t, slice(0, dof)) for t in range(1, total // tile)]
    copies = []
    for p, (t, rows) in enumerate(pieces):
        cols = slice(t * tile, (t + 1) * tile)
        moved = []
        for other in others:
            stack = jnp.concatenate([other[m, deep:, cols] for m in range(count)], axis=0)
            for m in range(count):
                moved.append(dot(inverse_ref[rows, :deep], other[m, :deep, cols]) + dot(spread_ref[m, rows, :], stack))
        for n in range(count):
            value = ready_ref[n, rows, cols]
            for k, part in enumerate(moved):
                at = n * len(moved) + k
                value -= factor_ref[at : at + 1, cols] * part
            made[t, n, rows, :] = value.astype(jnp.bfloat16)
        copy = pltpu.make_async_copy(made.at[t, :, rows, :], out_ref.at[:, rows, cols], sems.at[p])
        copy.start()
        copies.append(copy)
    for copy in copies:
        copy.wait()


def whole(array):
    return pl.BlockSpec(array.shape, lambda j: (0,) * array.ndim)


def body(solution, forcing, metric_scale, frequency, adjacency, partner, volume_matrix, trace_matrix, lift_matrix,
         block_inverse):
    current = solution[0]
    forcing_local = forcing[0]
    neighbours = adjacency[0]
    partner_rows = partner[0]
    count, dof, total = current.shape
    width = trace_matrix.shape[0] // 6
    iface_rows = partner_rows.shape[1]
    shards = lax.axis_size("space")
    peers = lax.axis_size("inst")
    section = lax.axis_index("row")
    place = jnp.stack([section, lax.axis_index("inst"), lax.axis_index("space")]).astype(jnp.int32)
    table = jnp.asarray(spectral_table(count * peers))
    smem = pl.BlockSpec(memory_space=pltpu.SMEM)
    bf16 = jnp.bfloat16

    with jax.named_scope("instances"):
        others = [lax.ppermute(current, "inst", [(i, (i + d) % peers) for i in range(peers)])
                  for d in range(1, peers)]

    with jax.named_scope("ends"):
        up, down, cross = pl.pallas_call(
            ends_kernel,
            grid=(1,),
            out_shape=(jax.ShapeDtypeStruct((count, 2 * width, LAYER), bf16),
                       jax.ShapeDtypeStruct((count, 2 * width, LAYER), bf16),
                       jax.ShapeDtypeStruct((count, width, iface_rows), bf16)),
            in_specs=[smem,
                      pl.BlockSpec((count, dof, LANES), lambda j: (0, 0, 0)),
                      pl.BlockSpec((count, dof, LANES), lambda j: (0, 0, total // LANES - 1)),
                      whole(trace_matrix)],
            out_specs=(pl.BlockSpec((count, 2 * width, LAYER), lambda j: (0, 0, 0)),
                       pl.BlockSpec((count, 2 * width, LAYER), lambda j: (0, 0, 0)),
                       pl.BlockSpec((count, width, iface_rows), lambda j: (0, 0, 0))),
            compiler_params=pltpu.CompilerParams(vmem_limit_bytes=VMEM_LIMIT),
            cost_estimate=pl.CostEstimate(flops=8 * width * dof * LANES * 2 * count,
                                          bytes_accessed=1_000_000, transcendentals=0),
            name="ends",
        )(place, current, current, trace_matrix)

    with jax.named_scope("halo"):
        low = lax.ppermute(up, "space", [(i, (i + 1) % shards) for i in range(shards)])
        high = lax.ppermute(down, "space", [(i, (i - 1) % shards) for i in range(shards)])
    with jax.named_scope("interface"):
        pieces = [lax.ppermute(cross, ("space", "row"),
                               [(i * 2 + r, (i + d) % shards * 2 + 1 - r) for i in range(shards) for r in range(2)])
                  for d in range(shards)]

    tile = 256
    steps = total // tile
    deep = dof // tile * tile
    by_tile = lambda *lead: pl.BlockSpec(lead + (tile,), lambda j: (0,) * len(lead) + (j,))
    with jax.named_scope("couple"):
        ready, factors, spread = pl.pallas_call(
            functools.partial(couple_kernel, shards, peers, deep),
            grid=(steps,),
            out_shape=(jax.ShapeDtypeStruct((count, dof, total), jnp.float32),
                       jax.ShapeDtypeStruct((count * count * (peers - 1), total), jnp.float32),
                       jax.ShapeDtypeStruct((count, dof, count * (dof - deep)), bf16)),
            in_specs=[smem, smem, smem, by_tile(6), whole(partner_rows), whole(current), by_tile(count, dof),
                      by_tile(count, dof), by_tile(1), whole(trace_matrix), whole(lift_matrix),
                      whole(volume_matrix), whole(block_inverse), whole(low), whole(high)] + [whole(p) for p in pieces],
            out_specs=(by_tile(count, dof), by_tile(count * count * (peers - 1)),
                       pl.BlockSpec((count, dof, count * (dof - deep)), lambda j: (0, 0, 0))),
            scratch_shapes=[pltpu.VMEM((6, count * width, total), bf16)],
            compiler_params=pltpu.CompilerParams(vmem_limit_bytes=VMEM_LIMIT),
            cost_estimate=pl.CostEstimate(
                flops=2 * count * total * (6 * width * dof * 2 + dof * dof + 6 * width * total),
                bytes_accessed=count * dof * total * 10, transcendentals=0),
            name="couple",
        )(place, frequency, table, neighbours, partner_rows, current, current, forcing_local, metric_scale,
          trace_matrix, lift_matrix, volume_matrix, block_inverse, low, high, *pieces)

    vmem = pl.BlockSpec(memory_space=pltpu.VMEM)
    with jax.named_scope("update"):
        result = pl.pallas_call(
            functools.partial(update_kernel, tile, deep),
            out_shape=jax.ShapeDtypeStruct((count, dof, total), bf16),
            in_specs=[vmem] * (3 + peers),
            out_specs=pl.BlockSpec(memory_space=pl.ANY),
            scratch_shapes=[pltpu.VMEM((steps, count, dof, tile), bf16), pltpu.SemaphoreType.DMA((steps + 1,))],
            compiler_params=pltpu.CompilerParams(vmem_limit_bytes=VMEM_LIMIT),
            cost_estimate=pl.CostEstimate(flops=2 * count * total * dof * dof * (peers - 1),
                                          bytes_accessed=count * dof * total * 8, transcendentals=0),
            name="update",
        )(ready, factors, block_inverse, spread, *others)
    return result[None]


def solution(mesh):
    in_specs = (
        P("row", "inst", None, ("groups", "space")),
        P("row", "inst", None, ("groups", "space")),
        P("row", ("groups", "space")),
        P(),
        P("row", None, ("groups", "space")),
        P("row", "inst", ("groups", "space")),
        P(),
        P(),
        P(),
        P(),
    )
    out_specs = P("row", "inst", None, ("groups", "space"))
    return jax.shard_map(body, mesh=mesh, in_specs=in_specs, out_specs=out_specs, check_vma=False)
```

```python
import functools

import jax
import jax.numpy as jnp
import numpy as np
from jax import lax
from jax.experimental import pallas as pl
from jax.experimental.pallas import tpu as pltpu
from jax.sharding import PartitionSpec as P

LAYER = 64
OPPOSITE = (1, 0, 3, 2, 5, 4)
LANES = 128
VMEM_LIMIT = 40 * 1024 * 1024


def spectral_table(instances):
    positions = np.arange(instances)
    distance = positions[:, None] - positions[None, :]
    parity = np.where(distance % 2 == 0, 1.0, -1.0)
    angles = np.pi * distance / instances
    sines = np.where(distance == 0, 1.0, np.sin(angles))
    cotangent = np.where(distance == 0, 0.0, np.cos(angles) / sines)
    return (0.5 * parity * cotangent).astype(np.float32)


def one_hot(picked, rows):
    numbers = lax.broadcasted_iota(jnp.int32, (rows, picked.shape[1]), 0)
    return jnp.where(numbers == picked, 1.0, 0.0).astype(jnp.bfloat16)


def dot(left, right):
    return jnp.dot(left, right, preferred_element_type=jnp.float32)


def ends_kernel(place_ref, first_ref, last_ref, trace_ref, up_ref, down_ref, cross_ref):
    width = trace_ref.shape[0] // 6
    section = place_ref[0]
    for n in range(first_ref.shape[0]):
        first = dot(trace_ref[...], first_ref[n]).astype(jnp.bfloat16)
        last = dot(trace_ref[4 * width :, :], last_ref[n]).astype(jnp.bfloat16)
        down_ref[n] = first[4 * width :, :LAYER]
        up_ref[n] = last[:, last.shape[1] - LAYER :]
        rows = cross_ref.shape[2]
        cross_ref[n] = jnp.where(section == 0, first[width : 2 * width, :rows], first[:width, :rows])


def couple_kernel(shards, peers, deep, place_ref, freq_ref, table_ref, adj_ref, partner_ref, all_ref, tile_ref, forcing_ref,
                  scale_ref, trace_ref, lift_ref, volume_ref, inverse_ref, low_ref, high_ref, *rest):
    pieces, (out_ref, factor_ref, spread_ref, traces) = rest[:shards], rest[shards:]
    step = pl.program_id(0)
    steps = pl.num_programs(0)
    count, dof, total = all_ref.shape
    width = trace_ref.shape[0] // 6
    tile = tile_ref.shape[2]
    section, inst, space = place_ref[0], place_ref[1], place_ref[2]

    @pl.when(step == 0)
    def _():
        for n in range(count):
            for c in range(total // tile):
                cols = slice(c * tile, (c + 1) * tile)
                made = dot(trace_ref[...], all_ref[n, :, cols]).astype(jnp.bfloat16)
                for f in range(6):
                    traces[f, n * width : (n + 1) * width, cols] = made[f * width : (f + 1) * width]

        left = dof - deep
        spread_ref[...] = jnp.zeros_like(spread_ref)
        for m in range(count):
            spread_ref[m, :, m * left : (m + 1) * left] = inverse_ref[:, deep:]

    column = lax.broadcasted_iota(jnp.int32, (1, tile), 1)
    at_edge = jnp.logical_or(step == 0, step == steps - 1)

    def gathered(edge):
        found = []
        for f in range(6):
            adj = adj_ref[f : f + 1, :]
            values = dot(traces[OPPOSITE[f]], one_hot(adj - LAYER, total))
            if edge and f >= 4:
                part = slice((5 - f) * width, (6 - f) * width)
                below = jnp.concatenate([low_ref[n, part, :] for n in range(count)], axis=0)
                above = jnp.concatenate([high_ref[n, part, :] for n in range(count)], axis=0)
                values += dot(below, one_hot(adj, LAYER))
                values += dot(above, one_hot(adj - (LAYER + total), LAYER))
            values = values.astype(jnp.bfloat16)
            if edge and f < 2:
                rows = partner_ref.shape[1]
                use = jnp.logical_and(step == 0, section == 1 - f)
                crossed = []
                for n in range(count):
                    wanted = partner_ref[n : n + 1, :]
                    arrived = jnp.zeros((width, rows), jnp.float32)
                    for d in range(shards):
                        source = lax.rem(space - d + shards, shards)
                        arrived += dot(pieces[d][n], one_hot(wanted - source * rows, rows))
                    crossed.append(arrived)
                crossed = jnp.concatenate(crossed, axis=0).astype(jnp.bfloat16)
                crossed = jnp.concatenate(
                    [crossed, jnp.zeros((count * width, tile - rows), jnp.bfloat16)], axis=1)
                take = jnp.logical_and(column < rows, use)
                values = jnp.where(take, crossed, values)
            found.append(values)
        return found

    def finish(edge):
        found = gathered(edge)
        frequency = freq_ref[0]
        scale = scale_ref[...]
        inverse_scale = 1.0 / scale
        for n in range(count):
            for d in range(1, peers):
                owner = lax.rem(inst - d + peers, peers)
                for m in range(count):
                    weight = table_ref[inst * count + n, owner * count + m] * frequency
                    at = (n * (peers - 1) + d - 1) * count + m
                    factor_ref[at : at + 1, :] = weight * inverse_scale
        for n in range(count):
            beside = jnp.concatenate([v[n * width : (n + 1) * width] for v in found], axis=0)
            inner = dot(lift_ref[...], beside) + dot(volume_ref[...], tile_ref[n])
            value = forcing_ref[n].astype(jnp.float32) - scale * inner
            for m in range(count):
                weight = table_ref[inst * count + n, inst * count + m] * frequency
                value -= weight * tile_ref[m].astype(jnp.float32)
            update = dot(inverse_ref[...], value.astype(jnp.bfloat16))
            out_ref[n] = tile_ref[n].astype(jnp.float32) + update * inverse_scale

    @pl.when(at_edge)
    def _():
        finish(True)

    @pl.when(jnp.logical_not(at_edge))
    def _():
        finish(False)


def update_kernel(tile, deep, ready_ref, factor_ref, inverse_ref, spread_ref, *rest):
    others, (out_ref, made, moved, sems) = rest[:-4], rest[-4:]
    count, dof, total = ready_ref.shape
    products = len(others) * count
    steps = total // tile
    copies = []

    def multiply(t):
        cols = slice(t * tile, (t + 1) * tile)
        for d, other in enumerate(others):
            stack = jnp.concatenate([other[m, deep:, cols] for m in range(count)], axis=0)
            for m in range(count):
                moved[t % 2, d * count + m] = (
                    dot(inverse_ref[:, :deep], other[m, :deep, cols]) + dot(spread_ref[m], stack))

    multiply(0)
    for t in range(steps):
        cols = slice(t * tile, (t + 1) * tile)
        if t + 1 < steps:
            multiply(t + 1)
        for n in range(count):
            value = ready_ref[n, :, cols]
            for k in range(products):
                at = n * products + k
                value -= factor_ref[at : at + 1, cols] * moved[t % 2, k]
            made[t, n] = value.astype(jnp.bfloat16)
        copy = pltpu.make_async_copy(made.at[t], out_ref.at[:, :, cols], sems.at[t])
        copy.start()
        copies.append(copy)
    for copy in copies:
        copy.wait()


def whole(array):
    return pl.BlockSpec(array.shape, lambda j: (0,) * array.ndim)


def body(solution, forcing, metric_scale, frequency, adjacency, partner, volume_matrix, trace_matrix, lift_matrix,
         block_inverse):
    current = solution[0]
    forcing_local = forcing[0]
    neighbours = adjacency[0]
    partner_rows = partner[0]
    count, dof, total = current.shape
    width = trace_matrix.shape[0] // 6
    iface_rows = partner_rows.shape[1]
    shards = lax.axis_size("space")
    peers = lax.axis_size("inst")
    section = lax.axis_index("row")
    place = jnp.stack([section, lax.axis_index("inst"), lax.axis_index("space")]).astype(jnp.int32)
    table = jnp.asarray(spectral_table(count * peers))
    smem = pl.BlockSpec(memory_space=pltpu.SMEM)
    bf16 = jnp.bfloat16

    with jax.named_scope("instances"):
        others = [lax.ppermute(current, "inst", [(i, (i + d) % peers) for i in range(peers)])
                  for d in range(1, peers)]

    with jax.named_scope("ends"):
        up, down, cross = pl.pallas_call(
            ends_kernel,
            grid=(1,),
            out_shape=(jax.ShapeDtypeStruct((count, 2 * width, LAYER), bf16),
                       jax.ShapeDtypeStruct((count, 2 * width, LAYER), bf16),
                       jax.ShapeDtypeStruct((count, width, iface_rows), bf16)),
            in_specs=[smem,
                      pl.BlockSpec((count, dof, LANES), lambda j: (0, 0, 0)),
                      pl.BlockSpec((count, dof, LANES), lambda j: (0, 0, total // LANES - 1)),
                      whole(trace_matrix)],
            out_specs=(pl.BlockSpec((count, 2 * width, LAYER), lambda j: (0, 0, 0)),
                       pl.BlockSpec((count, 2 * width, LAYER), lambda j: (0, 0, 0)),
                       pl.BlockSpec((count, width, iface_rows), lambda j: (0, 0, 0))),
            compiler_params=pltpu.CompilerParams(vmem_limit_bytes=VMEM_LIMIT),
            cost_estimate=pl.CostEstimate(flops=8 * width * dof * LANES * 2 * count,
                                          bytes_accessed=1_000_000, transcendentals=0),
            name="ends",
        )(place, current, current, trace_matrix)

    with jax.named_scope("halo"):
        low = lax.ppermute(up, "space", [(i, (i + 1) % shards) for i in range(shards)])
        high = lax.ppermute(down, "space", [(i, (i - 1) % shards) for i in range(shards)])
    with jax.named_scope("interface"):
        pieces = [lax.ppermute(cross, ("space", "row"),
                               [(i * 2 + r, (i + d) % shards * 2 + 1 - r) for i in range(shards) for r in range(2)])
                  for d in range(shards)]

    tile = 256
    steps = total // tile
    deep = dof // tile * tile
    by_tile = lambda *lead: pl.BlockSpec(lead + (tile,), lambda j: (0,) * len(lead) + (j,))
    with jax.named_scope("couple"):
        ready, factors, spread = pl.pallas_call(
            functools.partial(couple_kernel, shards, peers, deep),
            grid=(steps,),
            out_shape=(jax.ShapeDtypeStruct((count, dof, total), jnp.float32),
                       jax.ShapeDtypeStruct((count * count * (peers - 1), total), jnp.float32),
                       jax.ShapeDtypeStruct((count, dof, count * (dof - deep)), bf16)),
            in_specs=[smem, smem, smem, by_tile(6), whole(partner_rows), whole(current), by_tile(count, dof),
                      by_tile(count, dof), by_tile(1), whole(trace_matrix), whole(lift_matrix),
                      whole(volume_matrix), whole(block_inverse), whole(low), whole(high)] + [whole(p) for p in pieces],
            out_specs=(by_tile(count, dof), by_tile(count * count * (peers - 1)),
                       pl.BlockSpec((count, dof, count * (dof - deep)), lambda j: (0, 0, 0))),
            scratch_shapes=[pltpu.VMEM((6, count * width, total), bf16)],
            compiler_params=pltpu.CompilerParams(vmem_limit_bytes=VMEM_LIMIT),
            cost_estimate=pl.CostEstimate(
                flops=2 * count * total * (6 * width * dof * 2 + dof * dof + 6 * width * total),
                bytes_accessed=count * dof * total * 10, transcendentals=0),
            name="couple",
        )(place, frequency, table, neighbours, partner_rows, current, current, forcing_local, metric_scale,
          trace_matrix, lift_matrix, volume_matrix, block_inverse, low, high, *pieces)

    vmem = pl.BlockSpec(memory_space=pltpu.VMEM)
    with jax.named_scope("update"):
        result = pl.pallas_call(
            functools.partial(update_kernel, tile, deep),
            out_shape=jax.ShapeDtypeStruct((count, dof, total), bf16),
            in_specs=[vmem] * (3 + peers),
            out_specs=pl.BlockSpec(memory_space=pl.ANY),
            scratch_shapes=[pltpu.VMEM((steps, count, dof, tile), bf16),
                            pltpu.VMEM((2, (peers - 1) * count, dof, tile), jnp.float32),
                            pltpu.SemaphoreType.DMA((steps,))],
            compiler_params=pltpu.CompilerParams(vmem_limit_bytes=VMEM_LIMIT),
            cost_estimate=pl.CostEstimate(flops=2 * count * total * dof * dof * (peers - 1),
                                          bytes_accessed=count * dof * total * 8, transcendentals=0),
            name="update",
        )(ready, factors, block_inverse, spread, *others)
    return result[None]


def solution(mesh):
    in_specs = (
        P("row", "inst", None, ("groups", "space")),
        P("row", "inst", None, ("groups", "space")),
        P("row", ("groups", "space")),
        P(),
        P("row", None, ("groups", "space")),
        P("row", "inst", ("groups", "space")),
        P(),
        P(),
        P(),
        P(),
    )
    out_specs = P("row", "inst", None, ("groups", "space"))
    return jax.shard_map(body, mesh=mesh, in_specs=in_specs, out_specs=out_specs, check_vma=False)
```

```python
import functools

import jax
import jax.numpy as jnp
import numpy as np
from jax import lax
from jax.experimental import pallas as pl
from jax.experimental.pallas import tpu as pltpu
from jax.sharding import PartitionSpec as P

LAYER = 64
OPPOSITE = (1, 0, 3, 2, 5, 4)
LANES = 128
VMEM_LIMIT = 40 * 1024 * 1024


def spectral_table(instances):
    positions = np.arange(instances)
    distance = positions[:, None] - positions[None, :]
    parity = np.where(distance % 2 == 0, 1.0, -1.0)
    angles = np.pi * distance / instances
    sines = np.where(distance == 0, 1.0, np.sin(angles))
    cotangent = np.where(distance == 0, 0.0, np.cos(angles) / sines)
    return (0.5 * parity * cotangent).astype(np.float32)


def one_hot(picked, rows):
    numbers = lax.broadcasted_iota(jnp.int32, (rows, picked.shape[1]), 0)
    return jnp.where(numbers == picked, 1.0, 0.0).astype(jnp.bfloat16)


def dot(left, right):
    return jnp.dot(left, right, preferred_element_type=jnp.float32)


def ends_kernel(place_ref, first_ref, last_ref, trace_ref, up_ref, down_ref, cross_ref):
    width = trace_ref.shape[0] // 6
    section = place_ref[0]
    for n in range(first_ref.shape[0]):
        first = dot(trace_ref[...], first_ref[n]).astype(jnp.bfloat16)
        last = dot(trace_ref[4 * width :, :], last_ref[n]).astype(jnp.bfloat16)
        down_ref[n] = first[4 * width :, :LAYER]
        up_ref[n] = last[:, last.shape[1] - LAYER :]
        rows = cross_ref.shape[2]
        cross_ref[n] = jnp.where(section == 0, first[width : 2 * width, :rows], first[:width, :rows])


def couple_kernel(shards, peers, deep, place_ref, freq_ref, table_ref, adj_ref, partner_ref, all_ref, tile_ref, forcing_ref,
                  scale_ref, trace_ref, lift_ref, volume_ref, inverse_ref, low_ref, high_ref, *rest):
    pieces, (out_ref, factor_ref, spread_ref, traces) = rest[:shards], rest[shards:]
    step = pl.program_id(0)
    steps = pl.num_programs(0)
    count, dof, total = all_ref.shape
    width = trace_ref.shape[0] // 6
    tile = tile_ref.shape[2]
    section, inst, space = place_ref[0], place_ref[1], place_ref[2]

    @pl.when(step == 0)
    def _():
        for n in range(count):
            for c in range(total // tile):
                cols = slice(c * tile, (c + 1) * tile)
                made = dot(trace_ref[...], all_ref[n, :, cols]).astype(jnp.bfloat16)
                for f in range(6):
                    traces[f, n * width : (n + 1) * width, cols] = made[f * width : (f + 1) * width]

        left = dof - deep
        spread_ref[...] = jnp.zeros_like(spread_ref)
        for m in range(count):
            spread_ref[m, :, m * left : (m + 1) * left] = inverse_ref[:, deep:]

    column = lax.broadcasted_iota(jnp.int32, (1, tile), 1)
    at_edge = jnp.logical_or(step == 0, step == steps - 1)

    def gathered(edge):
        found = []
        for f in range(6):
            adj = adj_ref[f : f + 1, :]
            values = dot(traces[OPPOSITE[f]], one_hot(adj - LAYER, total))
            if edge and f >= 4:
                part = slice((5 - f) * width, (6 - f) * width)
                below = jnp.concatenate([low_ref[n, part, :] for n in range(count)], axis=0)
                above = jnp.concatenate([high_ref[n, part, :] for n in range(count)], axis=0)
                values += dot(below, one_hot(adj, LAYER))
                values += dot(above, one_hot(adj - (LAYER + total), LAYER))
            values = values.astype(jnp.bfloat16)
            if edge and f < 2:
                rows = partner_ref.shape[1]
                use = jnp.logical_and(step == 0, section == 1 - f)
                crossed = []
                for n in range(count):
                    wanted = partner_ref[n : n + 1, :]
                    arrived = jnp.zeros((width, rows), jnp.float32)
                    for d in range(shards):
                        source = lax.rem(space - d + shards, shards)
                        arrived += dot(pieces[d][n], one_hot(wanted - source * rows, rows))
                    crossed.append(arrived)
                crossed = jnp.concatenate(crossed, axis=0).astype(jnp.bfloat16)
                crossed = jnp.concatenate(
                    [crossed, jnp.zeros((count * width, tile - rows), jnp.bfloat16)], axis=1)
                take = jnp.logical_and(column < rows, use)
                values = jnp.where(take, crossed, values)
            found.append(values)
        return found

    def finish(edge):
        found = gathered(edge)
        frequency = freq_ref[0]
        scale = scale_ref[...]
        inverse_scale = 1.0 / scale
        for n in range(count):
            for d in range(1, peers):
                owner = lax.rem(inst - d + peers, peers)
                for m in range(count):
                    weight = table_ref[inst * count + n, owner * count + m] * frequency
                    at = (n * (peers - 1) + d - 1) * count + m
                    factor_ref[at : at + 1, :] = weight * inverse_scale
        for n in range(count):
            beside = jnp.concatenate([v[n * width : (n + 1) * width] for v in found], axis=0)
            inner = dot(lift_ref[...], beside) + dot(volume_ref[...], tile_ref[n])
            value = forcing_ref[n].astype(jnp.float32) - scale * inner
            for m in range(count):
                weight = table_ref[inst * count + n, inst * count + m] * frequency
                value -= weight * tile_ref[m].astype(jnp.float32)
            update = dot(inverse_ref[...], value.astype(jnp.bfloat16))
            out_ref[n] = tile_ref[n].astype(jnp.float32) + update * inverse_scale

    @pl.when(at_edge)
    def _():
        finish(True)

    @pl.when(jnp.logical_not(at_edge))
    def _():
        finish(False)


def update_kernel(tile, deep, ready_ref, factor_ref, inverse_ref, spread_ref, *rest):
    others, (out_ref, made, moved, sems) = rest[:-4], rest[-4:]
    count, dof, total = ready_ref.shape
    products = len(others) * count
    steps = total // tile
    copies = []

    def multiply(t):
        cols = slice(t * tile, (t + 1) * tile)
        for d, other in enumerate(others):
            stack = jnp.concatenate([other[m, deep:, cols] for m in range(count)], axis=0)
            for m in range(count):
                moved[t % 2, d * count + m] = (
                    dot(inverse_ref[:, :deep], other[m, :deep, cols]) + dot(spread_ref[m], stack))

    multiply(0)
    for t in range(steps):
        cols = slice(t * tile, (t + 1) * tile)
        if t + 1 < steps:
            multiply(t + 1)
        for n in range(count):
            value = ready_ref[n, :, cols]
            for k in range(products):
                at = n * products + k
                value -= factor_ref[at : at + 1, cols] * moved[t % 2, k]
            made[n, :, cols] = value.astype(jnp.bfloat16)
        if t > 0 or steps == 1:
            sent = slice(0 if t == 1 else t * tile, (t + 1) * tile)
            copy = pltpu.make_async_copy(made.at[:, :, sent], out_ref.at[:, :, sent], sems.at[t])
            copy.start()
            copies.append(copy)
    for copy in copies:
        copy.wait()


def whole(array):
    return pl.BlockSpec(array.shape, lambda j: (0,) * array.ndim)


def body(solution, forcing, metric_scale, frequency, adjacency, partner, volume_matrix, trace_matrix, lift_matrix,
         block_inverse):
    current = solution[0]
    forcing_local = forcing[0]
    neighbours = adjacency[0]
    partner_rows = partner[0]
    count, dof, total = current.shape
    width = trace_matrix.shape[0] // 6
    iface_rows = partner_rows.shape[1]
    shards = lax.axis_size("space")
    peers = lax.axis_size("inst")
    section = lax.axis_index("row")
    place = jnp.stack([section, lax.axis_index("inst"), lax.axis_index("space")]).astype(jnp.int32)
    table = jnp.asarray(spectral_table(count * peers))
    smem = pl.BlockSpec(memory_space=pltpu.SMEM)
    bf16 = jnp.bfloat16

    with jax.named_scope("instances"):
        others = [lax.ppermute(current, "inst", [(i, (i + d) % peers) for i in range(peers)])
                  for d in range(1, peers)]

    with jax.named_scope("ends"):
        up, down, cross = pl.pallas_call(
            ends_kernel,
            grid=(1,),
            out_shape=(jax.ShapeDtypeStruct((count, 2 * width, LAYER), bf16),
                       jax.ShapeDtypeStruct((count, 2 * width, LAYER), bf16),
                       jax.ShapeDtypeStruct((count, width, iface_rows), bf16)),
            in_specs=[smem,
                      pl.BlockSpec((count, dof, LANES), lambda j: (0, 0, 0)),
                      pl.BlockSpec((count, dof, LANES), lambda j: (0, 0, total // LANES - 1)),
                      whole(trace_matrix)],
            out_specs=(pl.BlockSpec((count, 2 * width, LAYER), lambda j: (0, 0, 0)),
                       pl.BlockSpec((count, 2 * width, LAYER), lambda j: (0, 0, 0)),
                       pl.BlockSpec((count, width, iface_rows), lambda j: (0, 0, 0))),
            compiler_params=pltpu.CompilerParams(vmem_limit_bytes=VMEM_LIMIT),
            cost_estimate=pl.CostEstimate(flops=8 * width * dof * LANES * 2 * count,
                                          bytes_accessed=1_000_000, transcendentals=0),
            name="ends",
        )(place, current, current, trace_matrix)

    with jax.named_scope("halo"):
        low = lax.ppermute(up, "space", [(i, (i + 1) % shards) for i in range(shards)])
        high = lax.ppermute(down, "space", [(i, (i - 1) % shards) for i in range(shards)])
    with jax.named_scope("interface"):
        pieces = [lax.ppermute(cross, ("space", "row"),
                               [(i * 2 + r, (i + d) % shards * 2 + 1 - r) for i in range(shards) for r in range(2)])
                  for d in range(shards)]

    tile = 256
    steps = total // tile
    deep = dof // tile * tile
    by_tile = lambda *lead: pl.BlockSpec(lead + (tile,), lambda j: (0,) * len(lead) + (j,))
    with jax.named_scope("couple"):
        ready, factors, spread = pl.pallas_call(
            functools.partial(couple_kernel, shards, peers, deep),
            grid=(steps,),
            out_shape=(jax.ShapeDtypeStruct((count, dof, total), jnp.float32),
                       jax.ShapeDtypeStruct((count * count * (peers - 1), total), jnp.float32),
                       jax.ShapeDtypeStruct((count, dof, count * (dof - deep)), bf16)),
            in_specs=[smem, smem, smem, by_tile(6), whole(partner_rows), whole(current), by_tile(count, dof),
                      by_tile(count, dof), by_tile(1), whole(trace_matrix), whole(lift_matrix),
                      whole(volume_matrix), whole(block_inverse), whole(low), whole(high)] + [whole(p) for p in pieces],
            out_specs=(by_tile(count, dof), by_tile(count * count * (peers - 1)),
                       pl.BlockSpec((count, dof, count * (dof - deep)), lambda j: (0, 0, 0))),
            scratch_shapes=[pltpu.VMEM((6, count * width, total), bf16)],
            compiler_params=pltpu.CompilerParams(vmem_limit_bytes=VMEM_LIMIT),
            cost_estimate=pl.CostEstimate(
                flops=2 * count * total * (6 * width * dof * 2 + dof * dof + 6 * width * total),
                bytes_accessed=count * dof * total * 10, transcendentals=0),
            name="couple",
        )(place, frequency, table, neighbours, partner_rows, current, current, forcing_local, metric_scale,
          trace_matrix, lift_matrix, volume_matrix, block_inverse, low, high, *pieces)

    vmem = pl.BlockSpec(memory_space=pltpu.VMEM)
    with jax.named_scope("update"):
        result = pl.pallas_call(
            functools.partial(update_kernel, tile, deep),
            out_shape=jax.ShapeDtypeStruct((count, dof, total), bf16),
            in_specs=[vmem] * (3 + peers),
            out_specs=pl.BlockSpec(memory_space=pl.ANY),
            scratch_shapes=[pltpu.VMEM((count, dof, total), bf16),
                            pltpu.VMEM((2, (peers - 1) * count, dof, tile), jnp.float32),
                            pltpu.SemaphoreType.DMA((steps,))],
            compiler_params=pltpu.CompilerParams(vmem_limit_bytes=VMEM_LIMIT),
            cost_estimate=pl.CostEstimate(flops=2 * count * total * dof * dof * (peers - 1),
                                          bytes_accessed=count * dof * total * 8, transcendentals=0),
            name="update",
        )(ready, factors, block_inverse, spread, *others)
    return result[None]


def solution(mesh):
    in_specs = (
        P("row", "inst", None, ("groups", "space")),
        P("row", "inst", None, ("groups", "space")),
        P("row", ("groups", "space")),
        P(),
        P("row", None, ("groups", "space")),
        P("row", "inst", ("groups", "space")),
        P(),
        P(),
        P(),
        P(),
    )
    out_specs = P("row", "inst", None, ("groups", "space"))
    return jax.shard_map(body, mesh=mesh, in_specs=in_specs, out_specs=out_specs, check_vma=False)
```

```python
import functools

import jax
import jax.numpy as jnp
import numpy as np
from jax import lax
from jax.experimental import pallas as pl
from jax.experimental.pallas import tpu as pltpu
from jax.sharding import PartitionSpec as P

LAYER = 64
OPPOSITE = (1, 0, 3, 2, 5, 4)
LANES = 128
VMEM_LIMIT = 40 * 1024 * 1024


def spectral_table(instances):
    positions = np.arange(instances)
    distance = positions[:, None] - positions[None, :]
    parity = np.where(distance % 2 == 0, 1.0, -1.0)
    angles = np.pi * distance / instances
    sines = np.where(distance == 0, 1.0, np.sin(angles))
    cotangent = np.where(distance == 0, 0.0, np.cos(angles) / sines)
    return (0.5 * parity * cotangent).astype(np.float32)


def one_hot(picked, rows):
    numbers = lax.broadcasted_iota(jnp.int32, (rows, picked.shape[1]), 0)
    return jnp.where(numbers == picked, 1.0, 0.0).astype(jnp.bfloat16)


def dot(left, right):
    return jnp.dot(left, right, preferred_element_type=jnp.float32)


def ends_kernel(place_ref, first_ref, last_ref, trace_ref, up_ref, down_ref, cross_ref):
    width = trace_ref.shape[0] // 6
    section = place_ref[0]
    for n in range(first_ref.shape[0]):
        first = dot(trace_ref[...], first_ref[n]).astype(jnp.bfloat16)
        last = dot(trace_ref[4 * width :, :], last_ref[n]).astype(jnp.bfloat16)
        down_ref[n] = first[4 * width :, :LAYER]
        up_ref[n] = last[:, last.shape[1] - LAYER :]
        rows = cross_ref.shape[2]
        cross_ref[n] = jnp.where(section == 0, first[width : 2 * width, :rows], first[:width, :rows])


def couple_kernel(shards, peers, place_ref, freq_ref, table_ref, adj_ref, partner_ref, all_ref, tile_ref, forcing_ref,
                  scale_ref, trace_ref, lift_ref, volume_ref, inverse_ref, low_ref, high_ref, *rest):
    pieces, (out_ref, factor_ref, traces) = rest[:shards], rest[shards:]
    step = pl.program_id(0)
    steps = pl.num_programs(0)
    count, dof, total = all_ref.shape
    width = trace_ref.shape[0] // 6
    tile = tile_ref.shape[2]
    section, inst, space = place_ref[0], place_ref[1], place_ref[2]

    @pl.when(step == 0)
    def _():
        for n in range(count):
            for c in range(total // tile):
                cols = slice(c * tile, (c + 1) * tile)
                made = dot(trace_ref[...], all_ref[n, :, cols]).astype(jnp.bfloat16)
                for f in range(6):
                    traces[f, n * width : (n + 1) * width, cols] = made[f * width : (f + 1) * width]

    column = lax.broadcasted_iota(jnp.int32, (1, tile), 1)
    at_edge = jnp.logical_or(step == 0, step == steps - 1)

    def gathered(edge):
        found = []
        for f in range(6):
            adj = adj_ref[f : f + 1, :]
            values = dot(traces[OPPOSITE[f]], one_hot(adj - LAYER, total))
            if edge and f >= 4:
                part = slice((5 - f) * width, (6 - f) * width)
                below = jnp.concatenate([low_ref[n, part, :] for n in range(count)], axis=0)
                above = jnp.concatenate([high_ref[n, part, :] for n in range(count)], axis=0)
                values += dot(below, one_hot(adj, LAYER))
                values += dot(above, one_hot(adj - (LAYER + total), LAYER))
            values = values.astype(jnp.bfloat16)
            if edge and f < 2:
                rows = partner_ref.shape[1]
                use = jnp.logical_and(step == 0, section == 1 - f)
                crossed = []
                for n in range(count):
                    wanted = partner_ref[n : n + 1, :]
                    arrived = jnp.zeros((width, rows), jnp.float32)
                    for d in range(shards):
                        source = lax.rem(space - d + shards, shards)
                        arrived += dot(pieces[d][n], one_hot(wanted - source * rows, rows))
                    crossed.append(arrived)
                crossed = jnp.concatenate(crossed, axis=0).astype(jnp.bfloat16)
                crossed = jnp.concatenate(
                    [crossed, jnp.zeros((count * width, tile - rows), jnp.bfloat16)], axis=1)
                take = jnp.logical_and(column < rows, use)
                values = jnp.where(take, crossed, values)
            found.append(values)
        return found

    def finish(edge):
        found = gathered(edge)
        frequency = freq_ref[0]
        scale = scale_ref[...]
        inverse_scale = 1.0 / scale
        for n in range(count):
            for d in range(1, peers):
                owner = lax.rem(inst - d + peers, peers)
                for m in range(count):
                    weight = table_ref[inst * count + n, owner * count + m] * frequency
                    at = (n * (peers - 1) + d - 1) * count + m
                    factor_ref[at : at + 1, :] = weight * inverse_scale
        for n in range(count):
            beside = jnp.concatenate([v[n * width : (n + 1) * width] for v in found], axis=0)
            inner = dot(lift_ref[...], beside) + dot(volume_ref[...], tile_ref[n])
            value = forcing_ref[n].astype(jnp.float32) - scale * inner
            for m in range(count):
                weight = table_ref[inst * count + n, inst * count + m] * frequency
                value -= weight * tile_ref[m].astype(jnp.float32)
            update = dot(inverse_ref[...], value.astype(jnp.bfloat16))
            out_ref[n] = tile_ref[n].astype(jnp.float32) + update * inverse_scale

    @pl.when(at_edge)
    def _():
        finish(True)

    @pl.when(jnp.logical_not(at_edge))
    def _():
        finish(False)


def update_kernel(tile, ready_ref, factor_ref, inverse_ref, *rest):
    others, (out_ref, made, sems) = rest[:-3], rest[-3:]
    count, dof, total = ready_ref.shape
    narrow = max(tile // count, LANES)
    cuts = list(range(0, total - tile + 1, tile)) + list(range(total - tile + narrow, total + 1, narrow))
    copies = []
    for p, (first, last) in enumerate(zip(cuts[:-1], cuts[1:])):
        cols, size = slice(first, last), last - first
        if size < tile:
            wide = [dot(inverse_ref[...], jnp.concatenate([other[m, :, cols] for m in range(count)], axis=1))
                    for other in others]
            moved = [w[:, m * size : (m + 1) * size] for w in wide for m in range(count)]
        else:
            moved = [dot(inverse_ref[...], other[m, :, cols]) for other in others for m in range(count)]
        for n in range(count):
            value = ready_ref[n, :, cols]
            for k, part in enumerate(moved):
                at = n * len(moved) + k
                value -= factor_ref[at : at + 1, cols] * part
            made[n, :, cols] = value.astype(jnp.bfloat16)
        copy = pltpu.make_async_copy(made.at[:, :, cols], out_ref.at[:, :, cols], sems.at[p])
        copy.start()
        copies.append(copy)
    for copy in copies:
        copy.wait()


def whole(array):
    return pl.BlockSpec(array.shape, lambda j: (0,) * array.ndim)


def body(solution, forcing, metric_scale, frequency, adjacency, partner, volume_matrix, trace_matrix, lift_matrix,
         block_inverse):
    current = solution[0]
    forcing_local = forcing[0]
    neighbours = adjacency[0]
    partner_rows = partner[0]
    count, dof, total = current.shape
    width = trace_matrix.shape[0] // 6
    iface_rows = partner_rows.shape[1]
    shards = lax.axis_size("space")
    peers = lax.axis_size("inst")
    section = lax.axis_index("row")
    place = jnp.stack([section, lax.axis_index("inst"), lax.axis_index("space")]).astype(jnp.int32)
    table = jnp.asarray(spectral_table(count * peers))
    smem = pl.BlockSpec(memory_space=pltpu.SMEM)
    bf16 = jnp.bfloat16

    with jax.named_scope("instances"):
        others = [lax.ppermute(current, "inst", [(i, (i + d) % peers) for i in range(peers)])
                  for d in range(1, peers)]

    with jax.named_scope("ends"):
        up, down, cross = pl.pallas_call(
            ends_kernel,
            grid=(1,),
            out_shape=(jax.ShapeDtypeStruct((count, 2 * width, LAYER), bf16),
                       jax.ShapeDtypeStruct((count, 2 * width, LAYER), bf16),
                       jax.ShapeDtypeStruct((count, width, iface_rows), bf16)),
            in_specs=[smem,
                      pl.BlockSpec((count, dof, LANES), lambda j: (0, 0, 0)),
                      pl.BlockSpec((count, dof, LANES), lambda j: (0, 0, total // LANES - 1)),
                      whole(trace_matrix)],
            out_specs=(pl.BlockSpec((count, 2 * width, LAYER), lambda j: (0, 0, 0)),
                       pl.BlockSpec((count, 2 * width, LAYER), lambda j: (0, 0, 0)),
                       pl.BlockSpec((count, width, iface_rows), lambda j: (0, 0, 0))),
            compiler_params=pltpu.CompilerParams(vmem_limit_bytes=VMEM_LIMIT),
            cost_estimate=pl.CostEstimate(flops=8 * width * dof * LANES * 2 * count,
                                          bytes_accessed=1_000_000, transcendentals=0),
            name="ends",
        )(place, current, current, trace_matrix)

    with jax.named_scope("halo"):
        low = lax.ppermute(up, "space", [(i, (i + 1) % shards) for i in range(shards)])
        high = lax.ppermute(down, "space", [(i, (i - 1) % shards) for i in range(shards)])
    with jax.named_scope("interface"):
        pieces = [lax.ppermute(cross, ("space", "row"),
                               [(i * 2 + r, (i + d) % shards * 2 + 1 - r) for i in range(shards) for r in range(2)])
                  for d in range(shards)]

    tile = 256
    steps = total // tile
    by_tile = lambda *lead: pl.BlockSpec(lead + (tile,), lambda j: (0,) * len(lead) + (j,))
    with jax.named_scope("couple"):
        ready, factors = pl.pallas_call(
            functools.partial(couple_kernel, shards, peers),
            grid=(steps,),
            out_shape=(jax.ShapeDtypeStruct((count, dof, total), jnp.float32),
                       jax.ShapeDtypeStruct((count * count * (peers - 1), total), jnp.float32)),
            in_specs=[smem, smem, smem, by_tile(6), whole(partner_rows), whole(current), by_tile(count, dof),
                      by_tile(count, dof), by_tile(1), whole(trace_matrix), whole(lift_matrix),
                      whole(volume_matrix), whole(block_inverse), whole(low), whole(high)] + [whole(p) for p in pieces],
            out_specs=(by_tile(count, dof), by_tile(count * count * (peers - 1))),
            scratch_shapes=[pltpu.VMEM((6, count * width, total), bf16)],
            compiler_params=pltpu.CompilerParams(vmem_limit_bytes=VMEM_LIMIT),
            cost_estimate=pl.CostEstimate(
                flops=2 * count * total * (6 * width * dof * 2 + dof * dof + 6 * width * total),
                bytes_accessed=count * dof * total * 10, transcendentals=0),
            name="couple",
        )(place, frequency, table, neighbours, partner_rows, current, current, forcing_local, metric_scale,
          trace_matrix, lift_matrix, volume_matrix, block_inverse, low, high, *pieces)

    vmem = pl.BlockSpec(memory_space=pltpu.VMEM)
    with jax.named_scope("update"):
        result = pl.pallas_call(
            functools.partial(update_kernel, tile),
            out_shape=jax.ShapeDtypeStruct((count, dof, total), bf16),
            in_specs=[vmem] * (2 + peers),
            out_specs=pl.BlockSpec(memory_space=pl.ANY),
            scratch_shapes=[pltpu.VMEM((count, dof, total), bf16), pltpu.SemaphoreType.DMA((steps + count,))],
            compiler_params=pltpu.CompilerParams(vmem_limit_bytes=VMEM_LIMIT),
            cost_estimate=pl.CostEstimate(flops=2 * count * total * dof * dof * (peers - 1),
                                          bytes_accessed=count * dof * total * 8, transcendentals=0),
            name="update",
        )(ready, factors, block_inverse, *others)
    return result[None]


def solution(mesh):
    in_specs = (
        P("row", "inst", None, ("groups", "space")),
        P("row", "inst", None, ("groups", "space")),
        P("row", ("groups", "space")),
        P(),
        P("row", None, ("groups", "space")),
        P("row", "inst", ("groups", "space")),
        P(),
        P(),
        P(),
        P(),
    )
    out_specs = P("row", "inst", None, ("groups", "space"))
    return jax.shard_map(body, mesh=mesh, in_specs=in_specs, out_specs=out_specs, check_vma=False)
```

```python
import functools

import jax
import jax.numpy as jnp
import numpy as np
from jax import lax
from jax.experimental import pallas as pl
from jax.experimental.pallas import tpu as pltpu
from jax.sharding import PartitionSpec as P

LAYER = 64
OPPOSITE = (1, 0, 3, 2, 5, 4)
LANES = 128
VMEM_LIMIT = 40 * 1024 * 1024


def spectral_table(instances):
    positions = np.arange(instances)
    distance = positions[:, None] - positions[None, :]
    parity = np.where(distance % 2 == 0, 1.0, -1.0)
    angles = np.pi * distance / instances
    sines = np.where(distance == 0, 1.0, np.sin(angles))
    cotangent = np.where(distance == 0, 0.0, np.cos(angles) / sines)
    return (0.5 * parity * cotangent).astype(np.float32)


def one_hot(picked, rows):
    numbers = lax.broadcasted_iota(jnp.int32, (rows, picked.shape[1]), 0)
    return jnp.where(numbers == picked, 1.0, 0.0).astype(jnp.bfloat16)


def dot(left, right):
    return jnp.dot(left, right, preferred_element_type=jnp.float32)


def ends_kernel(place_ref, first_ref, last_ref, trace_ref, up_ref, down_ref, cross_ref):
    width = trace_ref.shape[0] // 6
    section = place_ref[0]
    for n in range(first_ref.shape[0]):
        first = dot(trace_ref[...], first_ref[n]).astype(jnp.bfloat16)
        last = dot(trace_ref[4 * width :, :], last_ref[n]).astype(jnp.bfloat16)
        down_ref[:, n * LAYER : (n + 1) * LAYER] = first[4 * width :, :LAYER]
        up_ref[:, n * LAYER : (n + 1) * LAYER] = last[:, last.shape[1] - LAYER :]
        rows = cross_ref.shape[1] // first_ref.shape[0]
        cross_ref[:, n * rows : (n + 1) * rows] = jnp.where(
            section == 0, first[width : 2 * width, :rows], first[:width, :rows])


def couple_kernel(shards, peers, place_ref, freq_ref, table_ref, adj_ref, partner_ref, all_ref, tile_ref, forcing_ref,
                  scale_ref, trace_ref, lift_ref, volume_ref, inverse_ref, low_ref, high_ref, *rest):
    pieces, (out_ref, factor_ref, traces) = rest[:shards], rest[shards:]
    step = pl.program_id(0)
    steps = pl.num_programs(0)
    count, dof, total = all_ref.shape
    width = trace_ref.shape[0] // 6
    tile = tile_ref.shape[2]
    section, inst, space = place_ref[0], place_ref[1], place_ref[2]

    @pl.when(step == 0)
    def _():
        for n in range(count):
            for c in range(total // tile):
                cols = slice(c * tile, (c + 1) * tile)
                made = dot(trace_ref[...], all_ref[n, :, cols]).astype(jnp.bfloat16)
                for f in range(6):
                    traces[f, n * width : (n + 1) * width, cols] = made[f * width : (f + 1) * width]

    column = lax.broadcasted_iota(jnp.int32, (1, tile), 1)
    at_edge = jnp.logical_or(step == 0, step == steps - 1)

    def gathered(edge):
        found = []
        for f in range(6):
            adj = adj_ref[f : f + 1, :]
            values = dot(traces[OPPOSITE[f]], one_hot(adj - LAYER, total))
            if edge and f >= 4:
                part = slice((5 - f) * width, (6 - f) * width)
                below = jnp.concatenate([low_ref[part, n * LAYER : (n + 1) * LAYER] for n in range(count)], axis=0)
                above = jnp.concatenate([high_ref[part, n * LAYER : (n + 1) * LAYER] for n in range(count)], axis=0)
                values += dot(below, one_hot(adj, LAYER))
                values += dot(above, one_hot(adj - (LAYER + total), LAYER))
            values = values.astype(jnp.bfloat16)
            if edge and f < 2:
                rows = partner_ref.shape[1]
                use = jnp.logical_and(step == 0, section == 1 - f)
                crossed = []
                for n in range(count):
                    wanted = partner_ref[n : n + 1, :]
                    arrived = jnp.zeros((width, rows), jnp.float32)
                    for d in range(shards):
                        source = lax.rem(space - d + shards, shards)
                        arrived += dot(pieces[d][:, n * rows : (n + 1) * rows], one_hot(wanted - source * rows, rows))
                    crossed.append(arrived)
                crossed = jnp.concatenate(crossed, axis=0).astype(jnp.bfloat16)
                crossed = jnp.concatenate(
                    [crossed, jnp.zeros((count * width, tile - rows), jnp.bfloat16)], axis=1)
                take = jnp.logical_and(column < rows, use)
                values = jnp.where(take, crossed, values)
            found.append(values)
        return found

    def finish(edge):
        found = gathered(edge)
        frequency = freq_ref[0]
        scale = scale_ref[...]
        inverse_scale = 1.0 / scale
        for n in range(count):
            for d in range(1, peers):
                owner = lax.rem(inst - d + peers, peers)
                for m in range(count):
                    weight = table_ref[inst * count + n, owner * count + m] * frequency
                    at = (n * (peers - 1) + d - 1) * count + m
                    factor_ref[at : at + 1, :] = weight * inverse_scale
        for n in range(count):
            beside = jnp.concatenate([v[n * width : (n + 1) * width] for v in found], axis=0)
            inner = dot(lift_ref[...], beside) + dot(volume_ref[...], tile_ref[n])
            value = forcing_ref[n].astype(jnp.float32) - scale * inner
            for m in range(count):
                weight = table_ref[inst * count + n, inst * count + m] * frequency
                value -= weight * tile_ref[m].astype(jnp.float32)
            update = dot(inverse_ref[...], value.astype(jnp.bfloat16))
            out_ref[n] = tile_ref[n].astype(jnp.float32) + update * inverse_scale

    @pl.when(at_edge)
    def _():
        finish(True)

    @pl.when(jnp.logical_not(at_edge))
    def _():
        finish(False)


def update_kernel(tile, ready_ref, factor_ref, inverse_ref, *rest):
    others, (out_ref, made, sems) = rest[:-3], rest[-3:]
    count, dof, total = ready_ref.shape
    copies = []
    for t in range(total // tile):
        cols = slice(t * tile, (t + 1) * tile)
        moved = [dot(inverse_ref[...], other[m, :, cols]) for other in others for m in range(count)]
        for n in range(count):
            value = ready_ref[n, :, cols]
            for k, part in enumerate(moved):
                at = n * len(moved) + k
                value -= factor_ref[at : at + 1, cols] * part
            made[t, n] = value.astype(jnp.bfloat16)
        copy = pltpu.make_async_copy(made.at[t], out_ref.at[:, :, cols], sems.at[t])
        copy.start()
        copies.append(copy)
    for copy in copies:
        copy.wait()


def whole(array):
    return pl.BlockSpec(array.shape, lambda j: (0,) * array.ndim)


def body(solution, forcing, metric_scale, frequency, adjacency, partner, volume_matrix, trace_matrix, lift_matrix,
         block_inverse):
    current = solution[0]
    forcing_local = forcing[0]
    neighbours = adjacency[0]
    partner_rows = partner[0]
    count, dof, total = current.shape
    width = trace_matrix.shape[0] // 6
    iface_rows = partner_rows.shape[1]
    shards = lax.axis_size("space")
    peers = lax.axis_size("inst")
    section = lax.axis_index("row")
    place = jnp.stack([section, lax.axis_index("inst"), lax.axis_index("space")]).astype(jnp.int32)
    table = jnp.asarray(spectral_table(count * peers))
    smem = pl.BlockSpec(memory_space=pltpu.SMEM)
    bf16 = jnp.bfloat16

    with jax.named_scope("instances"):
        others = [lax.ppermute(current, "inst", [(i, (i + d) % peers) for i in range(peers)])
                  for d in range(1, peers)]

    with jax.named_scope("ends"):
        up, down, cross = pl.pallas_call(
            ends_kernel,
            grid=(1,),
            out_shape=(jax.ShapeDtypeStruct((2 * width, count * LAYER), bf16),
                       jax.ShapeDtypeStruct((2 * width, count * LAYER), bf16),
                       jax.ShapeDtypeStruct((width, count * iface_rows), bf16)),
            in_specs=[smem,
                      pl.BlockSpec((count, dof, LANES), lambda j: (0, 0, 0)),
                      pl.BlockSpec((count, dof, LANES), lambda j: (0, 0, total // LANES - 1)),
                      whole(trace_matrix)],
            out_specs=(pl.BlockSpec((2 * width, count * LAYER), lambda j: (0, 0)),
                       pl.BlockSpec((2 * width, count * LAYER), lambda j: (0, 0)),
                       pl.BlockSpec((width, count * iface_rows), lambda j: (0, 0))),
            compiler_params=pltpu.CompilerParams(vmem_limit_bytes=VMEM_LIMIT),
            cost_estimate=pl.CostEstimate(flops=8 * width * dof * LANES * 2 * count,
                                          bytes_accessed=1_000_000, transcendentals=0),
            name="ends",
        )(place, current, current, trace_matrix)

    with jax.named_scope("halo"):
        low = lax.ppermute(up, "space", [(i, (i + 1) % shards) for i in range(shards)])
        high = lax.ppermute(down, "space", [(i, (i - 1) % shards) for i in range(shards)])
    with jax.named_scope("interface"):
        pieces = [lax.ppermute(cross, ("space", "row"),
                               [(i * 2 + r, (i + d) % shards * 2 + 1 - r) for i in range(shards) for r in range(2)])
                  for d in range(shards)]

    tile = 256
    steps = total // tile
    by_tile = lambda *lead: pl.BlockSpec(lead + (tile,), lambda j: (0,) * len(lead) + (j,))
    with jax.named_scope("couple"):
        ready, factors = pl.pallas_call(
            functools.partial(couple_kernel, shards, peers),
            grid=(steps,),
            out_shape=(jax.ShapeDtypeStruct((count, dof, total), jnp.float32),
                       jax.ShapeDtypeStruct((count * count * (peers - 1), total), jnp.float32)),
            in_specs=[smem, smem, smem, by_tile(6), whole(partner_rows), whole(current), by_tile(count, dof),
                      by_tile(count, dof), by_tile(1), whole(trace_matrix), whole(lift_matrix),
                      whole(volume_matrix), whole(block_inverse), whole(low), whole(high)] + [whole(p) for p in pieces],
            out_specs=(by_tile(count, dof), by_tile(count * count * (peers - 1))),
            scratch_shapes=[pltpu.VMEM((6, count * width, total), bf16)],
            compiler_params=pltpu.CompilerParams(vmem_limit_bytes=VMEM_LIMIT),
            cost_estimate=pl.CostEstimate(
                flops=2 * count * total * (6 * width * dof * 2 + dof * dof + 6 * width * total),
                bytes_accessed=count * dof * total * 10, transcendentals=0),
            name="couple",
        )(place, frequency, table, neighbours, partner_rows, current, current, forcing_local, metric_scale,
          trace_matrix, lift_matrix, volume_matrix, block_inverse, low, high, *pieces)

    vmem = pl.BlockSpec(memory_space=pltpu.VMEM)
    with jax.named_scope("update"):
        result = pl.pallas_call(
            functools.partial(update_kernel, tile),
            out_shape=jax.ShapeDtypeStruct((count, dof, total), bf16),
            in_specs=[vmem] * (2 + peers),
            out_specs=pl.BlockSpec(memory_space=pl.ANY),
            scratch_shapes=[pltpu.VMEM((steps, count, dof, tile), bf16), pltpu.SemaphoreType.DMA((steps,))],
            compiler_params=pltpu.CompilerParams(vmem_limit_bytes=VMEM_LIMIT),
            cost_estimate=pl.CostEstimate(flops=2 * count * total * dof * dof * (peers - 1),
                                          bytes_accessed=count * dof * total * 8, transcendentals=0),
            name="update",
        )(ready, factors, block_inverse, *others)
    return result[None]


def solution(mesh):
    in_specs = (
        P("row", "inst", None, ("groups", "space")),
        P("row", "inst", None, ("groups", "space")),
        P("row", ("groups", "space")),
        P(),
        P("row", None, ("groups", "space")),
        P("row", "inst", ("groups", "space")),
        P(),
        P(),
        P(),
        P(),
    )
    out_specs = P("row", "inst", None, ("groups", "space"))
    return jax.shard_map(body, mesh=mesh, in_specs=in_specs, out_specs=out_specs, check_vma=False)
```

```python
import functools

import jax
import jax.numpy as jnp
import numpy as np
from jax import lax
from jax.experimental import pallas as pl
from jax.experimental.pallas import tpu as pltpu
from jax.sharding import PartitionSpec as P

LAYER = 64
OPPOSITE = (1, 0, 3, 2, 5, 4)
LANES = 128
VMEM_LIMIT = 40 * 1024 * 1024


def spectral_table(instances):
    positions = np.arange(instances)
    distance = positions[:, None] - positions[None, :]
    parity = np.where(distance % 2 == 0, 1.0, -1.0)
    angles = np.pi * distance / instances
    sines = np.where(distance == 0, 1.0, np.sin(angles))
    cotangent = np.where(distance == 0, 0.0, np.cos(angles) / sines)
    return (0.5 * parity * cotangent).astype(np.float32)


def one_hot(picked, rows):
    numbers = lax.broadcasted_iota(jnp.int32, (rows, picked.shape[1]), 0)
    return jnp.where(numbers == picked, 1.0, 0.0).astype(jnp.bfloat16)


def dot(left, right):
    return jnp.dot(left, right, preferred_element_type=jnp.float32)


def ends_kernel(place_ref, first_ref, last_ref, trace_ref, up_ref, down_ref, cross_ref):
    width = trace_ref.shape[0] // 6
    section = place_ref[0]
    for n in range(first_ref.shape[0]):
        first = dot(trace_ref[...], first_ref[n]).astype(jnp.bfloat16)
        last = dot(trace_ref[4 * width :, :], last_ref[n]).astype(jnp.bfloat16)
        down_ref[:, n * LAYER : (n + 1) * LAYER] = first[4 * width :, :LAYER]
        up_ref[:, n * LAYER : (n + 1) * LAYER] = last[:, last.shape[1] - LAYER :]
        rows = cross_ref.shape[1] // first_ref.shape[0]
        cross_ref[:, n * rows : (n + 1) * rows] = jnp.where(
            section == 0, first[width : 2 * width, :rows], first[:width, :rows])


def couple_kernel(shards, peers, deep, place_ref, freq_ref, table_ref, adj_ref, partner_ref, all_ref, tile_ref, forcing_ref,
                  scale_ref, trace_ref, lift_ref, volume_ref, inverse_ref, low_ref, high_ref, *rest):
    pieces, (out_ref, factor_ref, spread_ref, traces) = rest[:shards], rest[shards:]
    step = pl.program_id(0)
    steps = pl.num_programs(0)
    count, dof, total = all_ref.shape
    width = trace_ref.shape[0] // 6
    tile = tile_ref.shape[2]
    section, inst, space = place_ref[0], place_ref[1], place_ref[2]

    @pl.when(step == 0)
    def _():
        for n in range(count):
            for c in range(total // tile):
                cols = slice(c * tile, (c + 1) * tile)
                made = dot(trace_ref[...], all_ref[n, :, cols]).astype(jnp.bfloat16)
                for f in range(6):
                    traces[f, n * width : (n + 1) * width, cols] = made[f * width : (f + 1) * width]

        left = dof - deep
        spread_ref[...] = jnp.zeros_like(spread_ref)
        for m in range(count):
            spread_ref[m, :, m * left : (m + 1) * left] = inverse_ref[:, deep:]

    column = lax.broadcasted_iota(jnp.int32, (1, tile), 1)
    at_edge = jnp.logical_or(step == 0, step == steps - 1)

    def gathered(edge):
        found = []
        for f in range(6):
            adj = adj_ref[f : f + 1, :]
            values = dot(traces[OPPOSITE[f]], one_hot(adj - LAYER, total))
            if edge and f >= 4:
                part = slice((5 - f) * width, (6 - f) * width)
                below = jnp.concatenate([low_ref[part, n * LAYER : (n + 1) * LAYER] for n in range(count)], axis=0)
                above = jnp.concatenate([high_ref[part, n * LAYER : (n + 1) * LAYER] for n in range(count)], axis=0)
                values += dot(below, one_hot(adj, LAYER))
                values += dot(above, one_hot(adj - (LAYER + total), LAYER))
            values = values.astype(jnp.bfloat16)
            if edge and f < 2:
                rows = partner_ref.shape[1]
                use = jnp.logical_and(step == 0, section == 1 - f)
                crossed = []
                for n in range(count):
                    wanted = partner_ref[n : n + 1, :]
                    arrived = jnp.zeros((width, rows), jnp.float32)
                    for d in range(shards):
                        source = lax.rem(space - d + shards, shards)
                        arrived += dot(pieces[d][:, n * rows : (n + 1) * rows], one_hot(wanted - source * rows, rows))
                    crossed.append(arrived)
                crossed = jnp.concatenate(crossed, axis=0).astype(jnp.bfloat16)
                crossed = jnp.concatenate(
                    [crossed, jnp.zeros((count * width, tile - rows), jnp.bfloat16)], axis=1)
                take = jnp.logical_and(column < rows, use)
                values = jnp.where(take, crossed, values)
            found.append(values)
        return found

    def finish(edge):
        found = gathered(edge)
        frequency = freq_ref[0]
        scale = scale_ref[...]
        inverse_scale = 1.0 / scale
        for n in range(count):
            for d in range(1, peers):
                owner = lax.rem(inst - d + peers, peers)
                for m in range(count):
                    weight = table_ref[inst * count + n, owner * count + m] * frequency
                    at = (n * (peers - 1) + d - 1) * count + m
                    factor_ref[at : at + 1, :] = weight * inverse_scale
        for n in range(count):
            beside = jnp.concatenate([v[n * width : (n + 1) * width] for v in found], axis=0)
            inner = dot(lift_ref[...], beside) + dot(volume_ref[...], tile_ref[n])
            value = forcing_ref[n].astype(jnp.float32) - scale * inner
            for m in range(count):
                weight = table_ref[inst * count + n, inst * count + m] * frequency
                value -= weight * tile_ref[m].astype(jnp.float32)
            update = dot(inverse_ref[...], value.astype(jnp.bfloat16))
            out_ref[n] = tile_ref[n].astype(jnp.float32) + update * inverse_scale

    @pl.when(at_edge)
    def _():
        finish(True)

    @pl.when(jnp.logical_not(at_edge))
    def _():
        finish(False)


def update_kernel(tile, deep, ready_ref, factor_ref, inverse_ref, spread_ref, *rest):
    others, (out_ref, made, moved, sems) = rest[:-4], rest[-4:]
    count, dof, total = ready_ref.shape
    products = len(others) * count
    steps = total // tile
    copies = []

    def multiply(t):
        cols = slice(t * tile, (t + 1) * tile)
        for d, other in enumerate(others):
            stack = jnp.concatenate([other[m, deep:, cols] for m in range(count)], axis=0)
            for m in range(count):
                moved[t % 2, d * count + m] = (
                    dot(inverse_ref[:, :deep], other[m, :deep, cols]) + dot(spread_ref[m], stack))

    multiply(0)
    for t in range(steps):
        cols = slice(t * tile, (t + 1) * tile)
        if t + 1 < steps:
            multiply(t + 1)
        for n in range(count):
            value = ready_ref[n, :, cols]
            for k in range(products):
                at = n * products + k
                value -= factor_ref[at : at + 1, cols] * moved[t % 2, k]
            made[t, n] = value.astype(jnp.bfloat16)
        copy = pltpu.make_async_copy(made.at[t], out_ref.at[:, :, cols], sems.at[t])
        copy.start()
        copies.append(copy)
    for copy in copies:
        copy.wait()


def whole(array):
    return pl.BlockSpec(array.shape, lambda j: (0,) * array.ndim)


def body(solution, forcing, metric_scale, frequency, adjacency, partner, volume_matrix, trace_matrix, lift_matrix,
         block_inverse):
    current = solution[0]
    forcing_local = forcing[0]
    neighbours = adjacency[0]
    partner_rows = partner[0]
    count, dof, total = current.shape
    width = trace_matrix.shape[0] // 6
    iface_rows = partner_rows.shape[1]
    shards = lax.axis_size("space")
    peers = lax.axis_size("inst")
    section = lax.axis_index("row")
    place = jnp.stack([section, lax.axis_index("inst"), lax.axis_index("space")]).astype(jnp.int32)
    table = jnp.asarray(spectral_table(count * peers))
    smem = pl.BlockSpec(memory_space=pltpu.SMEM)
    bf16 = jnp.bfloat16

    with jax.named_scope("instances"):
        others = [lax.ppermute(current, "inst", [(i, (i + d) % peers) for i in range(peers)])
                  for d in range(1, peers)]

    with jax.named_scope("ends"):
        up, down, cross = pl.pallas_call(
            ends_kernel,
            grid=(1,),
            out_shape=(jax.ShapeDtypeStruct((2 * width, count * LAYER), bf16),
                       jax.ShapeDtypeStruct((2 * width, count * LAYER), bf16),
                       jax.ShapeDtypeStruct((width, count * iface_rows), bf16)),
            in_specs=[smem,
                      pl.BlockSpec((count, dof, LANES), lambda j: (0, 0, 0)),
                      pl.BlockSpec((count, dof, LANES), lambda j: (0, 0, total // LANES - 1)),
                      whole(trace_matrix)],
            out_specs=(pl.BlockSpec((2 * width, count * LAYER), lambda j: (0, 0)),
                       pl.BlockSpec((2 * width, count * LAYER), lambda j: (0, 0)),
                       pl.BlockSpec((width, count * iface_rows), lambda j: (0, 0))),
            compiler_params=pltpu.CompilerParams(vmem_limit_bytes=VMEM_LIMIT),
            cost_estimate=pl.CostEstimate(flops=8 * width * dof * LANES * 2 * count,
                                          bytes_accessed=1_000_000, transcendentals=0),
            name="ends",
        )(place, current, current, trace_matrix)

    with jax.named_scope("halo"):
        low = lax.ppermute(up, "space", [(i, (i + 1) % shards) for i in range(shards)])
        high = lax.ppermute(down, "space", [(i, (i - 1) % shards) for i in range(shards)])
    with jax.named_scope("interface"):
        pieces = [lax.ppermute(cross, ("space", "row"),
                               [(i * 2 + r, (i + d) % shards * 2 + 1 - r) for i in range(shards) for r in range(2)])
                  for d in range(shards)]

    tile = 256
    steps = total // tile
    deep = dof // tile * tile
    by_tile = lambda *lead: pl.BlockSpec(lead + (tile,), lambda j: (0,) * len(lead) + (j,))
    with jax.named_scope("couple"):
        ready, factors, spread = pl.pallas_call(
            functools.partial(couple_kernel, shards, peers, deep),
            grid=(steps,),
            out_shape=(jax.ShapeDtypeStruct((count, dof, total), jnp.float32),
                       jax.ShapeDtypeStruct((count * count * (peers - 1), total), jnp.float32),
                       jax.ShapeDtypeStruct((count, dof, count * (dof - deep)), bf16)),
            in_specs=[smem, smem, smem, by_tile(6), whole(partner_rows), whole(current), by_tile(count, dof),
                      by_tile(count, dof), by_tile(1), whole(trace_matrix), whole(lift_matrix),
                      whole(volume_matrix), whole(block_inverse), whole(low), whole(high)] + [whole(p) for p in pieces],
            out_specs=(by_tile(count, dof), by_tile(count * count * (peers - 1)),
                       pl.BlockSpec((count, dof, count * (dof - deep)), lambda j: (0, 0, 0))),
            scratch_shapes=[pltpu.VMEM((6, count * width, total), bf16)],
            compiler_params=pltpu.CompilerParams(vmem_limit_bytes=VMEM_LIMIT),
            cost_estimate=pl.CostEstimate(
                flops=2 * count * total * (6 * width * dof * 2 + dof * dof + 6 * width * total),
                bytes_accessed=count * dof * total * 10, transcendentals=0),
            name="couple",
        )(place, frequency, table, neighbours, partner_rows, current, current, forcing_local, metric_scale,
          trace_matrix, lift_matrix, volume_matrix, block_inverse, low, high, *pieces)

    vmem = pl.BlockSpec(memory_space=pltpu.VMEM)
    with jax.named_scope("update"):
        result = pl.pallas_call(
            functools.partial(update_kernel, tile, deep),
            out_shape=jax.ShapeDtypeStruct((count, dof, total), bf16),
            in_specs=[vmem] * (3 + peers),
            out_specs=pl.BlockSpec(memory_space=pl.ANY),
            scratch_shapes=[pltpu.VMEM((steps, count, dof, tile), bf16),
                            pltpu.VMEM((2, (peers - 1) * count, dof, tile), jnp.float32),
                            pltpu.SemaphoreType.DMA((steps,))],
            compiler_params=pltpu.CompilerParams(vmem_limit_bytes=VMEM_LIMIT),
            cost_estimate=pl.CostEstimate(flops=2 * count * total * dof * dof * (peers - 1),
                                          bytes_accessed=count * dof * total * 8, transcendentals=0),
            name="update",
        )(ready, factors, block_inverse, spread, *others)
    return result[None]


def solution(mesh):
    in_specs = (
        P("row", "inst", None, ("groups", "space")),
        P("row", "inst", None, ("groups", "space")),
        P("row", ("groups", "space")),
        P(),
        P("row", None, ("groups", "space")),
        P("row", "inst", ("groups", "space")),
        P(),
        P(),
        P(),
        P(),
    )
    out_specs = P("row", "inst", None, ("groups", "space"))
    return jax.shard_map(body, mesh=mesh, in_specs=in_specs, out_specs=out_specs, check_vma=False)
```

```python
import functools

import jax
import jax.numpy as jnp
import numpy as np
from jax import lax
from jax.experimental import pallas as pl
from jax.experimental.pallas import tpu as pltpu
from jax.sharding import PartitionSpec as P

LAYER = 64
OPPOSITE = (1, 0, 3, 2, 5, 4)
LANES = 128
VMEM_LIMIT = 40 * 1024 * 1024


def spectral_table(instances):
    positions = np.arange(instances)
    distance = positions[:, None] - positions[None, :]
    parity = np.where(distance % 2 == 0, 1.0, -1.0)
    angles = np.pi * distance / instances
    sines = np.where(distance == 0, 1.0, np.sin(angles))
    cotangent = np.where(distance == 0, 0.0, np.cos(angles) / sines)
    return (0.5 * parity * cotangent).astype(np.float32)


def one_hot(picked, rows):
    numbers = lax.broadcasted_iota(jnp.int32, (rows, picked.shape[1]), 0)
    return jnp.where(numbers == picked, 1.0, 0.0).astype(jnp.bfloat16)


def dot(left, right):
    return jnp.dot(left, right, preferred_element_type=jnp.float32)


def ends_kernel(place_ref, first_ref, last_ref, trace_ref, up_ref, down_ref, cross_ref):
    width = trace_ref.shape[0] // 6
    section = place_ref[0]
    for n in range(first_ref.shape[0]):
        first = dot(trace_ref[...], first_ref[n]).astype(jnp.bfloat16)
        last = dot(trace_ref[4 * width :, :], last_ref[n]).astype(jnp.bfloat16)
        down_ref[:, n * LAYER : (n + 1) * LAYER] = first[4 * width :, :LAYER]
        up_ref[:, n * LAYER : (n + 1) * LAYER] = last[:, last.shape[1] - LAYER :]
        rows = cross_ref.shape[1] // first_ref.shape[0]
        cross_ref[:, n * rows : (n + 1) * rows] = jnp.where(
            section == 0, first[width : 2 * width, :rows], first[:width, :rows])


def couple_kernel(shards, peers, place_ref, freq_ref, table_ref, adj_ref, partner_ref, all_ref, tile_ref, forcing_ref,
                  scale_ref, trace_ref, lift_ref, volume_ref, inverse_ref, low_ref, high_ref, *rest):
    pieces, (out_ref, factor_ref, traces) = rest[:shards], rest[shards:]
    step = pl.program_id(0)
    steps = pl.num_programs(0)
    count, dof, total = all_ref.shape
    width = trace_ref.shape[0] // 6
    tile = tile_ref.shape[2]
    section, inst, space = place_ref[0], place_ref[1], place_ref[2]

    @pl.when(step == 0)
    def _():
        for n in range(count):
            for c in range(total // tile):
                cols = slice(c * tile, (c + 1) * tile)
                made = dot(trace_ref[...], all_ref[n, :, cols]).astype(jnp.bfloat16)
                for f in range(6):
                    traces[f, n * width : (n + 1) * width, cols] = made[f * width : (f + 1) * width]

    column = lax.broadcasted_iota(jnp.int32, (1, tile), 1)
    at_edge = jnp.logical_or(step == 0, step == steps - 1)

    def gathered(edge):
        found = []
        for f in range(6):
            adj = adj_ref[f : f + 1, :]
            values = dot(traces[OPPOSITE[f]], one_hot(adj - LAYER, total))
            if edge and f >= 4:
                part = slice((5 - f) * width, (6 - f) * width)
                below = jnp.concatenate([low_ref[part, n * LAYER : (n + 1) * LAYER] for n in range(count)], axis=0)
                above = jnp.concatenate([high_ref[part, n * LAYER : (n + 1) * LAYER] for n in range(count)], axis=0)
                values += dot(below, one_hot(adj, LAYER))
                values += dot(above, one_hot(adj - (LAYER + total), LAYER))
            values = values.astype(jnp.bfloat16)
            if edge and f < 2:
                rows = partner_ref.shape[1]
                use = jnp.logical_and(step == 0, section == 1 - f)
                crossed = []
                for n in range(count):
                    wanted = partner_ref[n : n + 1, :]
                    arrived = jnp.zeros((width, rows), jnp.float32)
                    for d in range(shards):
                        source = lax.rem(space - d + shards, shards)
                        arrived += dot(pieces[d][:, n * rows : (n + 1) * rows], one_hot(wanted - source * rows, rows))
                    crossed.append(arrived)
                crossed = jnp.concatenate(crossed, axis=0).astype(jnp.bfloat16)
                crossed = jnp.concatenate(
                    [crossed, jnp.zeros((count * width, tile - rows), jnp.bfloat16)], axis=1)
                take = jnp.logical_and(column < rows, use)
                values = jnp.where(take, crossed, values)
            found.append(values)
        return found

    def finish(edge):
        found = gathered(edge)
        frequency = freq_ref[0]
        scale = scale_ref[...]
        inverse_scale = 1.0 / scale
        for n in range(count):
            for d in range(1, peers):
                owner = lax.rem(inst - d + peers, peers)
                for m in range(count):
                    weight = table_ref[inst * count + n, owner * count + m] * frequency
                    at = (n * (peers - 1) + d - 1) * count + m
                    factor_ref[at : at + 1, :] = weight * inverse_scale
        for n in range(count):
            beside = jnp.concatenate([v[n * width : (n + 1) * width] for v in found], axis=0)
            inner = dot(lift_ref[...], beside) + dot(volume_ref[...], tile_ref[n])
            value = forcing_ref[n].astype(jnp.float32) - scale * inner
            for m in range(count):
                weight = table_ref[inst * count + n, inst * count + m] * frequency
                value -= weight * tile_ref[m].astype(jnp.float32)
            update = dot(inverse_ref[...], value.astype(jnp.bfloat16))
            out_ref[n] = tile_ref[n].astype(jnp.float32) + update * inverse_scale

    @pl.when(at_edge)
    def _():
        finish(True)

    @pl.when(jnp.logical_not(at_edge))
    def _():
        finish(False)


def update_kernel(tile, ready_ref, factor_ref, inverse_ref, *rest):
    others, (out_ref, made, sems) = rest[:-3], rest[-3:]
    count, dof, total = ready_ref.shape
    copies = []
    for t in range(total // tile):
        cols = slice(t * tile, (t + 1) * tile)
        moved = [dot(inverse_ref[...], other[m, :, cols]) for other in others for m in range(count)]
        for n in range(count):
            value = ready_ref[n, :, cols]
            for k, part in enumerate(moved):
                at = n * len(moved) + k
                value -= factor_ref[at : at + 1, cols] * part
            made[t, n] = value.astype(jnp.bfloat16)
            if t == total // tile - 1:
                copy = pltpu.make_async_copy(made.at[t, n], out_ref.at[n, :, cols], sems.at[t + n])
                copy.start()
                copies.append(copy)
        if t < total // tile - 1:
            copy = pltpu.make_async_copy(made.at[t], out_ref.at[:, :, cols], sems.at[t])
            copy.start()
            copies.append(copy)
    for copy in copies:
        copy.wait()


def whole(array):
    return pl.BlockSpec(array.shape, lambda j: (0,) * array.ndim)


def body(solution, forcing, metric_scale, frequency, adjacency, partner, volume_matrix, trace_matrix, lift_matrix,
         block_inverse):
    current = solution[0]
    forcing_local = forcing[0]
    neighbours = adjacency[0]
    partner_rows = partner[0]
    count, dof, total = current.shape
    width = trace_matrix.shape[0] // 6
    iface_rows = partner_rows.shape[1]
    shards = lax.axis_size("space")
    peers = lax.axis_size("inst")
    section = lax.axis_index("row")
    place = jnp.stack([section, lax.axis_index("inst"), lax.axis_index("space")]).astype(jnp.int32)
    table = jnp.asarray(spectral_table(count * peers))
    smem = pl.BlockSpec(memory_space=pltpu.SMEM)
    bf16 = jnp.bfloat16

    with jax.named_scope("instances"):
        others = [lax.ppermute(current, "inst", [(i, (i + d) % peers) for i in range(peers)])
                  for d in range(1, peers)]

    with jax.named_scope("ends"):
        up, down, cross = pl.pallas_call(
            ends_kernel,
            grid=(1,),
            out_shape=(jax.ShapeDtypeStruct((2 * width, count * LAYER), bf16),
                       jax.ShapeDtypeStruct((2 * width, count * LAYER), bf16),
                       jax.ShapeDtypeStruct((width, count * iface_rows), bf16)),
            in_specs=[smem,
                      pl.BlockSpec((count, dof, LANES), lambda j: (0, 0, 0)),
                      pl.BlockSpec((count, dof, LANES), lambda j: (0, 0, total // LANES - 1)),
                      whole(trace_matrix)],
            out_specs=(pl.BlockSpec((2 * width, count * LAYER), lambda j: (0, 0)),
                       pl.BlockSpec((2 * width, count * LAYER), lambda j: (0, 0)),
                       pl.BlockSpec((width, count * iface_rows), lambda j: (0, 0))),
            compiler_params=pltpu.CompilerParams(vmem_limit_bytes=VMEM_LIMIT),
            cost_estimate=pl.CostEstimate(flops=8 * width * dof * LANES * 2 * count,
                                          bytes_accessed=1_000_000, transcendentals=0),
            name="ends",
        )(place, current, current, trace_matrix)

    with jax.named_scope("halo"):
        low = lax.ppermute(up, "space", [(i, (i + 1) % shards) for i in range(shards)])
        high = lax.ppermute(down, "space", [(i, (i - 1) % shards) for i in range(shards)])
    with jax.named_scope("interface"):
        pieces = [lax.ppermute(cross, ("space", "row"),
                               [(i * 2 + r, (i + d) % shards * 2 + 1 - r) for i in range(shards) for r in range(2)])
                  for d in range(shards)]

    tile = 256
    steps = total // tile
    by_tile = lambda *lead: pl.BlockSpec(lead + (tile,), lambda j: (0,) * len(lead) + (j,))
    with jax.named_scope("couple"):
        ready, factors = pl.pallas_call(
            functools.partial(couple_kernel, shards, peers),
            grid=(steps,),
            out_shape=(jax.ShapeDtypeStruct((count, dof, total), jnp.float32),
                       jax.ShapeDtypeStruct((count * count * (peers - 1), total), jnp.float32)),
            in_specs=[smem, smem, smem, by_tile(6), whole(partner_rows), whole(current), by_tile(count, dof),
                      by_tile(count, dof), by_tile(1), whole(trace_matrix), whole(lift_matrix),
                      whole(volume_matrix), whole(block_inverse), whole(low), whole(high)] + [whole(p) for p in pieces],
            out_specs=(by_tile(count, dof), by_tile(count * count * (peers - 1))),
            scratch_shapes=[pltpu.VMEM((6, count * width, total), bf16)],
            compiler_params=pltpu.CompilerParams(vmem_limit_bytes=VMEM_LIMIT),
            cost_estimate=pl.CostEstimate(
                flops=2 * count * total * (6 * width * dof * 2 + dof * dof + 6 * width * total),
                bytes_accessed=count * dof * total * 10, transcendentals=0),
            name="couple",
        )(place, frequency, table, neighbours, partner_rows, current, current, forcing_local, metric_scale,
          trace_matrix, lift_matrix, volume_matrix, block_inverse, low, high, *pieces)

    vmem = pl.BlockSpec(memory_space=pltpu.VMEM)
    with jax.named_scope("update"):
        result = pl.pallas_call(
            functools.partial(update_kernel, tile),
            out_shape=jax.ShapeDtypeStruct((count, dof, total), bf16),
            in_specs=[vmem] * (2 + peers),
            out_specs=pl.BlockSpec(memory_space=pl.ANY),
            scratch_shapes=[pltpu.VMEM((steps, count, dof, tile), bf16), pltpu.SemaphoreType.DMA((steps + count - 1,))],
            compiler_params=pltpu.CompilerParams(vmem_limit_bytes=VMEM_LIMIT),
            cost_estimate=pl.CostEstimate(flops=2 * count * total * dof * dof * (peers - 1),
                                          bytes_accessed=count * dof * total * 8, transcendentals=0),
            name="update",
        )(ready, factors, block_inverse, *others)
    return result[None]


def solution(mesh):
    in_specs = (
        P("row", "inst", None, ("groups", "space")),
        P("row", "inst", None, ("groups", "space")),
        P("row", ("groups", "space")),
        P(),
        P("row", None, ("groups", "space")),
        P("row", "inst", ("groups", "space")),
        P(),
        P(),
        P(),
        P(),
    )
    out_specs = P("row", "inst", None, ("groups", "space"))
    return jax.shard_map(body, mesh=mesh, in_specs=in_specs, out_specs=out_specs, check_vma=False)
```

```python
import functools

import jax
import jax.numpy as jnp
import numpy as np
from jax import lax
from jax.experimental import pallas as pl
from jax.experimental.pallas import tpu as pltpu
from jax.sharding import PartitionSpec as P

LAYER = 64
OPPOSITE = (1, 0, 3, 2, 5, 4)
LANES = 128
VMEM_LIMIT = 40 * 1024 * 1024


def spectral_table(instances):
    positions = np.arange(instances)
    distance = positions[:, None] - positions[None, :]
    parity = np.where(distance % 2 == 0, 1.0, -1.0)
    angles = np.pi * distance / instances
    sines = np.where(distance == 0, 1.0, np.sin(angles))
    cotangent = np.where(distance == 0, 0.0, np.cos(angles) / sines)
    return (0.5 * parity * cotangent).astype(np.float32)


def one_hot(picked, rows):
    numbers = lax.broadcasted_iota(jnp.int32, (rows, picked.shape[1]), 0)
    return jnp.where(numbers == picked, 1.0, 0.0).astype(jnp.bfloat16)


def dot(left, right):
    return jnp.dot(left, right, preferred_element_type=jnp.float32)


def ends_kernel(place_ref, first_ref, last_ref, trace_ref, up_ref, down_ref, cross_ref):
    width = trace_ref.shape[0] // 6
    section = place_ref[0]
    for n in range(first_ref.shape[0]):
        first = dot(trace_ref[...], first_ref[n]).astype(jnp.bfloat16)
        last = dot(trace_ref[4 * width :, :], last_ref[n]).astype(jnp.bfloat16)
        down_ref[:, n * LAYER : (n + 1) * LAYER] = first[4 * width :, :LAYER]
        up_ref[:, n * LAYER : (n + 1) * LAYER] = last[:, last.shape[1] - LAYER :]
        rows = cross_ref.shape[1] // first_ref.shape[0]
        cross_ref[:, n * rows : (n + 1) * rows] = jnp.where(
            section == 0, first[width : 2 * width, :rows], first[:width, :rows])


def couple_kernel(shards, peers, place_ref, freq_ref, table_ref, adj_ref, partner_ref, all_ref, tile_ref, forcing_ref,
                  scale_ref, trace_ref, lift_ref, volume_ref, inverse_ref, low_ref, high_ref, *rest):
    pieces, (out_ref, factor_ref, traces) = rest[:shards], rest[shards:]
    step = pl.program_id(0)
    steps = pl.num_programs(0)
    count, dof, total = all_ref.shape
    width = trace_ref.shape[0] // 6
    tile = tile_ref.shape[2]
    section, inst, space = place_ref[0], place_ref[1], place_ref[2]

    @pl.when(step == 0)
    def _():
        for n in range(count):
            for c in range(total // tile):
                cols = slice(c * tile, (c + 1) * tile)
                made = dot(trace_ref[...], all_ref[n, :, cols]).astype(jnp.bfloat16)
                for f in range(6):
                    traces[f, n * width : (n + 1) * width, cols] = made[f * width : (f + 1) * width]

    column = lax.broadcasted_iota(jnp.int32, (1, tile), 1)
    at_edge = jnp.logical_or(step == 0, step == steps - 1)

    def gathered(edge):
        found = []
        for f in range(6):
            adj = adj_ref[f : f + 1, :]
            values = dot(traces[OPPOSITE[f]], one_hot(adj - LAYER, total))
            if edge and f >= 4:
                part = slice((5 - f) * width, (6 - f) * width)
                below = jnp.concatenate([low_ref[part, n * LAYER : (n + 1) * LAYER] for n in range(count)], axis=0)
                above = jnp.concatenate([high_ref[part, n * LAYER : (n + 1) * LAYER] for n in range(count)], axis=0)
                values += dot(below, one_hot(adj, LAYER))
                values += dot(above, one_hot(adj - (LAYER + total), LAYER))
            values = values.astype(jnp.bfloat16)
            if edge and f < 2:
                rows = partner_ref.shape[1]
                use = jnp.logical_and(step == 0, section == 1 - f)
                crossed = []
                for n in range(count):
                    wanted = partner_ref[n : n + 1, :]
                    arrived = jnp.zeros((width, rows), jnp.float32)
                    for d in range(shards):
                        source = lax.rem(space - d + shards, shards)
                        arrived += dot(pieces[d][:, n * rows : (n + 1) * rows], one_hot(wanted - source * rows, rows))
                    crossed.append(arrived)
                crossed = jnp.concatenate(crossed, axis=0).astype(jnp.bfloat16)
                crossed = jnp.concatenate(
                    [crossed, jnp.zeros((count * width, tile - rows), jnp.bfloat16)], axis=1)
                take = jnp.logical_and(column < rows, use)
                values = jnp.where(take, crossed, values)
            found.append(values)
        return found

    def finish(edge):
        found = gathered(edge)
        frequency = freq_ref[0]
        scale = scale_ref[...]
        inverse_scale = 1.0 / scale
        for n in range(count):
            for d in range(1, peers):
                owner = lax.rem(inst - d + peers, peers)
                for m in range(count):
                    weight = table_ref[inst * count + n, owner * count + m] * frequency
                    at = (n * (peers - 1) + d - 1) * count + m
                    factor_ref[at : at + 1, :] = weight * inverse_scale
        for n in range(count):
            beside = jnp.concatenate([v[n * width : (n + 1) * width] for v in found], axis=0)
            inner = dot(lift_ref[...], beside) + dot(volume_ref[...], tile_ref[n])
            value = forcing_ref[n].astype(jnp.float32) - scale * inner
            for m in range(count):
                weight = table_ref[inst * count + n, inst * count + m] * frequency
                value -= weight * tile_ref[m].astype(jnp.float32)
            update = dot(inverse_ref[...], value.astype(jnp.bfloat16))
            out_ref[n] = tile_ref[n].astype(jnp.float32) + update * inverse_scale

    @pl.when(at_edge)
    def _():
        finish(True)

    @pl.when(jnp.logical_not(at_edge))
    def _():
        finish(False)


def update_kernel(tile, ready_ref, factor_ref, inverse_ref, *rest):
    others, (out_ref, made, sems) = rest[:-3], rest[-3:]
    count, dof, total = ready_ref.shape
    depths = [(low, min(low + tile, dof)) for low in range(0, dof, tile)]
    copies = []
    for t in range(total // tile):
        cols = slice(t * tile, (t + 1) * tile)
        moved = [[dot(inverse_ref[:, low:high], other[m, low:high, cols]) for low, high in depths]
                 for other in others for m in range(count)]
        moved = [functools.reduce(jnp.add, parts) for parts in moved]
        for n in range(count):
            value = ready_ref[n, :, cols]
            for k, part in enumerate(moved):
                at = n * len(moved) + k
                value -= factor_ref[at : at + 1, cols] * part
            made[t, n] = value.astype(jnp.bfloat16)
            if t == total // tile - 1:
                copy = pltpu.make_async_copy(made.at[t, n], out_ref.at[n, :, cols], sems.at[t + n])
                copy.start()
                copies.append(copy)
        if t < total // tile - 1:
            copy = pltpu.make_async_copy(made.at[t], out_ref.at[:, :, cols], sems.at[t])
            copy.start()
            copies.append(copy)
    for copy in copies:
        copy.wait()


def whole(array):
    return pl.BlockSpec(array.shape, lambda j: (0,) * array.ndim)


def body(solution, forcing, metric_scale, frequency, adjacency, partner, volume_matrix, trace_matrix, lift_matrix,
         block_inverse):
    current = solution[0]
    forcing_local = forcing[0]
    neighbours = adjacency[0]
    partner_rows = partner[0]
    count, dof, total = current.shape
    width = trace_matrix.shape[0] // 6
    iface_rows = partner_rows.shape[1]
    shards = lax.axis_size("space")
    peers = lax.axis_size("inst")
    section = lax.axis_index("row")
    place = jnp.stack([section, lax.axis_index("inst"), lax.axis_index("space")]).astype(jnp.int32)
    table = jnp.asarray(spectral_table(count * peers))
    smem = pl.BlockSpec(memory_space=pltpu.SMEM)
    bf16 = jnp.bfloat16

    with jax.named_scope("instances"):
        others = [lax.ppermute(current, "inst", [(i, (i + d) % peers) for i in range(peers)])
                  for d in range(1, peers)]

    with jax.named_scope("ends"):
        up, down, cross = pl.pallas_call(
            ends_kernel,
            grid=(1,),
            out_shape=(jax.ShapeDtypeStruct((2 * width, count * LAYER), bf16),
                       jax.ShapeDtypeStruct((2 * width, count * LAYER), bf16),
                       jax.ShapeDtypeStruct((width, count * iface_rows), bf16)),
            in_specs=[smem,
                      pl.BlockSpec((count, dof, LANES), lambda j: (0, 0, 0)),
                      pl.BlockSpec((count, dof, LANES), lambda j: (0, 0, total // LANES - 1)),
                      whole(trace_matrix)],
            out_specs=(pl.BlockSpec((2 * width, count * LAYER), lambda j: (0, 0)),
                       pl.BlockSpec((2 * width, count * LAYER), lambda j: (0, 0)),
                       pl.BlockSpec((width, count * iface_rows), lambda j: (0, 0))),
            compiler_params=pltpu.CompilerParams(vmem_limit_bytes=VMEM_LIMIT),
            cost_estimate=pl.CostEstimate(flops=8 * width * dof * LANES * 2 * count,
                                          bytes_accessed=1_000_000, transcendentals=0),
            name="ends",
        )(place, current, current, trace_matrix)

    with jax.named_scope("halo"):
        low = lax.ppermute(up, "space", [(i, (i + 1) % shards) for i in range(shards)])
        high = lax.ppermute(down, "space", [(i, (i - 1) % shards) for i in range(shards)])
    with jax.named_scope("interface"):
        pieces = [lax.ppermute(cross, ("space", "row"),
                               [(i * 2 + r, (i + d) % shards * 2 + 1 - r) for i in range(shards) for r in range(2)])
                  for d in range(shards)]

    tile = 256
    steps = total // tile
    by_tile = lambda *lead: pl.BlockSpec(lead + (tile,), lambda j: (0,) * len(lead) + (j,))
    with jax.named_scope("couple"):
        ready, factors = pl.pallas_call(
            functools.partial(couple_kernel, shards, peers),
            grid=(steps,),
            out_shape=(jax.ShapeDtypeStruct((count, dof, total), jnp.float32),
                       jax.ShapeDtypeStruct((count * count * (peers - 1), total), jnp.float32)),
            in_specs=[smem, smem, smem, by_tile(6), whole(partner_rows), whole(current), by_tile(count, dof),
                      by_tile(count, dof), by_tile(1), whole(trace_matrix), whole(lift_matrix),
                      whole(volume_matrix), whole(block_inverse), whole(low), whole(high)] + [whole(p) for p in pieces],
            out_specs=(by_tile(count, dof), by_tile(count * count * (peers - 1))),
            scratch_shapes=[pltpu.VMEM((6, count * width, total), bf16)],
            compiler_params=pltpu.CompilerParams(vmem_limit_bytes=VMEM_LIMIT),
            cost_estimate=pl.CostEstimate(
                flops=2 * count * total * (6 * width * dof * 2 + dof * dof + 6 * width * total),
                bytes_accessed=count * dof * total * 10, transcendentals=0),
            name="couple",
        )(place, frequency, table, neighbours, partner_rows, current, current, forcing_local, metric_scale,
          trace_matrix, lift_matrix, volume_matrix, block_inverse, low, high, *pieces)

    vmem = pl.BlockSpec(memory_space=pltpu.VMEM)
    with jax.named_scope("update"):
        result = pl.pallas_call(
            functools.partial(update_kernel, tile),
            out_shape=jax.ShapeDtypeStruct((count, dof, total), bf16),
            in_specs=[vmem] * (2 + peers),
            out_specs=pl.BlockSpec(memory_space=pl.ANY),
            scratch_shapes=[pltpu.VMEM((steps, count, dof, tile), bf16), pltpu.SemaphoreType.DMA((steps + count - 1,))],
            compiler_params=pltpu.CompilerParams(vmem_limit_bytes=VMEM_LIMIT),
            cost_estimate=pl.CostEstimate(flops=2 * count * total * dof * dof * (peers - 1),
                                          bytes_accessed=count * dof * total * 8, transcendentals=0),
            name="update",
        )(ready, factors, block_inverse, *others)
    return result[None]


def solution(mesh):
    in_specs = (
        P("row", "inst", None, ("groups", "space")),
        P("row", "inst", None, ("groups", "space")),
        P("row", ("groups", "space")),
        P(),
        P("row", None, ("groups", "space")),
        P("row", "inst", ("groups", "space")),
        P(),
        P(),
        P(),
        P(),
    )
    out_specs = P("row", "inst", None, ("groups", "space"))
    return jax.shard_map(body, mesh=mesh, in_specs=in_specs, out_specs=out_specs, check_vma=False)
```
